32 devices in a mesh: group: 4 (over z), dev: 8 (over y, x, core).
Axes of the slice: x: 2, y: 2, z: 4, core: 2. Of those that a mesh axis runs over, the one named last changes fastest.
Arguments:
- density: float32 [16, 64, 128], P('dev', 'group'), may hold values from 0.9 to 1.1
- velocity: float32 [3, 16, 64, 128], P(None, 'dev', 'group'), may hold values from -0.2 to 0.2
- basis: bfloat16 [32, 3, 8, 2048], P(None, None, 'dev', 'group'), may hold values from -0.02734375 to 0.02734375
- snap_steps: int32 [4], replicated, may hold values from 0 to 5
Outputs:
- populations: float32 [19, 16, 64, 128], P(None, 'dev', 'group')
- coefficients: float32 [32, 4], replicated
- r_factor: float32 [4, 4], replicated
- new_modes: float32 [4, 3, 8, 2048], P(None, None, 'dev', 'group')
The draws below stay inside these ranges and needn't reach their ends.
All inputs are finite; a program needn't handle non-finite values.
Results may differ from the reference program's by a relative error of at most 0.0003.
Values sent between devices are 32-bit elements; how exact they have to be, the bound alone decides.
No kernel may reach another device: no remote copies, remote signals or barrier semaphores. Data moves between devices by JAX's collectives and lax.ppermute only.
A program may use at most 64 MiB of HBM per device.

```python
import math
import jax
import jax.numpy as jnp
from jax import lax

NY = 64
NZ = 128
STEPS = 6
SNAPS = 4
RANK = 32
NX = 16
ROWS = 49152


def draw_snap_steps(key, part):
    key = jax.random.fold_in(key, 11)
    middle = jax.random.permutation(jax.random.fold_in(key, 1), STEPS - 2)[:SNAPS - 2] + 1
    chosen = jnp.concatenate([jnp.array([0, STEPS - 1], jnp.int32), middle.astype(jnp.int32)])
    order = jax.random.permutation(jax.random.fold_in(key, 2), SNAPS)
    return chosen[order]


def block_levels(rng, dims, split, low, largest):
    gain = 1.0
    for axis_at, shards_of in split:
        draws = jax.random.uniform(jax.random.fold_in(jax.random.fold_in(rng, 6), axis_at), (shards_of,), jnp.float32, low / len(split), largest / len(split))
        gain = gain * jnp.repeat(jnp.exp(draws), dims[axis_at] // shards_of).reshape((-1,) + (1,) * (len(dims) - 1 - axis_at))
    return gain


def gaussian(rng, dims, width, limit, split=(), held_as=jnp.bfloat16):
    values = jax.random.normal(rng, dims, jnp.float32) * width
    if len(split) > 0:
        values = block_levels(rng, dims, split, -0.22, 0.18) * values
    return jnp.clip(values, min=-limit, max=limit).astype(held_as)


def setup_inputs(seed: int = 0) -> dict:
    streams_of = jax.random.split(jax.random.key(seed), 5)
    return {
        "density": jnp.clip(0.9 + 0.20000005 * jax.random.uniform(streams_of[0], (NX, NY, NZ), jnp.float32) ** block_levels(streams_of[0], (NX, NY, NZ), ((0, 8), (1, 4)), -0.2, 0.2), 0.9, 1.1),
        "velocity": gaussian(streams_of[1], (3, NX, NY, NZ), 0.05, 0.2, ((1, 8), (2, 4)), jnp.float32),
        "basis": gaussian(streams_of[2], (RANK, 3, NX // 2, (NY // 2) * (NZ // 2)), ROWS ** -0.5, 0.02734375, ((2, 8), (3, 4))),
        "snap_steps": draw_snap_steps(jax.random.fold_in(streams_of[4], 71), 0),
    }


DIR_X = [0, 1, -1, 0, 0, 0, 0, 1, -1, 1, -1, 1, -1, 1, -1, 0, 0, 0, 0]
DIR_Y = [0, 0, 0, 1, -1, 0, 0, 1, 1, -1, -1, 0, 0, 0, 0, 1, -1, 1, -1]
DIR_Z = [0, 0, 0, 0, 0, 1, -1, 0, 0, 0, 0, 1, 1, -1, -1, 1, 1, -1, -1]
WEIGHTS = [1.0 / 3.0] + [1.0 / 18.0] * 6 + [1.0 / 36.0] * 12
OMEGA = 1.6
UNIT = 10.0

def equilibrium(dens, vel):
    usq = vel[0] * vel[0] + vel[1] * vel[1] + vel[2] * vel[2]
    pieces = []
    for i in range(19):
        proj = float(DIR_X[i]) * vel[0] + float(DIR_Y[i]) * vel[1] + float(DIR_Z[i]) * vel[2]
        pieces.append(WEIGHTS[i] * dens * (1.0 + 3.0 * proj + 4.5 * proj * proj - 1.5 * usq))
    return jnp.stack(pieces)

def moments(pops):
    dens = lax.optimization_barrier(jnp.sum(pops, axis=0))
    comps = []
    for table in (DIR_X, DIR_Y, DIR_Z):
        total = jnp.zeros_like(dens)
        for i in range(19):
            if table[i] != 0:
                total = total + float(table[i]) * pops[i]
        comps.append(total / dens)
    return (dens, jnp.stack(comps))

def coarsen(vel):
    three, xs, ys, zs = vel.shape
    blocks = vel.reshape(three, xs // 2, 2, ys // 2, 2, zs // 2, 2)
    return lax.optimization_barrier(jnp.mean(blocks, axis=(2, 4, 6))).reshape(three, xs // 2, ys // 2 * (zs // 2))

def forward_solve(lower, flat):
    solved = []
    for k in range(flat.shape[0]):
        value = flat[k]
        for j in range(k):
            value = value - lower[k, j] * solved[j]
        solved.append(value / lower[k, k])
    return jnp.stack(solved)

def reference(density, velocity, basis, snap_steps):
    pops = equilibrium(density, velocity)
    snaps = jnp.zeros((SNAPS, 3, NX // 2, NY // 2 * (NZ // 2)), jnp.float32)
    for step in range(STEPS):
        dens, vel = moments(pops)
        view = coarsen(vel) * UNIT
        pick = (snap_steps == step).astype(jnp.float32)
        snaps = snaps + pick[:, None, None, None] * view[None]
        post = pops - OMEGA * (pops - equilibrium(dens, vel))
        pops = jnp.stack([jnp.roll(post[i], (DIR_X[i], DIR_Y[i], DIR_Z[i]), axis=(0, 1, 2)) for i in range(19)])
    modes = basis.astype(jnp.float32)
    coefficients = jnp.einsum('rabc,kabc->rk', modes, snaps, precision=lax.Precision.HIGHEST)
    resid = snaps - jnp.einsum('rk,rabc->kabc', coefficients, modes, precision=lax.Precision.HIGHEST)
    gram = jnp.einsum('kabc,labc->kl', resid, resid, precision=lax.Precision.HIGHEST)
    lower = jnp.linalg.cholesky(gram)
    scale = math.sqrt(ROWS)
    flat = resid.reshape(SNAPS, -1)
    new_modes = (forward_solve(lower, flat) * scale).reshape(resid.shape)
    r_factor = lower.T / scale
    return (pops, coefficients, r_factor, new_modes)
```

```python
import functools
import math

import jax
import jax.numpy as jnp
from jax import lax
from jax.experimental import pallas as pl
from jax.experimental.pallas import tpu as pltpu
from jax.sharding import PartitionSpec as P

STEPS = 6
DIRS = 19
DIR_X = [0, 1, -1, 0, 0, 0, 0, 1, -1, 1, -1, 1, -1, 1, -1, 0, 0, 0, 0]
DIR_Y = [0, 0, 0, 1, -1, 0, 0, 1, 1, -1, -1, 0, 0, 0, 0, 1, -1, 1, -1]
DIR_Z = [0, 0, 0, 0, 0, 1, -1, 0, 0, 0, 0, 1, 1, -1, -1, 1, 1, -1, -1]
OPPOSITE = [(1, 2), (3, 4), (5, 6), (7, 10), (8, 9), (11, 14), (12, 13), (15, 18), (16, 17)]
OMEGA = 1.6
UNIT = 10.0
SUB = 8
LANES = 128
HALO = 8
HIGHEST = lax.Precision.HIGHEST
NT = (((1,), (1,)), ((), ()))
VMEM_LIMIT = 48 * 1024 * 1024


def along(direction, parts):
    total = None
    for sign, part in zip(direction, parts):
        if sign == 0:
            continue
        if total is None:
            total = part if sign > 0 else -part
        else:
            total = total + part if sign > 0 else total - part
    return total


def relaxed(rate, dens, flow, speed, pops):
    keep = 1.0 - rate
    twice = [2.0 * f for f in flow]
    squares = [t * s for t, s in zip(twice, speed)]
    base = (rate / 36.0) * dens - (squares[0] + squares[1] + squares[2]) * (1.0 / 6.0)
    base2 = 2.0 * base
    out = [None] * DIRS

    def put(i, value):
        out[i] = value if pops is None else keep * pops[i] + value

    put(0, 12.0 * base)
    for a, b in OPPOSITE:
        direction = (DIR_X[a], DIR_Y[a], DIR_Z[a])
        if a < 7:
            axis = [abs(d) for d in direction].index(1)
            even = base2 + squares[axis]
            odd = twice[axis]
        else:
            odd = along(direction, flow)
            even = base + odd * along(direction, speed)
        put(a, even + odd)
        put(b, even - odd)
    return out


def moments(pops):
    dens = pops[0]
    diff = {}
    for a, b in OPPOSITE:
        dens = dens + (pops[a] + pops[b])
        diff[a] = pops[a] - pops[b]
    mom = []
    for table in (DIR_X, DIR_Y, DIR_Z):
        total = None
        for a, _ in OPPOSITE:
            if table[a] == 0:
                continue
            if total is None:
                total = diff[a] if table[a] > 0 else -diff[a]
            else:
                total = total + diff[a] if table[a] > 0 else total - diff[a]
        mom.append(total)
    return dens, mom


def streamed(src, x, tiles, row):
    turned = {}

    def turn(i, t):
        if (i, t) not in turned:
            tile = src[i, x - DIR_X[i], pl.ds(SUB * t, SUB), :]
            turned[i, t] = pltpu.roll(tile, DIR_Y[i] % SUB, 0)
        return turned[i, t]

    def get(i, t):
        if DIR_Y[i] == 0:
            tile = src[i, x - DIR_X[i], pl.ds(SUB * t, SUB), :]
        elif DIR_Y[i] > 0:
            tile = jnp.where(row == 0, turn(i, max(t - 1, 0)), turn(i, t))
        else:
            tile = jnp.where(row == SUB - 1, turn(i, min(t + 1, tiles - 1)), turn(i, t))
        if DIR_Z[i] != 0:
            tile = pltpu.roll(tile, DIR_Z[i] % LANES, 1)
        return tile

    return get


def edges_kernel(dens, vel, top, bottom):
    rows = dens.shape[1]
    top[0] = dens[:, rows - HALO :, :]
    bottom[0] = dens[:, :HALO, :]
    for c in range(3):
        top[c + 1] = vel[c, :, rows - HALO :, :]
        bottom[c + 1] = vel[c, :, :HALO, :]


def widen_kernel(dens, vel, upper, lower, wide):
    rows = dens.shape[1]
    wide[:, :, :HALO, :] = upper[...]
    wide[:, :, HALO + rows :, :] = lower[...]
    wide[0, :, HALO : HALO + rows, :] = dens[...]
    for c in range(3):
        wide[c + 1, :, HALO : HALO + rows, :] = vel[c]


def lattice_kernel(
    place, snap_steps, b0, b1, b2, b3, b4, b5, b6, basis, pops, snaps, sums, fields, ping, pong, speeds, views, picked, gram
):
    blocks = (b0, b1, b2, b3, b4, b5, b6)
    _, planes, wide, lanes = b0.shape
    reach = STEPS
    span = planes + 2 * reach
    tiles = wide // SUB
    rows = wide - 2 * HALO
    count = snap_steps.shape[0]
    row = lax.broadcasted_iota(jnp.int32, (SUB, lanes), 0)
    for n, block in enumerate(blocks):
        start = place[n]
        for p in range(planes):
            fields[start + p] = block[:, p]

    def put_speed(x, t, speed):
        if HALO <= SUB * t < HALO + rows:
            for c in range(3):
                speeds[x, c, pl.ds(SUB * t - HALO, SUB), :] = speed[c]

    def keep_view(step):
        for c in range(3):
            total = speeds[reach, c]
            for p in range(1, planes):
                total = total + speeds[reach + p, c]
            views[step, c] = total

    def first(x, carry):
        for t in range(tiles):
            at = pl.ds(SUB * t, SUB)
            dens = fields[x, 0, at, :]
            vel = [fields[x, c + 1, at, :] for c in range(3)]
            part = dens * (3.0 / 36.0)
            speed = [1.5 * v for v in vel]
            out = relaxed(1.0, dens, [part * v for v in vel], speed, None)
            for i in range(DIRS):
                ping[i, x, at, :] = out[i]
            put_speed(x, t, speed)
        return carry

    lax.fori_loop(0, span, first, 0)
    keep_view(0)

    src, dst = ping, pong
    for step in range(1, STEPS):

        def later(x, carry, src=src, dst=dst):
            get = streamed(src, x, tiles, row)
            for t in range(tiles):
                pop = [get(i, t) for i in range(DIRS)]
                dens, mom = moments(pop)
                inverse = 1.5 / dens
                speed = [m * inverse for m in mom]
                flow = [m * (OMEGA * 3.0 / 36.0) for m in mom]
                out = relaxed(OMEGA, dens, flow, speed, pop)
                for i in range(DIRS):
                    dst[i, x, pl.ds(SUB * t, SUB), :] = out[i]
                put_speed(x, t, speed)
            return carry

        lax.fori_loop(step, span - step, later, 0)
        keep_view(step)
        src, dst = dst, src

    for p in range(planes):
        get = streamed(src, reach + p, tiles, row)
        for t in range(HALO // SUB, (HALO + rows) // SUB):
            for i in range(DIRS):
                pops[i, p, pl.ds(SUB * t - HALO, SUB), :] = get(i, t)

    picked[...] = jnp.zeros_like(picked)
    for k in range(count):
        at_step = snap_steps[k]
        for c in range(3):
            picked[c, pl.ds(rows * k, rows), :] = views[at_step, c]
    groups = rows // 4
    lefts, rights = [], []
    for c in range(3):
        for t in range(groups):
            part = [picked[c, pl.ds(4 * t + j, SUB, stride=rows), :] for j in range(4)]
            lefts.append(part[0] + part[1])
            rights.append(part[2] + part[3])
    lane = lax.broadcasted_iota(jnp.int32, (lanes, lanes), 0) // 2
    col = lax.broadcasted_iota(jnp.int32, (lanes, lanes), 1)
    to_left = jnp.where(lane == col, 1.0, 0.0).astype(jnp.float32)
    to_right = jnp.where(lane + lanes // 2 == col, 1.0, 0.0).astype(jnp.float32)
    flat = jnp.dot(jnp.concatenate(lefts, axis=0), to_left, precision=HIGHEST, preferred_element_type=jnp.float32)
    flat = flat + jnp.dot(
        jnp.concatenate(rights, axis=0), to_right, precision=HIGHEST, preferred_element_type=jnp.float32
    )
    flat = flat * (UNIT / (4 * planes) / 1.5)
    rank = basis.shape[1]
    width = groups * lanes
    for c in range(3):
        for t in range(groups):
            n = c * groups + t
            snaps[c, :, pl.ds(lanes * t, lanes)] = flat[SUB * n : SUB * (n + 1), :]

    proj = jnp.zeros((SUB, rank), jnp.float32)
    inner = jnp.zeros((SUB, SUB), jnp.float32)
    modes2 = jnp.zeros((rank, rank), jnp.float32)
    for c in range(3):
        snap = snaps[c]
        mode = basis[c].astype(jnp.float32)
        proj += lax.dot_general(snap, mode, NT, precision=HIGHEST, preferred_element_type=jnp.float32)
        inner += lax.dot_general(snap, snap, NT, precision=HIGHEST, preferred_element_type=jnp.float32)
        modes2 += lax.dot_general(basis[c], basis[c], NT, preferred_element_type=jnp.float32)
    sums[...] = jnp.zeros_like(sums)
    gram[...] = jnp.zeros_like(gram)
    sums[0:SUB, 0:rank] = proj
    gram[0:rank, 0:rank] = modes2
    gram[rank : rank + SUB, 0:SUB] = inner
    sums[0:SUB, :] = sums[0:SUB, :] + pltpu.roll(gram[rank : rank + SUB, :], rank, 1)
    packed = gram[0:SUB, :]
    for j in range(1, rank // SUB):
        packed = packed + pltpu.roll(gram[SUB * j : SUB * (j + 1), :], rank * j, 1)
    sums[SUB : 2 * SUB, :] = packed


def finish_kernel(scale, count, rank, *refs):
    parts, (snaps, basis, coef, factor, modes, flag, gram) = refs[:-7], refs[-7:]
    total = tree_sum([part[...] for part in parts])
    lanes = total.shape[1]
    head = total[0:SUB, :]
    proj = head[:, 0:rank]
    inner = pltpu.roll(head, lanes - rank, 1)[:, 0:SUB]
    packed = total[SUB : 2 * SUB, :]
    for j in range(rank // SUB):
        gram[SUB * j : SUB * (j + 1), :] = packed if j == 0 else pltpu.roll(packed, lanes - rank * j, 1)
    modes2 = gram[:, 0:rank]
    dot = functools.partial(lax.dot_general, precision=HIGHEST, preferred_element_type=jnp.float32)
    turned = dot(proj, modes2, (((1,), (0,)), ((), ())))
    crossed = dot(proj, proj, NT)
    bent = dot(turned, proj, NT)
    small = inner - 2.0 * crossed + bent
    r = lax.broadcasted_iota(jnp.int32, (SUB, SUB), 0)
    c = lax.broadcasted_iota(jnp.int32, (SUB, SUB), 1)
    loss = jnp.where((r == c) & (r < count), inner + 2.0 * crossed + bent - 8.0 * small, -1.0)
    flag[0, 0] = jnp.max(jnp.where(loss < 0.0, 0.0, 1.0)).astype(jnp.int32)
    coef[...] = proj[0:count, :]
    resid = []
    for n in range(3):
        mode = basis[n].astype(jnp.float32)
        resid.append(snaps[n] - dot(proj, mode, (((1,), (0,)), ((), ()))))
    small = jnp.where((r < count) & (c < count), small, jnp.where(r == c, 1.0, 0.0))
    below = lax.broadcasted_iota(jnp.int32, (SUB, 1), 0)
    pivots = jnp.ones((SUB, 1), jnp.float32)
    for j in range(count):
        pivot = small[j : j + 1, j : j + 1]
        pivots = jnp.where(below == j, pivot, pivots)
        share = jnp.where(below > j, small[:, j : j + 1] / pivot, 0.0)
        resid = [v - share * v[j : j + 1, :] for v in resid]
        small = small - share * small[j : j + 1, :]
    root = jnp.sqrt(pivots)
    upper = jnp.where(c >= r, small / root, 0.0)
    factor[...] = upper[0:count, 0:count] * (1.0 / scale)
    gain = scale / root
    groups = snaps.shape[2] // lanes
    for n in range(3):
        value = resid[n] * gain
        for t in range(groups):
            modes[pl.ds(groups * n + t, count, stride=3 * groups), :] = value[0:count, lanes * t : lanes * (t + 1)]


def tree_sum(parts):
    parts = list(parts)
    while len(parts) > 1:
        parts = [a + b for a, b in zip(parts[::2], parts[1::2])] + ([parts[-1]] if len(parts) % 2 else [])
    return parts[0]


def moved(block, axis, target):
    return lax.ppermute(block, axis, [(i, target(i)) for i in range(lax.axis_size(axis))])


def partners(block, axis, stride, count):
    digit = lambda i: i // stride % count
    if count & (count - 1) == 0:
        return [block] + [
            moved(block, axis, lambda i, j=j: i + ((digit(i) ^ j) - digit(i)) * stride) for j in range(1, count)
        ]
    got = [block] + [
        moved(block, axis, lambda i, j=j: i + ((digit(i) + j) % count - digit(i)) * stride) for j in range(1, count)
    ]
    mine = lax.axis_index(axis) // stride % count
    return list(jnp.roll(jnp.stack(got)[::-1], mine + 1, axis=0))


def digits(size):
    found, rest = [], size
    for base in (8, 4, 2):
        while rest % base == 0:
            found.append(base)
            rest //= base
    base = 3
    while rest > 1:
        while rest % base == 0:
            found.append(base)
            rest //= base
        base += 2
    return found


def from_residuals(coefficients, snaps, basis, scale):
    modes = basis[:, :, 0, :].astype(jnp.float32)
    count = coefficients.shape[1]
    held = jnp.transpose(snaps[:, :count, :], (1, 0, 2))
    resid = held - jnp.einsum("rk,rab->kab", coefficients, modes, precision=HIGHEST)
    gram = lax.psum(jnp.einsum("kab,lab->kl", resid, resid, precision=HIGHEST), ("group", "dev"))
    lower = jnp.linalg.cholesky(gram)
    solved = []
    for k in range(count):
        value = resid[k]
        for j in range(k):
            value = value - lower[k, j] * solved[j]
        solved.append(value / lower[k, k])
    return lower.T / scale, (jnp.stack(solved) * scale).reshape(-1, LANES)


def per_device(density, velocity, basis, snap_steps):
    planes, rows, lanes = density.shape
    count = snap_steps.shape[0]
    rank = basis.shape[0]
    reach = STEPS
    n_dev, n_group = lax.axis_size("dev"), lax.axis_size("group")
    vmem = pl.BlockSpec(memory_space=pltpu.VMEM)
    smem = pl.BlockSpec(memory_space=pltpu.SMEM)
    f32 = jnp.float32
    params = pltpu.CompilerParams(vmem_limit_bytes=VMEM_LIMIT)

    edge = jax.ShapeDtypeStruct((4, planes, HALO, lanes), f32)
    top, bottom = pl.pallas_call(
        edges_kernel, out_shape=(edge, edge), in_specs=[vmem] * 2, out_specs=(vmem, vmem), compiler_params=params
    )(density, velocity)
    upper = moved(top, "group", lambda i: (i + 1) % n_group)
    lower = moved(bottom, "group", lambda i: (i - 1) % n_group)
    wide_rows = rows + 2 * HALO
    own = pl.pallas_call(
        widen_kernel,
        out_shape=jax.ShapeDtypeStruct((4, planes, wide_rows, lanes), f32),
        in_specs=[vmem] * 4,
        out_specs=vmem,
        compiler_params=params,
    )(density, velocity, upper, lower)

    ahead = moved(own, "dev", lambda i: (i - 2) % n_dev)
    behind = moved(own, "dev", lambda i: (i + 2) % n_dev)
    far = moved(own, "dev", lambda i: (i + 3 if i % 2 else i - 3) % n_dev)
    other = moved(own, "dev", lambda i: i ^ 1)
    other_ahead = moved(ahead, "dev", lambda i: i ^ 1)
    other_behind = moved(behind, "dev", lambda i: i ^ 1)
    odd = lax.axis_index("dev") % 2
    offsets = jnp.where(
        odd == 1, jnp.array([0, 2, -2, 3, -1, 1, -3], jnp.int32), jnp.array([0, 2, -2, -3, 1, 3, -1], jnp.int32)
    )
    place = reach + planes * offsets
    modes = jnp.transpose(basis[:, :, 0, :], (1, 0, 2))
    span = planes + 2 * reach
    width = basis.shape[3]
    pops, snaps, sums = pl.pallas_call(
        lattice_kernel,
        out_shape=(
            jax.ShapeDtypeStruct((DIRS, planes, rows, lanes), f32),
            jax.ShapeDtypeStruct((3, SUB, width), f32),
            jax.ShapeDtypeStruct((2 * SUB, lanes), f32),
        ),
        in_specs=[smem, smem] + [vmem] * 8,
        out_specs=(vmem, vmem, vmem),
        scratch_shapes=[
            pltpu.VMEM((span, 4, wide_rows, lanes), f32),
            pltpu.VMEM((DIRS, span, wide_rows, lanes), f32),
            pltpu.VMEM((DIRS, span, wide_rows, lanes), f32),
            pltpu.VMEM((span, 3, rows, lanes), f32),
            pltpu.VMEM((STEPS, 3, rows, lanes), f32),
            pltpu.VMEM((3, SUB * rows, lanes), f32),
            pltpu.VMEM((rank + SUB, lanes), f32),
        ],
        compiler_params=params,
    )(place, snap_steps, own, ahead, behind, far, other, other_ahead, other_behind, modes)

    rounds = []
    for axis, size in (("dev", n_dev), ("group", n_group)):
        stride = 1
        for base in digits(size):
            rounds.append((axis, stride, base))
            stride *= base
    parts = [sums]
    for axis, stride, base in rounds:
        parts = partners(tree_sum(parts), axis, stride, base)
    scale = math.sqrt(3 * width * n_dev * n_group)
    coef, factor, new_modes, flag = pl.pallas_call(
        functools.partial(finish_kernel, scale, count, rank),
        out_shape=(
            jax.ShapeDtypeStruct((count, rank), f32),
            jax.ShapeDtypeStruct((count, count), f32),
            jax.ShapeDtypeStruct((count * 3 * width // lanes, lanes), f32),
            jax.ShapeDtypeStruct((1, 1), jnp.int32),
        ),
        in_specs=[vmem] * (len(parts) + 2),
        out_specs=(vmem, vmem, vmem, smem),
        scratch_shapes=[pltpu.VMEM((rank, lanes), f32)],
        compiler_params=params,
    )(*parts, snaps, modes)
    coefficients = coef.T
    factor, new_modes = lax.cond(
        flag[0, 0] != 0,
        lambda: from_residuals(coefficients, snaps, basis, scale),
        lambda: (factor, new_modes),
    )
    return (pops, coefficients, factor, new_modes.reshape(count, 3, 1, width))


def solution(mesh):
    placed = (
        P("dev", "group", None),
        P(None, "dev", "group", None),
        P(None, None, "dev", "group"),
        P(),
    )
    return jax.shard_map(
        per_device,
        mesh=mesh,
        in_specs=placed,
        out_specs=(P(None, "dev", "group", None), P(), P(), P(None, None, "dev", "group")),
        check_vma=False,
    )
```

```python
import functools
import math

import jax
import jax.numpy as jnp
from jax import lax
from jax.experimental import pallas as pl
from jax.experimental.pallas import tpu as pltpu
from jax.sharding import PartitionSpec as P

STEPS = 6
DIRS = 19
DIR_X = [0, 1, -1, 0, 0, 0, 0, 1, -1, 1, -1, 1, -1, 1, -1, 0, 0, 0, 0]
DIR_Y = [0, 0, 0, 1, -1, 0, 0, 1, 1, -1, -1, 0, 0, 0, 0, 1, -1, 1, -1]
DIR_Z = [0, 0, 0, 0, 0, 1, -1, 0, 0, 0, 0, 1, 1, -1, -1, 1, 1, -1, -1]
OPPOSITE = [(1, 2), (3, 4), (5, 6), (7, 10), (8, 9), (11, 14), (12, 13), (15, 18), (16, 17)]
OMEGA = 1.6
UNIT = 10.0
SUB = 8
LANES = 128
HALO = 8
HIGHEST = lax.Precision.HIGHEST
NT = (((1,), (1,)), ((), ()))
VMEM_LIMIT = 48 * 1024 * 1024


def along(direction, parts):
    total = None
    for sign, part in zip(direction, parts):
        if sign == 0:
            continue
        if total is None:
            total = part if sign > 0 else -part
        else:
            total = total + part if sign > 0 else total - part
    return total


def relaxed(rate, dens, flow, speed, pops):
    keep = 1.0 - rate
    twice = [2.0 * f for f in flow]
    squares = [t * s for t, s in zip(twice, speed)]
    base = (rate / 36.0) * dens - (squares[0] + squares[1] + squares[2]) * (1.0 / 6.0)
    base2 = 2.0 * base
    out = [None] * DIRS

    def put(i, value):
        out[i] = value if pops is None else keep * pops[i] + value

    put(0, 12.0 * base)
    for a, b in OPPOSITE:
        direction = (DIR_X[a], DIR_Y[a], DIR_Z[a])
        if a < 7:
            axis = [abs(d) for d in direction].index(1)
            even = base2 + squares[axis]
            odd = twice[axis]
        else:
            odd = along(direction, flow)
            even = base + odd * along(direction, speed)
        put(a, even + odd)
        put(b, even - odd)
    return out


def moments(pops):
    dens = pops[0]
    diff = {}
    for a, b in OPPOSITE:
        dens = dens + (pops[a] + pops[b])
        diff[a] = pops[a] - pops[b]
    mom = []
    for table in (DIR_X, DIR_Y, DIR_Z):
        total = None
        for a, _ in OPPOSITE:
            if table[a] == 0:
                continue
            if total is None:
                total = diff[a] if table[a] > 0 else -diff[a]
            else:
                total = total + diff[a] if table[a] > 0 else total - diff[a]
        mom.append(total)
    return dens, mom


def streamed(src, x, tiles, row):
    turned = {}

    def turn(i, t):
        if (i, t) not in turned:
            tile = src[i, x - DIR_X[i], pl.ds(SUB * t, SUB), :]
            turned[i, t] = pltpu.roll(tile, DIR_Y[i] % SUB, 0)
        return turned[i, t]

    def get(i, t):
        if DIR_Y[i] == 0:
            tile = src[i, x - DIR_X[i], pl.ds(SUB * t, SUB), :]
        elif DIR_Y[i] > 0:
            tile = jnp.where(row == 0, turn(i, max(t - 1, 0)), turn(i, t))
        else:
            tile = jnp.where(row == SUB - 1, turn(i, min(t + 1, tiles - 1)), turn(i, t))
        if DIR_Z[i] != 0:
            tile = pltpu.roll(tile, DIR_Z[i] % LANES, 1)
        return tile

    return get


def edges_kernel(dens, vel, top, bottom):
    rows = dens.shape[1]
    top[0] = dens[:, rows - HALO :, :]
    bottom[0] = dens[:, :HALO, :]
    for c in range(3):
        top[c + 1] = vel[c, :, rows - HALO :, :]
        bottom[c + 1] = vel[c, :, :HALO, :]


def widen_kernel(dens, vel, upper, lower, wide):
    rows = dens.shape[1]
    wide[:, :, :HALO, :] = upper[...]
    wide[:, :, HALO + rows :, :] = lower[...]
    wide[0, :, HALO : HALO + rows, :] = dens[...]
    for c in range(3):
        wide[c + 1, :, HALO : HALO + rows, :] = vel[c]


def lattice_kernel(place, snap_steps, *refs):
    blocks, refs = refs[:-11], refs[-11:]
    basis, pops, snaps, sums, fields, ping, pong, speeds, views, picked, gram = refs
    planes, wide, lanes = blocks[0].shape[-3:]
    reach = STEPS
    span = planes + 2 * reach
    tiles = wide // SUB
    rows = wide - 2 * HALO
    count = snap_steps.shape[0]
    row = lax.broadcasted_iota(jnp.int32, (SUB, lanes), 0)
    for n in range(1 + 2 * (reach // planes)):
        for p in range(planes):
            if len(blocks) == 1:
                fields[planes * n + p] = blocks[0][place[n], :, p]
            else:
                fields[place[n] + p] = blocks[n][:, p]

    def put_speed(x, t, speed):
        if HALO <= SUB * t < HALO + rows:
            for c in range(3):
                speeds[x, c, pl.ds(SUB * t - HALO, SUB), :] = speed[c]

    def keep_view(step):
        for c in range(3):
            total = speeds[reach, c]
            for p in range(1, planes):
                total = total + speeds[reach + p, c]
            views[step, c] = total

    def first(x, carry):
        for t in range(tiles):
            at = pl.ds(SUB * t, SUB)
            dens = fields[x, 0, at, :]
            vel = [fields[x, c + 1, at, :] for c in range(3)]
            part = dens * (3.0 / 36.0)
            speed = [1.5 * v for v in vel]
            out = relaxed(1.0, dens, [part * v for v in vel], speed, None)
            for i in range(DIRS):
                ping[i, x, at, :] = out[i]
            put_speed(x, t, speed)
        return carry

    lax.fori_loop(0, span, first, 0)
    keep_view(0)

    src, dst = ping, pong
    for step in range(1, STEPS):

        def later(x, carry, src=src, dst=dst):
            get = streamed(src, x, tiles, row)
            for t in range(tiles):
                pop = [get(i, t) for i in range(DIRS)]
                dens, mom = moments(pop)
                inverse = 1.5 / dens
                speed = [m * inverse for m in mom]
                flow = [m * (OMEGA * 3.0 / 36.0) for m in mom]
                out = relaxed(OMEGA, dens, flow, speed, pop)
                for i in range(DIRS):
                    dst[i, x, pl.ds(SUB * t, SUB), :] = out[i]
                put_speed(x, t, speed)
            return carry

        lax.fori_loop(step, span - step, later, 0)
        keep_view(step)
        src, dst = dst, src

    for p in range(planes):
        get = streamed(src, reach + p, tiles, row)
        for t in range(HALO // SUB, (HALO + rows) // SUB):
            for i in range(DIRS):
                pops[i, p, pl.ds(SUB * t - HALO, SUB), :] = get(i, t)

    picked[...] = jnp.zeros_like(picked)
    for k in range(count):
        at_step = snap_steps[k]
        for c in range(3):
            picked[c, pl.ds(rows * k, rows), :] = views[at_step, c]
    groups = rows // 4
    lefts, rights = [], []
    for c in range(3):
        for t in range(groups):
            part = [picked[c, pl.ds(4 * t + j, SUB, stride=rows), :] for j in range(4)]
            lefts.append(part[0] + part[1])
            rights.append(part[2] + part[3])
    lane = lax.broadcasted_iota(jnp.int32, (lanes, lanes), 0) // 2
    col = lax.broadcasted_iota(jnp.int32, (lanes, lanes), 1)
    to_left = jnp.where(lane == col, 1.0, 0.0).astype(jnp.float32)
    to_right = jnp.where(lane + lanes // 2 == col, 1.0, 0.0).astype(jnp.float32)
    flat = jnp.dot(jnp.concatenate(lefts, axis=0), to_left, precision=HIGHEST, preferred_element_type=jnp.float32)
    flat = flat + jnp.dot(
        jnp.concatenate(rights, axis=0), to_right, precision=HIGHEST, preferred_element_type=jnp.float32
    )
    flat = flat * (UNIT / (4 * planes) / 1.5)
    rank = basis.shape[1]
    width = groups * lanes
    for c in range(3):
        for t in range(groups):
            n = c * groups + t
            snaps[c, :, pl.ds(lanes * t, lanes)] = flat[SUB * n : SUB * (n + 1), :]

    proj = jnp.zeros((SUB, rank), jnp.float32)
    inner = jnp.zeros((SUB, SUB), jnp.float32)
    modes2 = jnp.zeros((rank, rank), jnp.float32)
    for c in range(3):
        snap = snaps[c]
        mode = basis[c].astype(jnp.float32)
        proj += lax.dot_general(snap, mode, NT, precision=HIGHEST, preferred_element_type=jnp.float32)
        inner += lax.dot_general(snap, snap, NT, precision=HIGHEST, preferred_element_type=jnp.float32)
        modes2 += lax.dot_general(basis[c], basis[c], NT, preferred_element_type=jnp.float32)
    sums[...] = jnp.zeros_like(sums)
    gram[...] = jnp.zeros_like(gram)
    sums[0:SUB, 0:rank] = proj
    gram[0:rank, 0:rank] = modes2
    gram[rank : rank + SUB, 0:SUB] = inner
    sums[0:SUB, :] = sums[0:SUB, :] + pltpu.roll(gram[rank : rank + SUB, :], rank, 1)
    packed = gram[0:SUB, :]
    for j in range(1, rank // SUB):
        packed = packed + pltpu.roll(gram[SUB * j : SUB * (j + 1), :], rank * j, 1)
    sums[SUB : 2 * SUB, :] = packed


def finish_kernel(scale, count, rank, *refs):
    parts, (snaps, basis, coef, factor, modes, flag, gram) = refs[:-7], refs[-7:]
    if len(parts) == 1:
        total = tree_sum([parts[0][n] for n in range(parts[0].shape[0])])
    else:
        total = tree_sum([part[...] for part in parts])
    lanes = total.shape[1]
    head = total[0:SUB, :]
    proj = head[:, 0:rank]
    inner = pltpu.roll(head, lanes - rank, 1)[:, 0:SUB]
    packed = total[SUB : 2 * SUB, :]
    for j in range(rank // SUB):
        gram[SUB * j : SUB * (j + 1), :] = packed if j == 0 else pltpu.roll(packed, lanes - rank * j, 1)
    modes2 = gram[:, 0:rank]
    dot = functools.partial(lax.dot_general, precision=HIGHEST, preferred_element_type=jnp.float32)
    turned = dot(proj, modes2, (((1,), (0,)), ((), ())))
    crossed = dot(proj, proj, NT)
    bent = dot(turned, proj, NT)
    small = inner - 2.0 * crossed + bent
    r = lax.broadcasted_iota(jnp.int32, (SUB, SUB), 0)
    c = lax.broadcasted_iota(jnp.int32, (SUB, SUB), 1)
    loss = jnp.where((r == c) & (r < count), inner + 2.0 * crossed + bent - 8.0 * small, -1.0)
    flag[0, 0] = jnp.max(jnp.where(loss < 0.0, 0.0, 1.0)).astype(jnp.int32)
    coef[...] = proj[0:count, :]
    resid = []
    for n in range(3):
        mode = basis[n].astype(jnp.float32)
        resid.append(snaps[n] - dot(proj, mode, (((1,), (0,)), ((), ()))))
    small = jnp.where((r < count) & (c < count), small, jnp.where(r == c, 1.0, 0.0))
    below = lax.broadcasted_iota(jnp.int32, (SUB, 1), 0)
    pivots = jnp.ones((SUB, 1), jnp.float32)
    for j in range(count):
        pivot = small[j : j + 1, j : j + 1]
        pivots = jnp.where(below == j, pivot, pivots)
        share = jnp.where(below > j, small[:, j : j + 1] / pivot, 0.0)
        resid = [v - share * v[j : j + 1, :] for v in resid]
        small = small - share * small[j : j + 1, :]
    root = jnp.sqrt(pivots)
    upper = jnp.where(c >= r, small / root, 0.0)
    factor[...] = upper[0:count, 0:count] * (1.0 / scale)
    gain = scale / root
    groups = snaps.shape[2] // lanes
    for n in range(3):
        value = resid[n] * gain
        for t in range(groups):
            modes[pl.ds(groups * n + t, count, stride=3 * groups), :] = value[0:count, lanes * t : lanes * (t + 1)]


def tree_sum(parts):
    parts = list(parts)
    while len(parts) > 1:
        parts = [a + b for a, b in zip(parts[::2], parts[1::2])] + ([parts[-1]] if len(parts) % 2 else [])
    return parts[0]


def moved(block, axis, target):
    return lax.ppermute(block, axis, [(i, target(i)) for i in range(lax.axis_size(axis))])


def partners(block, axis, stride, count):
    digit = lambda i: i // stride % count
    if count & (count - 1) == 0:
        return [block] + [
            moved(block, axis, lambda i, j=j: i + ((digit(i) ^ j) - digit(i)) * stride) for j in range(1, count)
        ]
    got = [block] + [
        moved(block, axis, lambda i, j=j: i + ((digit(i) + j) % count - digit(i)) * stride) for j in range(1, count)
    ]
    mine = lax.axis_index(axis) // stride % count
    return list(jnp.roll(jnp.stack(got)[::-1], mine + 1, axis=0))


def digits(size):
    found, rest = [], size
    for base in (8, 4, 2):
        while rest % base == 0:
            found.append(base)
            rest //= base
    base = 3
    while rest > 1:
        while rest % base == 0:
            found.append(base)
            rest //= base
        base += 2
    return found


def summed(sums, n_dev, n_group):
    rounds = []
    for axis, size in (("dev", n_dev), ("group", n_group)):
        stride = 1
        for base in digits(size):
            rounds.append((axis, stride, base))
            stride *= base
    parts = [sums]
    for axis, stride, base in rounds:
        parts = partners(tree_sum(parts), axis, stride, base)
    return parts


def from_residuals(coefficients, snaps, basis, scale):
    modes = basis[:, :, 0, :].astype(jnp.float32)
    count = coefficients.shape[1]
    held = jnp.transpose(snaps[:, :count, :], (1, 0, 2))
    resid = held - jnp.einsum("rk,rab->kab", coefficients, modes, precision=HIGHEST)
    gram = lax.psum(jnp.einsum("kab,lab->kl", resid, resid, precision=HIGHEST), ("group", "dev"))
    lower = jnp.linalg.cholesky(gram)
    solved = []
    for k in range(count):
        value = resid[k]
        for j in range(k):
            value = value - lower[k, j] * solved[j]
        solved.append(value / lower[k, k])
    return lower.T / scale, (jnp.stack(solved) * scale).reshape(-1, LANES)


def ring_blocks(own, n_dev, planes, reach):
    ahead = moved(own, "dev", lambda i: (i - 2) % n_dev)
    behind = moved(own, "dev", lambda i: (i + 2) % n_dev)
    far = moved(own, "dev", lambda i: (i + 3 if i % 2 else i - 3) % n_dev)
    other = moved(own, "dev", lambda i: i ^ 1)
    other_ahead = moved(ahead, "dev", lambda i: i ^ 1)
    other_behind = moved(behind, "dev", lambda i: i ^ 1)
    odd = lax.axis_index("dev") % 2
    offsets = jnp.where(
        odd == 1, jnp.array([0, 2, -2, 3, -1, 1, -3], jnp.int32), jnp.array([0, 2, -2, -3, 1, 3, -1], jnp.int32)
    )
    return [own, ahead, behind, far, other, other_ahead, other_behind], reach + planes * offsets


def per_device(density, velocity, basis, snap_steps):
    planes, rows, lanes = density.shape
    count = snap_steps.shape[0]
    rank = basis.shape[0]
    reach = STEPS
    n_dev, n_group = lax.axis_size("dev"), lax.axis_size("group")
    vmem = pl.BlockSpec(memory_space=pltpu.VMEM)
    smem = pl.BlockSpec(memory_space=pltpu.SMEM)
    f32 = jnp.float32
    params = pltpu.CompilerParams(vmem_limit_bytes=VMEM_LIMIT)

    edge = jax.ShapeDtypeStruct((4, planes, HALO, lanes), f32)
    top, bottom = pl.pallas_call(
        edges_kernel, out_shape=(edge, edge), in_specs=[vmem] * 2, out_specs=(vmem, vmem), compiler_params=params
    )(density, velocity)
    upper = moved(top, "group", lambda i: (i + 1) % n_group)
    lower = moved(bottom, "group", lambda i: (i - 1) % n_group)
    wide_rows = rows + 2 * HALO
    own = pl.pallas_call(
        widen_kernel,
        out_shape=jax.ShapeDtypeStruct((4, planes, wide_rows, lanes), f32),
        in_specs=[vmem] * 4,
        out_specs=vmem,
        compiler_params=params,
    )(density, velocity, upper, lower)

    near = reach // planes
    if n_dev == 2 * near + 2:
        blocks = [lax.all_gather(own, "dev")]
        place = (lax.axis_index("dev") + jnp.arange(-near, near + 1, dtype=jnp.int32)) % n_dev
    else:
        blocks, place = ring_blocks(own, n_dev, planes, reach)
    modes = jnp.transpose(basis[:, :, 0, :], (1, 0, 2))
    span = planes + 2 * reach
    width = basis.shape[3]
    pops, snaps, sums = pl.pallas_call(
        lattice_kernel,
        out_shape=(
            jax.ShapeDtypeStruct((DIRS, planes, rows, lanes), f32),
            jax.ShapeDtypeStruct((3, SUB, width), f32),
            jax.ShapeDtypeStruct((2 * SUB, lanes), f32),
        ),
        in_specs=[smem, smem] + [vmem] * (len(blocks) + 1),
        out_specs=(vmem, vmem, vmem),
        scratch_shapes=[
            pltpu.VMEM((span, 4, wide_rows, lanes), f32),
            pltpu.VMEM((DIRS, span, wide_rows, lanes), f32),
            pltpu.VMEM((DIRS, span, wide_rows, lanes), f32),
            pltpu.VMEM((span, 3, rows, lanes), f32),
            pltpu.VMEM((STEPS, 3, rows, lanes), f32),
            pltpu.VMEM((3, SUB * rows, lanes), f32),
            pltpu.VMEM((rank + SUB, lanes), f32),
        ],
        compiler_params=params,
    )(place, snap_steps, *blocks, modes)

    if n_dev * n_group <= 32:
        parts = [lax.all_gather(sums, ("group", "dev"))]
    else:
        parts = summed(sums, n_dev, n_group)
    scale = math.sqrt(3 * width * n_dev * n_group)
    coef, factor, new_modes, flag = pl.pallas_call(
        functools.partial(finish_kernel, scale, count, rank),
        out_shape=(
            jax.ShapeDtypeStruct((count, rank), f32),
            jax.ShapeDtypeStruct((count, count), f32),
            jax.ShapeDtypeStruct((count * 3 * width // lanes, lanes), f32),
            jax.ShapeDtypeStruct((1, 1), jnp.int32),
        ),
        in_specs=[vmem] * (len(parts) + 2),
        out_specs=(vmem, vmem, vmem, smem),
        scratch_shapes=[pltpu.VMEM((rank, lanes), f32)],
        compiler_params=params,
    )(*parts, snaps, modes)
    coefficients = coef.T
    factor, new_modes = lax.cond(
        flag[0, 0] != 0,
        lambda: from_residuals(coefficients, snaps, basis, scale),
        lambda: (factor, new_modes),
    )
    return (pops, coefficients, factor, new_modes.reshape(count, 3, 1, width))


def solution(mesh):
    placed = (
        P("dev", "group", None),
        P(None, "dev", "group", None),
        P(None, None, "dev", "group"),
        P(),
    )
    return jax.shard_map(
        per_device,
        mesh=mesh,
        in_specs=placed,
        out_specs=(P(None, "dev", "group", None), P(), P(), P(None, None, "dev", "group")),
        check_vma=False,
    )
```

```python
import functools
import math

import jax
import jax.numpy as jnp
from jax import lax
from jax.experimental import pallas as pl
from jax.experimental.pallas import tpu as pltpu
from jax.sharding import PartitionSpec as P

STEPS = 6
DIRS = 19
DIR_X = [0, 1, -1, 0, 0, 0, 0, 1, -1, 1, -1, 1, -1, 1, -1, 0, 0, 0, 0]
DIR_Y = [0, 0, 0, 1, -1, 0, 0, 1, 1, -1, -1, 0, 0, 0, 0, 1, -1, 1, -1]
DIR_Z = [0, 0, 0, 0, 0, 1, -1, 0, 0, 0, 0, 1, 1, -1, -1, 1, 1, -1, -1]
OPPOSITE = [(1, 2), (3, 4), (5, 6), (7, 10), (8, 9), (11, 14), (12, 13), (15, 18), (16, 17)]
OMEGA = 1.6
UNIT = 10.0
SUB = 8
LANES = 128
HALO = 8
HIGHEST = lax.Precision.HIGHEST
NT = (((1,), (1,)), ((), ()))
VMEM_LIMIT = 48 * 1024 * 1024


def along(direction, parts):
    total = None
    for sign, part in zip(direction, parts):
        if sign == 0:
            continue
        if total is None:
            total = part if sign > 0 else -part
        else:
            total = total + part if sign > 0 else total - part
    return total


def relaxed(rate, dens, flow, speed, pops):
    keep = 1.0 - rate
    twice = [2.0 * f for f in flow]
    squares = [t * s for t, s in zip(twice, speed)]
    base = (rate / 36.0) * dens - (squares[0] + squares[1] + squares[2]) * (1.0 / 6.0)
    base2 = 2.0 * base
    out = [None] * DIRS

    def put(i, value):
        out[i] = value if pops is None else keep * pops[i] + value

    put(0, 12.0 * base)
    for a, b in OPPOSITE:
        direction = (DIR_X[a], DIR_Y[a], DIR_Z[a])
        if a < 7:
            axis = [abs(d) for d in direction].index(1)
            even = base2 + squares[axis]
            odd = twice[axis]
        else:
            odd = along(direction, flow)
            even = base + odd * along(direction, speed)
        put(a, even + odd)
        put(b, even - odd)
    return out


def moments(pops):
    dens = pops[0]
    diff = {}
    for a, b in OPPOSITE:
        dens = dens + (pops[a] + pops[b])
        diff[a] = pops[a] - pops[b]
    mom = []
    for table in (DIR_X, DIR_Y, DIR_Z):
        total = None
        for a, _ in OPPOSITE:
            if table[a] == 0:
                continue
            if total is None:
                total = diff[a] if table[a] > 0 else -diff[a]
            else:
                total = total + diff[a] if table[a] > 0 else total - diff[a]
        mom.append(total)
    return dens, mom


def streamed(src, x, tiles, row):
    turned = {}

    def turn(i, t):
        if (i, t) not in turned:
            tile = src[i, x - DIR_X[i], pl.ds(SUB * t, SUB), :]
            turned[i, t] = pltpu.roll(tile, DIR_Y[i] % SUB, 0)
        return turned[i, t]

    def get(i, t):
        if DIR_Y[i] == 0:
            tile = src[i, x - DIR_X[i], pl.ds(SUB * t, SUB), :]
        elif DIR_Y[i] > 0:
            tile = jnp.where(row == 0, turn(i, max(t - 1, 0)), turn(i, t))
        else:
            tile = jnp.where(row == SUB - 1, turn(i, min(t + 1, tiles - 1)), turn(i, t))
        if DIR_Z[i] != 0:
            tile = pltpu.roll(tile, DIR_Z[i] % LANES, 1)
        return tile

    return get


def edges_kernel(dens, vel, top, bottom):
    rows = dens.shape[1]
    top[0] = dens[:, rows - HALO :, :]
    bottom[0] = dens[:, :HALO, :]
    for c in range(3):
        top[c + 1] = vel[c, :, rows - HALO :, :]
        bottom[c + 1] = vel[c, :, :HALO, :]


def widen_kernel(dens, vel, upper, lower, wide):
    rows = dens.shape[1]
    wide[:, :, :HALO, :] = upper[...]
    wide[:, :, HALO + rows :, :] = lower[...]
    wide[0, :, HALO : HALO + rows, :] = dens[...]
    for c in range(3):
        wide[c + 1, :, HALO : HALO + rows, :] = vel[c]


def lattice_kernel(place, snap_steps, *refs):
    blocks, refs = refs[:-11], refs[-11:]
    basis, pops, snaps, sums, fields, ping, pong, speeds, views, picked, gram = refs
    planes, wide, lanes = blocks[0].shape[-3:]
    reach = STEPS
    span = planes + 2 * reach
    tiles = wide // SUB
    rows = wide - 2 * HALO
    count = snap_steps.shape[0]
    row = lax.broadcasted_iota(jnp.int32, (SUB, lanes), 0)
    for n in range(1 + 2 * (reach // planes)):
        for p in range(planes):
            if len(blocks) == 1:
                fields[planes * n + p] = blocks[0][place[n], :, p]
            else:
                fields[place[n] + p] = blocks[n][:, p]

    def put_speed(x, t, speed):
        if HALO <= SUB * t < HALO + rows:
            for c in range(3):
                speeds[x, c, pl.ds(SUB * t - HALO, SUB), :] = speed[c]

    def keep_view(step):
        for c in range(3):
            total = speeds[reach, c]
            for p in range(1, planes):
                total = total + speeds[reach + p, c]
            views[step, c] = total

    def first(x, carry):
        for t in range(tiles):
            at = pl.ds(SUB * t, SUB)
            dens = fields[x, 0, at, :]
            vel = [fields[x, c + 1, at, :] for c in range(3)]
            part = dens * (3.0 / 36.0)
            speed = [1.5 * v for v in vel]
            out = relaxed(1.0, dens, [part * v for v in vel], speed, None)
            for i in range(DIRS):
                ping[i, x, at, :] = out[i]
            put_speed(x, t, speed)
        return carry

    lax.fori_loop(0, span, first, 0)
    keep_view(0)

    src, dst = ping, pong
    for step in range(1, STEPS):

        def later(x, carry, src=src, dst=dst):
            get = streamed(src, x, tiles, row)
            for t in range(tiles):
                pop = [get(i, t) for i in range(DIRS)]
                dens, mom = moments(pop)
                inverse = 1.5 / dens
                speed = [m * inverse for m in mom]
                flow = [m * (OMEGA * 3.0 / 36.0) for m in mom]
                out = relaxed(OMEGA, dens, flow, speed, pop)
                for i in range(DIRS):
                    dst[i, x, pl.ds(SUB * t, SUB), :] = out[i]
                put_speed(x, t, speed)
            return carry

        lax.fori_loop(step, span - step, later, 0)
        keep_view(step)
        src, dst = dst, src

    for p in range(planes):
        get = streamed(src, reach + p, tiles, row)
        for t in range(HALO // SUB, (HALO + rows) // SUB):
            for i in range(DIRS):
                pops[i, p, pl.ds(SUB * t - HALO, SUB), :] = get(i, t)

    picked[...] = jnp.zeros_like(picked)
    for k in range(count):
        at_step = snap_steps[k]
        for c in range(3):
            picked[c, pl.ds(rows * k, rows), :] = views[at_step, c]
    groups = rows // 4
    lefts, rights = [], []
    for c in range(3):
        for t in range(groups):
            part = [picked[c, pl.ds(4 * t + j, SUB, stride=rows), :] for j in range(4)]
            lefts.append(part[0] + part[1])
            rights.append(part[2] + part[3])
    lane = lax.broadcasted_iota(jnp.int32, (lanes, lanes), 0) // 2
    col = lax.broadcasted_iota(jnp.int32, (lanes, lanes), 1)
    to_left = jnp.where(lane == col, 1.0, 0.0).astype(jnp.float32)
    to_right = jnp.where(lane + lanes // 2 == col, 1.0, 0.0).astype(jnp.float32)
    flat = jnp.dot(jnp.concatenate(lefts, axis=0), to_left, precision=HIGHEST, preferred_element_type=jnp.float32)
    flat = flat + jnp.dot(
        jnp.concatenate(rights, axis=0), to_right, precision=HIGHEST, preferred_element_type=jnp.float32
    )
    flat = flat * (UNIT / (4 * planes) / 1.5)
    rank = basis.shape[1]
    width = groups * lanes
    for c in range(3):
        for t in range(groups):
            n = c * groups + t
            snaps[c, :, pl.ds(lanes * t, lanes)] = flat[SUB * n : SUB * (n + 1), :]

    proj = jnp.zeros((SUB, rank), jnp.float32)
    inner = jnp.zeros((SUB, SUB), jnp.float32)
    modes2 = jnp.zeros((rank, rank), jnp.float32)
    for c in range(3):
        snap = snaps[c]
        mode = basis[c].astype(jnp.float32)
        proj += lax.dot_general(snap, mode, NT, precision=HIGHEST, preferred_element_type=jnp.float32)
        inner += lax.dot_general(snap, snap, NT, precision=HIGHEST, preferred_element_type=jnp.float32)
        modes2 += lax.dot_general(basis[c], basis[c], NT, preferred_element_type=jnp.float32)
    sums[...] = jnp.zeros_like(sums)
    gram[...] = jnp.zeros_like(gram)
    sums[0:SUB, 0:rank] = proj
    gram[0:rank, 0:rank] = modes2
    gram[rank : rank + SUB, 0:SUB] = inner
    sums[0:SUB, :] = sums[0:SUB, :] + pltpu.roll(gram[rank : rank + SUB, :], rank, 1)
    packed = gram[0:SUB, :]
    for j in range(1, rank // SUB):
        packed = packed + pltpu.roll(gram[SUB * j : SUB * (j + 1), :], rank * j, 1)
    sums[SUB : 2 * SUB, :] = packed


def finish_kernel(scale, count, rank, *refs):
    parts, (snaps, basis, coef, factor, modes, flag, gram) = refs[:-7], refs[-7:]
    if len(parts) == 1:
        total = tree_sum([parts[0][n] for n in range(parts[0].shape[0])])
    else:
        total = tree_sum([part[...] for part in parts])
    lanes = total.shape[1]
    head = total[0:SUB, :]
    proj = head[:, 0:rank]
    inner = pltpu.roll(head, lanes - rank, 1)[:, 0:SUB]
    packed = total[SUB : 2 * SUB, :]
    for j in range(rank // SUB):
        gram[SUB * j : SUB * (j + 1), :] = packed if j == 0 else pltpu.roll(packed, lanes - rank * j, 1)
    modes2 = gram[:, 0:rank]
    dot = functools.partial(lax.dot_general, precision=HIGHEST, preferred_element_type=jnp.float32)
    turned = dot(proj, modes2, (((1,), (0,)), ((), ())))
    crossed = dot(proj, proj, NT)
    bent = dot(turned, proj, NT)
    small = inner - 2.0 * crossed + bent
    r = lax.broadcasted_iota(jnp.int32, (SUB, SUB), 0)
    c = lax.broadcasted_iota(jnp.int32, (SUB, SUB), 1)
    loss = jnp.where((r == c) & (r < count), inner + 2.0 * crossed + bent - 8.0 * small, -1.0)
    flag[0, 0] = jnp.max(jnp.where(loss < 0.0, 0.0, 1.0)).astype(jnp.int32)
    coef[...] = proj[0:count, :]
    resid = []
    for n in range(3):
        mode = basis[n].astype(jnp.float32)
        resid.append(snaps[n] - dot(proj, mode, (((1,), (0,)), ((), ()))))
    small = jnp.where((r < count) & (c < count), small, jnp.where(r == c, 1.0, 0.0))
    below = lax.broadcasted_iota(jnp.int32, (SUB, 1), 0)
    pivots = jnp.ones((SUB, 1), jnp.float32)
    for j in range(count):
        pivot = small[j : j + 1, j : j + 1]
        pivots = jnp.where(below == j, pivot, pivots)
        share = jnp.where(below > j, small[:, j : j + 1] / pivot, 0.0)
        resid = [v - share * v[j : j + 1, :] for v in resid]
        small = small - share * small[j : j + 1, :]
    root = jnp.sqrt(pivots)
    upper = jnp.where(c >= r, small / root, 0.0)
    factor[...] = upper[0:count, 0:count] * (1.0 / scale)
    gain = scale / root
    groups = snaps.shape[2] // lanes
    for n in range(3):
        value = resid[n] * gain
        for t in range(groups):
            modes[pl.ds(groups * n + t, count, stride=3 * groups), :] = value[0:count, lanes * t : lanes * (t + 1)]


def tree_sum(parts):
    parts = list(parts)
    while len(parts) > 1:
        parts = [a + b for a, b in zip(parts[::2], parts[1::2])] + ([parts[-1]] if len(parts) % 2 else [])
    return parts[0]


def moved(block, axis, target):
    return lax.ppermute(block, axis, [(i, target(i)) for i in range(lax.axis_size(axis))])


def partners(block, axis, stride, count):
    digit = lambda i: i // stride % count
    if count & (count - 1) == 0:
        return [block] + [
            moved(block, axis, lambda i, j=j: i + ((digit(i) ^ j) - digit(i)) * stride) for j in range(1, count)
        ]
    got = [block] + [
        moved(block, axis, lambda i, j=j: i + ((digit(i) + j) % count - digit(i)) * stride) for j in range(1, count)
    ]
    mine = lax.axis_index(axis) // stride % count
    return list(jnp.roll(jnp.stack(got)[::-1], mine + 1, axis=0))


def digits(size):
    found, rest = [], size
    for base in (8, 4, 2):
        while rest % base == 0:
            found.append(base)
            rest //= base
    base = 3
    while rest > 1:
        while rest % base == 0:
            found.append(base)
            rest //= base
        base += 2
    return found


def summed(sums, n_dev, n_group):
    rounds = []
    for axis, size in (("dev", n_dev), ("group", n_group)):
        stride = 1
        for base in digits(size):
            rounds.append((axis, stride, base))
            stride *= base
    parts = [sums]
    for axis, stride, base in rounds:
        parts = partners(tree_sum(parts), axis, stride, base)
    return parts


def from_residuals(coefficients, snaps, basis, scale):
    modes = basis[:, :, 0, :].astype(jnp.float32)
    count = coefficients.shape[1]
    held = jnp.transpose(snaps[:, :count, :], (1, 0, 2))
    resid = held - jnp.einsum("rk,rab->kab", coefficients, modes, precision=HIGHEST)
    gram = lax.psum(jnp.einsum("kab,lab->kl", resid, resid, precision=HIGHEST), ("group", "dev"))
    lower = jnp.linalg.cholesky(gram)
    solved = []
    for k in range(count):
        value = resid[k]
        for j in range(k):
            value = value - lower[k, j] * solved[j]
        solved.append(value / lower[k, k])
    return lower.T / scale, (jnp.stack(solved) * scale).reshape(-1, LANES)


def ring_blocks(own, n_dev, planes, reach):
    ahead = moved(own, "dev", lambda i: (i - 2) % n_dev)
    behind = moved(own, "dev", lambda i: (i + 2) % n_dev)
    far = moved(own, "dev", lambda i: (i + 3 if i % 2 else i - 3) % n_dev)
    other = moved(own, "dev", lambda i: i ^ 1)
    other_ahead = moved(ahead, "dev", lambda i: i ^ 1)
    other_behind = moved(behind, "dev", lambda i: i ^ 1)
    odd = lax.axis_index("dev") % 2
    offsets = jnp.where(
        odd == 1, jnp.array([0, 2, -2, 3, -1, 1, -3], jnp.int32), jnp.array([0, 2, -2, -3, 1, 3, -1], jnp.int32)
    )
    return [own, ahead, behind, far, other, other_ahead, other_behind], reach + planes * offsets


def per_device(density, velocity, basis, snap_steps):
    planes, rows, lanes = density.shape
    count = snap_steps.shape[0]
    rank = basis.shape[0]
    reach = STEPS
    n_dev, n_group = lax.axis_size("dev"), lax.axis_size("group")
    vmem = pl.BlockSpec(memory_space=pltpu.VMEM)
    smem = pl.BlockSpec(memory_space=pltpu.SMEM)
    f32 = jnp.float32
    params = pltpu.CompilerParams(vmem_limit_bytes=VMEM_LIMIT)

    edge = jax.ShapeDtypeStruct((4, planes, HALO, lanes), f32)
    top, bottom = pl.pallas_call(
        edges_kernel, out_shape=(edge, edge), in_specs=[vmem] * 2, out_specs=(vmem, vmem), compiler_params=params
    )(density, velocity)
    upper = moved(top, "group", lambda i: (i + 1) % n_group)
    lower = moved(bottom, "group", lambda i: (i - 1) % n_group)
    wide_rows = rows + 2 * HALO
    own = pl.pallas_call(
        widen_kernel,
        out_shape=jax.ShapeDtypeStruct((4, planes, wide_rows, lanes), f32),
        in_specs=[vmem] * 4,
        out_specs=vmem,
        compiler_params=params,
    )(density, velocity, upper, lower)

    near = reach // planes
    if n_dev == 2 * near + 2:
        blocks = [lax.all_to_all(jnp.broadcast_to(own, (n_dev, *own.shape)), "dev", 0, 0)]
        place = (lax.axis_index("dev") + jnp.arange(-near, near + 1, dtype=jnp.int32)) % n_dev
    else:
        blocks, place = ring_blocks(own, n_dev, planes, reach)
    modes = jnp.transpose(basis[:, :, 0, :], (1, 0, 2))
    span = planes + 2 * reach
    width = basis.shape[3]
    pops, snaps, sums = pl.pallas_call(
        lattice_kernel,
        out_shape=(
            jax.ShapeDtypeStruct((DIRS, planes, rows, lanes), f32),
            jax.ShapeDtypeStruct((3, SUB, width), f32),
            jax.ShapeDtypeStruct((2 * SUB, lanes), f32),
        ),
        in_specs=[smem, smem] + [vmem] * (len(blocks) + 1),
        out_specs=(vmem, vmem, vmem),
        scratch_shapes=[
            pltpu.VMEM((span, 4, wide_rows, lanes), f32),
            pltpu.VMEM((DIRS, span, wide_rows, lanes), f32),
            pltpu.VMEM((DIRS, span, wide_rows, lanes), f32),
            pltpu.VMEM((span, 3, rows, lanes), f32),
            pltpu.VMEM((STEPS, 3, rows, lanes), f32),
            pltpu.VMEM((3, SUB * rows, lanes), f32),
            pltpu.VMEM((rank + SUB, lanes), f32),
        ],
        compiler_params=params,
    )(place, snap_steps, *blocks, modes)

    if n_dev * n_group <= 32:
        parts = [lax.all_to_all(jnp.broadcast_to(sums, (n_dev * n_group, *sums.shape)), ("group", "dev"), 0, 0)]
    else:
        parts = summed(sums, n_dev, n_group)
    scale = math.sqrt(3 * width * n_dev * n_group)
    coef, factor, new_modes, flag = pl.pallas_call(
        functools.partial(finish_kernel, scale, count, rank),
        out_shape=(
            jax.ShapeDtypeStruct((count, rank), f32),
            jax.ShapeDtypeStruct((count, count), f32),
            jax.ShapeDtypeStruct((count * 3 * width // lanes, lanes), f32),
            jax.ShapeDtypeStruct((1, 1), jnp.int32),
        ),
        in_specs=[vmem] * (len(parts) + 2),
        out_specs=(vmem, vmem, vmem, smem),
        scratch_shapes=[pltpu.VMEM((rank, lanes), f32)],
        compiler_params=params,
    )(*parts, snaps, modes)
    coefficients = coef.T
    factor, new_modes = lax.cond(
        flag[0, 0] != 0,
        lambda: from_residuals(coefficients, snaps, basis, scale),
        lambda: (factor, new_modes),
    )
    return (pops, coefficients, factor, new_modes.reshape(count, 3, 1, width))


def solution(mesh):
    placed = (
        P("dev", "group", None),
        P(None, "dev", "group", None),
        P(None, None, "dev", "group"),
        P(),
    )
    return jax.shard_map(
        per_device,
        mesh=mesh,
        in_specs=placed,
        out_specs=(P(None, "dev", "group", None), P(), P(), P(None, None, "dev", "group")),
        check_vma=False,
    )
```

```python
import functools
import math

import jax
import jax.numpy as jnp
from jax import lax
from jax.experimental import pallas as pl
from jax.experimental.pallas import tpu as pltpu
from jax.sharding import PartitionSpec as P

STEPS = 6
DIRS = 19
DIR_X = [0, 1, -1, 0, 0, 0, 0, 1, -1, 1, -1, 1, -1, 1, -1, 0, 0, 0, 0]
DIR_Y = [0, 0, 0, 1, -1, 0, 0, 1, 1, -1, -1, 0, 0, 0, 0, 1, -1, 1, -1]
DIR_Z = [0, 0, 0, 0, 0, 1, -1, 0, 0, 0, 0, 1, 1, -1, -1, 1, 1, -1, -1]
OPPOSITE = [(1, 2), (3, 4), (5, 6), (7, 10), (8, 9), (11, 14), (12, 13), (15, 18), (16, 17)]
OMEGA = 1.6
UNIT = 10.0
SUB = 8
LANES = 128
HALO = 8
HIGHEST = lax.Precision.HIGHEST
NT = (((1,), (1,)), ((), ()))
VMEM_LIMIT = 48 * 1024 * 1024


def along(direction, parts):
    total = None
    for sign, part in sorted(zip(direction, parts), key=lambda pair: -pair[0]):
        if sign == 0:
            continue
        if total is None:
            total = part if sign > 0 else -part
        else:
            total = total + part if sign > 0 else total - part
    return total


def relaxed(rate, dens, flow, speed, pops):
    keep = 1.0 - rate
    twice = [2.0 * f for f in flow]
    squares = [t * s for t, s in zip(twice, speed)]
    base = (rate / 36.0) * dens - (squares[0] + squares[1] + squares[2]) * (1.0 / 6.0)
    base2 = 2.0 * base
    out = [None] * DIRS

    def put(i, value):
        out[i] = value if pops is None else keep * pops[i] + value

    put(0, 12.0 * base)
    for a, b in OPPOSITE:
        direction = (DIR_X[a], DIR_Y[a], DIR_Z[a])
        if a < 7:
            axis = [abs(d) for d in direction].index(1)
            even = base2 + squares[axis]
            odd = twice[axis]
        else:
            odd = along(direction, flow)
            even = base + odd * along(direction, speed)
        put(a, even + odd)
        put(b, even - odd)
    return out


def moments(pops):
    dens = pops[0]
    diff = {}
    for a, b in OPPOSITE:
        dens = dens + (pops[a] + pops[b])
        diff[a] = pops[a] - pops[b]
    mom = []
    for table in (DIR_X, DIR_Y, DIR_Z):
        total = None
        for a, _ in OPPOSITE:
            if table[a] == 0:
                continue
            if total is None:
                total = diff[a] if table[a] > 0 else -diff[a]
            else:
                total = total + diff[a] if table[a] > 0 else total - diff[a]
        mom.append(total)
    return dens, mom


def streamed(src, x, tiles):
    def get(i, t):
        at = t - DIR_Y[i]
        tile = src[i, x - DIR_X[i], at % tiles]
        if at < 0 or at >= tiles:
            tile = pltpu.roll(tile, DIR_Y[i] % SUB, 0)
        if DIR_Z[i] != 0:
            tile = pltpu.roll(tile, DIR_Z[i] % LANES, 1)
        return tile

    return get


def edges_kernel(dens, vel, top, bottom, sems):
    rows = dens.shape[1]
    last, first = pl.ds(rows - HALO, HALO), pl.ds(0, HALO)
    copies = [
        pltpu.make_async_copy(dens.at[:, last, :], top.at[0], sems.at[0]),
        pltpu.make_async_copy(vel.at[:, :, last, :], top.at[pl.ds(1, 3)], sems.at[1]),
        pltpu.make_async_copy(dens.at[:, first, :], bottom.at[0], sems.at[2]),
        pltpu.make_async_copy(vel.at[:, :, first, :], bottom.at[pl.ds(1, 3)], sems.at[3]),
    ]
    for copy in copies:
        copy.start()
    for copy in copies:
        copy.wait()


def widen_kernel(dens, vel, upper, lower, wide, whole):
    planes, rows, _ = dens.shape
    whole[:, :, :HALO, :] = upper[...]
    whole[:, :, HALO + rows :, :] = lower[...]
    whole[0, :, HALO : HALO + rows, :] = dens[...]
    tiles = wide.shape[2]
    for c in range(3):
        whole[c + 1, :, HALO : HALO + rows, :] = vel[c]
    for f in range(4):
        for p in range(planes):
            for t in range(tiles):
                wide[f, p, t] = whole[f, p, pl.ds(t, SUB, stride=tiles), :]


def split3(value):
    a = value.astype(jnp.bfloat16).astype(jnp.float32)
    rest = value - a
    b = rest.astype(jnp.bfloat16).astype(jnp.float32)
    return a, b, rest - b


def lattice_kernel(place, snap_steps, *refs):
    blocks, refs = refs[:-12], refs[-12:]
    basis, pops, snaps, sums, ping, pong, speeds, views, coarse, rowwise, gram, whole = refs
    planes, tiles, _, lanes = blocks[0].shape[1:]
    reach = STEPS
    span = planes + 2 * reach
    rows = pops.shape[2]
    inner = HALO // tiles
    count = snap_steps.shape[0]

    def put_speed(x, held):
        for c in range(3):
            for half in range(2):
                speeds[x, c, half] = held[2 * half][c] + held[2 * half + 1][c]

    def keep_view(step):
        for c in range(3):
            for half in range(2):
                total = speeds[reach, c, half]
                for p in range(1, planes):
                    total = total + speeds[reach + p, c, half]
                views[step, c, half] = total

    for n, block in enumerate(blocks):
        start = place[n]

        def first(p, carry, block=block, start=start):
            held = []
            for t in range(tiles):
                dens = block[0, p, t]
                vel = [block[c + 1, p, t] for c in range(3)]
                part = dens * (3.0 / 36.0)
                speed = [1.5 * v for v in vel]
                out = relaxed(1.0, dens, [part * v for v in vel], speed, None)
                for i in range(DIRS):
                    ping[i, start + p, t] = out[i]
                held.append(speed)
            put_speed(start + p, held)
            return carry

        lax.fori_loop(0, planes, first, 0)
    keep_view(0)

    src, dst = ping, pong
    for step in range(1, STEPS):

        def later(x, carry, src=src, dst=dst):
            get = streamed(src, x, tiles)
            held = []
            for t in range(tiles):
                pop = [get(i, t) for i in range(DIRS)]
                dens, mom = moments(pop)
                inverse = 1.5 / dens
                speed = [m * inverse for m in mom]
                flow = [m * (OMEGA * 3.0 / 36.0) for m in mom]
                out = relaxed(OMEGA, dens, flow, speed, pop)
                for i in range(DIRS):
                    dst[i, x, t] = out[i]
                held.append(speed)
            put_speed(x, held)
            return carry

        lax.fori_loop(step, span - step, later, 0)
        keep_view(step)
        src, dst = dst, src

    for p in range(planes):
        get = streamed(src, reach + p, tiles)
        for i in range(DIRS):
            for t in range(tiles):
                whole[p, i, pl.ds(t, SUB, stride=tiles), :] = get(i, t)
            pops[i, p] = whole[p, i, HALO : HALO + rows, :]

    halves = [[views[snap_steps[k], c, half] for k in range(count) for c in range(3)] for half in range(2)]
    lane = lax.broadcasted_iota(jnp.int32, (lanes, lanes), 0) // 2
    col = lax.broadcasted_iota(jnp.int32, (lanes, lanes), 1)
    flat = None
    for half in range(2):
        gather = jnp.where(lane + half * (lanes // 2) == col, 1.0, 0.0).astype(jnp.bfloat16)
        stack = jnp.concatenate(halves[half], axis=0)
        for part in split3(stack):
            term = jnp.dot(part.astype(jnp.bfloat16), gather, preferred_element_type=jnp.float32)
            flat = term if flat is None else flat + term
    height = 3 * SUB * count
    coarse[height:, :] = jnp.zeros_like(coarse[height:, :])
    coarse[0:height, :] = flat * (UNIT / (4 * planes) / 1.5)
    rank = basis.shape[1]
    groups = rows // tiles
    total = None
    for c in range(3):
        parts = [coarse[pl.ds(SUB * c + inner + t, SUB, stride=3 * SUB), :] for t in range(groups)]
        snap = jnp.concatenate(parts, axis=1)
        snaps[c] = snap
        a, b, d = split3(snap)
        rowwise[0:rank, :] = basis[c]
        rowwise[rank : rank + 2 * SUB, :] = jnp.concatenate([a, b], axis=0).astype(jnp.bfloat16)
        rowwise[rank + 2 * SUB :, :] = jnp.concatenate([d, jnp.zeros_like(d)], axis=0).astype(jnp.bfloat16)
        term = lax.dot_general(rowwise[...], rowwise[...], NT, preferred_element_type=jnp.float32)
        total = term if total is None else total + term
    gram[...] = jnp.zeros_like(gram)
    gram[:, 0 : total.shape[1]] = total
    half = rank // 2
    lane = lax.broadcasted_iota(jnp.int32, (SUB, lanes), 1)
    row = lax.broadcasted_iota(jnp.int32, (SUB, lanes), 0)
    packed = None
    for j in range(rank // SUB):
        part = gram[SUB * j : SUB * (j + 1), :]
        if SUB * j < half:
            part = jnp.where(lane < half, 0.5 * part, jnp.where(lane < rank, part, 0.0))
        else:
            part = jnp.where((lane >= half) & (lane < rank), 0.5 * part, 0.0)
        shift = pack_shift(j, rank)
        packed = part if packed is None else packed + (pltpu.roll(part, shift, 1) if shift else part)
    crossed = gram[rank : rank + SUB, :] + gram[rank + SUB : rank + 2 * SUB, :]
    crossed = crossed + gram[rank + 2 * SUB : rank + 3 * SUB, :]
    selves = crossed + pltpu.roll(crossed, lanes - SUB, 1) + pltpu.roll(crossed, lanes - 2 * SUB, 1)
    first_lane = lanes - rank
    crossed = pltpu.roll(crossed, first_lane, 1)
    selves = pltpu.roll(pltpu.roll(selves, first_lane - rank, 1), count, 0)
    tail = jnp.where(row < count, crossed, jnp.where(lane < first_lane + count, selves, 0.0))
    packed = jnp.where(lane < first_lane, packed, tail)
    if len(sums.shape) == 2:
        sums[...] = packed
    else:
        for n in range(sums.shape[0]):
            sums[n] = packed


def pack_shift(j, rank):
    half = rank // 2
    if SUB * j < half:
        return rank * j
    return half // SUB * rank + half * (j - half // SUB) - half


def finish_kernel(scale, count, rank, *refs):
    parts, (snaps, basis, coef, factor, modes, flag, gram) = refs[:-7], refs[-7:]
    if len(parts) == 1 and len(parts[0].shape) == 3:
        packed = tree_sum([parts[0][n] for n in range(parts[0].shape[0])])
    else:
        packed = tree_sum([part[...] for part in parts])
    lanes = packed.shape[1]
    half = rank // 2
    lane = lax.broadcasted_iota(jnp.int32, (SUB, lanes), 1)
    row = lax.broadcasted_iota(jnp.int32, (SUB, lanes), 0)
    for j in range(rank // SUB):
        shift = pack_shift(j, rank)
        part = pltpu.roll(packed, lanes - shift, 1) if shift else packed
        if SUB * j >= half:
            part = jnp.where(lane < half, 0.0, part)
        gram[SUB * j : SUB * (j + 1), :] = part
    tail = pltpu.roll(packed, rank, 1)
    proj = jnp.where(row < count, tail, 0.0)[:, 0:rank]
    inner = pltpu.roll(tail, SUB - count, 0)[:, 0:SUB]
    dot = functools.partial(lax.dot_general, precision=HIGHEST, preferred_element_type=jnp.float32)
    turned = dot(proj, gram[:, 0:rank], (((1,), (0,)), ((), ())))
    crossed = dot(proj, proj, NT)
    bent = dot(turned, proj, NT) + dot(proj, turned, NT)
    small = inner - 2.0 * crossed + bent
    r = lax.broadcasted_iota(jnp.int32, (SUB, SUB), 0)
    c = lax.broadcasted_iota(jnp.int32, (SUB, SUB), 1)
    loss = jnp.where((r == c) & (r < count), inner + 2.0 * crossed + bent - 8.0 * small, -1.0)
    flag[0, 0] = jnp.max(jnp.where(loss < 0.0, 0.0, 1.0)).astype(jnp.int32)
    coef[...] = proj[0:count, :]
    resid = []
    thirds = [part.astype(jnp.bfloat16) for part in split3(proj)]
    for n in range(3):
        value = snaps[n]
        for third in thirds:
            value = value - jnp.dot(third, basis[n], preferred_element_type=jnp.float32)
        resid.append(value)
    small = jnp.where((r < count) & (c < count), small, jnp.where(r == c, 1.0, 0.0))
    below = lax.broadcasted_iota(jnp.int32, (SUB, 1), 0)
    pivots = jnp.ones((SUB, 1), jnp.float32)
    for j in range(count):
        pivot = small[j : j + 1, j : j + 1]
        pivots = jnp.where(below == j, pivot, pivots)
        share = jnp.where(below > j, small[:, j : j + 1] / pivot, 0.0)
        resid = [v - share * v[j : j + 1, :] for v in resid]
        small = small - share * small[j : j + 1, :]
    root = jnp.sqrt(pivots)
    upper = jnp.where(c >= r, small / root, 0.0)
    factor[...] = upper[0:count, 0:count] * (1.0 / scale)
    gain = scale / root
    groups = snaps.shape[2] // lanes
    for n in range(3):
        value = resid[n] * gain
        for t in range(groups):
            modes[pl.ds(groups * n + t, count, stride=3 * groups), :] = value[0:count, lanes * t : lanes * (t + 1)]


def tree_sum(parts):
    parts = list(parts)
    while len(parts) > 1:
        parts = [a + b for a, b in zip(parts[::2], parts[1::2])] + ([parts[-1]] if len(parts) % 2 else [])
    return parts[0]


def moved(block, axis, target):
    return lax.ppermute(block, axis, [(i, target(i)) for i in range(lax.axis_size(axis))])


def partners(block, axis, stride, count):
    digit = lambda i: i // stride % count
    if count & (count - 1) == 0:
        return [block] + [
            moved(block, axis, lambda i, j=j: i + ((digit(i) ^ j) - digit(i)) * stride) for j in range(1, count)
        ]
    got = [block] + [
        moved(block, axis, lambda i, j=j: i + ((digit(i) + j) % count - digit(i)) * stride) for j in range(1, count)
    ]
    mine = lax.axis_index(axis) // stride % count
    return list(jnp.roll(jnp.stack(got)[::-1], mine + 1, axis=0))


def digits(size):
    found, rest = [], size
    for base in (8, 4, 2):
        while rest % base == 0:
            found.append(base)
            rest //= base
    base = 3
    while rest > 1:
        while rest % base == 0:
            found.append(base)
            rest //= base
        base += 2
    return found


def summed(sums, n_dev, n_group):
    rounds = []
    for axis, size in (("dev", n_dev), ("group", n_group)):
        stride = 1
        for base in digits(size):
            rounds.append((axis, stride, base))
            stride *= base
    parts = [sums]
    for axis, stride, base in rounds:
        parts = partners(tree_sum(parts), axis, stride, base)
    return parts


def from_residuals(coefficients, snaps, basis, scale):
    modes = basis[:, :, 0, :].astype(jnp.float32)
    count = coefficients.shape[1]
    held = jnp.transpose(snaps[:, :count, :], (1, 0, 2))
    resid = held - jnp.einsum("rk,rab->kab", coefficients, modes, precision=HIGHEST)
    gram = lax.psum(jnp.einsum("kab,lab->kl", resid, resid, precision=HIGHEST), ("group", "dev"))
    lower = jnp.linalg.cholesky(gram)
    solved = []
    for k in range(count):
        value = resid[k]
        for j in range(k):
            value = value - lower[k, j] * solved[j]
        solved.append(value / lower[k, k])
    return lower.T / scale, (jnp.stack(solved) * scale).reshape(-1, LANES)


def ring_blocks(own, n_dev, planes, reach):
    ahead = moved(own, "dev", lambda i: (i - 2) % n_dev)
    behind = moved(own, "dev", lambda i: (i + 2) % n_dev)
    far = moved(own, "dev", lambda i: (i + 3 if i % 2 else i - 3) % n_dev)
    other = moved(own, "dev", lambda i: i ^ 1)
    other_ahead = moved(ahead, "dev", lambda i: i ^ 1)
    other_behind = moved(behind, "dev", lambda i: i ^ 1)
    odd = lax.axis_index("dev") % 2
    offsets = jnp.where(
        odd == 1, jnp.array([0, 2, -2, 3, -1, 1, -3], jnp.int32), jnp.array([0, 2, -2, -3, 1, 3, -1], jnp.int32)
    )
    return [own, ahead, behind, far, other, other_ahead, other_behind], reach + planes * offsets


def per_device(density, velocity, basis, snap_steps):
    planes, rows, lanes = density.shape
    count = snap_steps.shape[0]
    rank = basis.shape[0]
    reach = STEPS
    n_dev, n_group = lax.axis_size("dev"), lax.axis_size("group")
    vmem = pl.BlockSpec(memory_space=pltpu.VMEM)
    smem = pl.BlockSpec(memory_space=pltpu.SMEM)
    f32 = jnp.float32
    params = pltpu.CompilerParams(vmem_limit_bytes=VMEM_LIMIT)

    edge = jax.ShapeDtypeStruct((4, planes, HALO, lanes), f32)
    hbm = pl.BlockSpec(memory_space=pltpu.HBM)
    top, bottom = pl.pallas_call(
        edges_kernel,
        out_shape=(edge, edge),
        in_specs=[hbm, hbm],
        out_specs=(hbm, hbm),
        scratch_shapes=[pltpu.SemaphoreType.DMA((4,))],
        compiler_params=pltpu.CompilerParams(vmem_limit_bytes=62 * 1024 * 1024),
    )(density, velocity)
    upper = moved(top, "group", lambda i: (i + 1) % n_group)
    lower = moved(bottom, "group", lambda i: (i - 1) % n_group)
    wide_rows = rows + 2 * HALO
    tiles = wide_rows // SUB
    own = pl.pallas_call(
        widen_kernel,
        out_shape=jax.ShapeDtypeStruct((4, planes, tiles, SUB, lanes), f32),
        in_specs=[vmem] * 4,
        out_specs=vmem,
        scratch_shapes=[pltpu.VMEM((4, planes, wide_rows, lanes), f32)],
        compiler_params=params,
    )(density, velocity, upper, lower)
    blocks, place = ring_blocks(own, n_dev, planes, reach)
    modes = jnp.transpose(basis[:, :, 0, :], (1, 0, 2))
    span = planes + 2 * reach
    width = basis.shape[3]
    members = n_dev * n_group
    at_once = members <= 32
    pops, snaps, sums = pl.pallas_call(
        lattice_kernel,
        out_shape=(
            jax.ShapeDtypeStruct((DIRS, planes, rows, lanes), f32),
            jax.ShapeDtypeStruct((3, SUB, width), f32),
            jax.ShapeDtypeStruct((members, SUB, lanes) if at_once else (SUB, lanes), f32),
        ),
        in_specs=[smem, smem] + [vmem] * (len(blocks) + 1),
        out_specs=(vmem, vmem, vmem),
        scratch_shapes=[
            pltpu.VMEM((DIRS, span, tiles, SUB, lanes), f32),
            pltpu.VMEM((DIRS, span, tiles, SUB, lanes), f32),
            pltpu.VMEM((span, 3, 2, SUB, lanes), f32),
            pltpu.VMEM((STEPS, 3, 2, SUB, lanes), f32),
            pltpu.VMEM((3 * SUB * SUB, lanes), f32),
            pltpu.VMEM((rank + 4 * SUB, width), jnp.bfloat16),
            pltpu.VMEM((rank + 4 * SUB, lanes), f32),
            pltpu.VMEM((planes, DIRS, wide_rows, lanes), f32),
        ],
        compiler_params=params,
    )(place, snap_steps, *blocks, modes)

    if at_once:
        parts = [lax.all_to_all(sums, ("group", "dev"), 0, 0)]
    else:
        parts = summed(sums, n_dev, n_group)
    scale = math.sqrt(3 * width * members)
    coef, factor, new_modes, flag = pl.pallas_call(
        functools.partial(finish_kernel, scale, count, rank),
        out_shape=(
            jax.ShapeDtypeStruct((count, rank), f32),
            jax.ShapeDtypeStruct((count, count), f32),
            jax.ShapeDtypeStruct((count * 3 * width // lanes, lanes), f32),
            jax.ShapeDtypeStruct((1, 1), jnp.int32),
        ),
        in_specs=[vmem] * (len(parts) + 2),
        out_specs=(vmem, vmem, vmem, smem),
        scratch_shapes=[pltpu.VMEM((rank, lanes), f32)],
        compiler_params=params,
    )(*parts, snaps, modes)
    coefficients = coef.T
    factor, new_modes = lax.cond(
        flag[0, 0] != 0,
        lambda: from_residuals(coefficients, snaps, basis, scale),
        lambda: (factor, new_modes),
    )
    return (pops, coefficients, factor, new_modes.reshape(count, 3, 1, width))


def solution(mesh):
    placed = (
        P("dev", "group", None),
        P(None, "dev", "group", None),
        P(None, None, "dev", "group"),
        P(),
    )
    return jax.shard_map(
        per_device,
        mesh=mesh,
        in_specs=placed,
        out_specs=(P(None, "dev", "group", None), P(), P(), P(None, None, "dev", "group")),
        check_vma=False,
    )
```

```python
import functools
import math

import jax
import jax.numpy as jnp
from jax import lax
from jax.experimental import pallas as pl
from jax.experimental.pallas import tpu as pltpu
from jax.sharding import PartitionSpec as P

STEPS = 6
DIRS = 19
DIR_X = [0, 1, -1, 0, 0, 0, 0, 1, -1, 1, -1, 1, -1, 1, -1, 0, 0, 0, 0]
DIR_Y = [0, 0, 0, 1, -1, 0, 0, 1, 1, -1, -1, 0, 0, 0, 0, 1, -1, 1, -1]
DIR_Z = [0, 0, 0, 0, 0, 1, -1, 0, 0, 0, 0, 1, 1, -1, -1, 1, 1, -1, -1]
OPPOSITE = [(1, 2), (3, 4), (5, 6), (7, 10), (8, 9), (11, 14), (12, 13), (15, 18), (16, 17)]
OMEGA = 1.6
UNIT = 10.0
SUB = 8
LANES = 128
HALO = 8
AT_ONCE = 2
HIGHEST = lax.Precision.HIGHEST
NT = (((1,), (1,)), ((), ()))
VMEM_LIMIT = 48 * 1024 * 1024


def along(direction, parts):
    total = None
    for sign, part in sorted(zip(direction, parts), key=lambda pair: -pair[0]):
        if sign == 0:
            continue
        if total is None:
            total = part if sign > 0 else -part
        else:
            total = total + part if sign > 0 else total - part
    return total


def relaxed(rate, dens, flow, speed, pops):
    keep = 1.0 - rate
    twice = [2.0 * f for f in flow]
    squares = [t * s for t, s in zip(twice, speed)]
    base = (rate / 36.0) * dens - (squares[0] + squares[1] + squares[2]) * (1.0 / 6.0)
    base2 = 2.0 * base
    out = [None] * DIRS

    def put(i, value):
        out[i] = value if pops is None else keep * pops[i] + value

    put(0, 12.0 * base)
    for a, b in OPPOSITE:
        direction = (DIR_X[a], DIR_Y[a], DIR_Z[a])
        if a < 7:
            axis = [abs(d) for d in direction].index(1)
            even = base2 + squares[axis]
            odd = twice[axis]
        else:
            odd = along(direction, flow)
            even = base + odd * along(direction, speed)
        put(a, even + odd)
        put(b, even - odd)
    return out


def moments(pops):
    dens = tree_sum([pops[0]] + [pops[a] + pops[b] for a, b in OPPOSITE])
    diff = {a: pops[a] - pops[b] for a, b in OPPOSITE}
    mom = []
    for table in (DIR_X, DIR_Y, DIR_Z):
        total = None
        for a, _ in OPPOSITE:
            if table[a] == 0:
                continue
            if total is None:
                total = diff[a] if table[a] > 0 else -diff[a]
            else:
                total = total + diff[a] if table[a] > 0 else total - diff[a]
        mom.append(total)
    return dens, mom


def reciprocal(value):
    near = pl.reciprocal(value, approx=True)
    near = near * (2.0 - value * near)
    return near * (2.0 - value * near)


def streamed(src, x, tiles):
    def get(i, t):
        at = t - DIR_Y[i]
        tile = src[i, x - DIR_X[i], at % tiles]
        if at < 0 or at >= tiles:
            tile = pltpu.roll(tile, DIR_Y[i] % SUB, 0)
        if DIR_Z[i] != 0:
            tile = pltpu.roll(tile, DIR_Z[i] % LANES, 1)
        return tile

    return get


def widen_kernel(held, up_dens, up_vel, low_dens, low_vel, wide, whole):
    fields, planes, rows, _ = held.shape
    below = HALO + rows
    whole[0, :, :HALO, :] = up_dens[:, rows - HALO :, :]
    whole[0, :, below:, :] = low_dens[:, :HALO, :]
    for c in range(3):
        whole[c + 1, :, :HALO, :] = up_vel[c, :, rows - HALO :, :]
        whole[c + 1, :, below:, :] = low_vel[c, :, :HALO, :]
    whole[:, :, HALO:below, :] = held[...]
    tiles = wide.shape[2]
    for f in range(fields):
        for p in range(planes):
            for t in range(tiles):
                wide[f, p, t] = whole[f, p, pl.ds(t, SUB, stride=tiles), :]


def split3(value):
    a = value.astype(jnp.bfloat16).astype(jnp.float32)
    rest = value - a
    b = rest.astype(jnp.bfloat16).astype(jnp.float32)
    return a, b, rest - b


def lattice_kernel(place, snap_steps, *refs):
    blocks, refs = refs[:-13], refs[-13:]
    basis, pops, snaps, sums, ping, pong, speeds, views, coarse, rowwise, gram, whole, sems = refs
    planes, tiles, _, lanes = blocks[0].shape[1:]
    reach = STEPS
    span = planes + 2 * reach
    rows = pops.shape[2]
    inner = HALO // tiles
    count = snap_steps.shape[0]

    def put_speed(x, held):
        for c in range(3):
            for half in range(2):
                speeds[x, c, half] = held[2 * half][c] + held[2 * half + 1][c]

    def keep_view(step):
        for c in range(3):
            for half in range(2):
                total = speeds[reach, c, half]
                for p in range(1, planes):
                    total = total + speeds[reach + p, c, half]
                views[step, c, half] = total

    for n, block in enumerate(blocks):
        for p in range(planes):
            x = place[n] + p
            held = []
            for t in range(tiles):
                dens = block[0, p, t]
                vel = [block[c + 1, p, t] for c in range(3)]
                part = dens * (3.0 / 36.0)
                speed = [1.5 * v for v in vel]
                out = relaxed(1.0, dens, [part * v for v in vel], speed, None)
                for i in range(DIRS):
                    ping[i, x, t] = out[i]
                held.append(speed)
            put_speed(x, held)
    keep_view(0)

    src, dst = ping, pong
    for step in range(1, STEPS):
        size = span - 2 * step
        together = math.gcd(size, AT_ONCE)

        def later(n, carry, src=src, dst=dst, step=step, together=together):
            for x in [step + together * n + m for m in range(together)]:
                get = streamed(src, x, tiles)
                held = []
                for t in range(tiles):
                    pop = [get(i, t) for i in range(DIRS)]
                    dens, mom = moments(pop)
                    inverse = 1.5 * reciprocal(dens)
                    speed = [m * inverse for m in mom]
                    flow = [m * (OMEGA * 3.0 / 36.0) for m in mom]
                    out = relaxed(OMEGA, dens, flow, speed, pop)
                    for i in range(DIRS):
                        dst[i, x, t] = out[i]
                    held.append(speed)
                put_speed(x, held)
            return carry

        lax.fori_loop(0, size // together, later, 0)
        keep_view(step)
        src, dst = dst, src

    copies = []
    for p in range(planes):
        get = streamed(src, reach + p, tiles)
        for i in range(DIRS):
            for t in range(tiles):
                whole[p, i, pl.ds(t, SUB, stride=tiles), :] = get(i, t)
        copies.append(pltpu.make_async_copy(whole.at[p, :, pl.ds(HALO, rows), :], pops.at[:, p], sems.at[p]))
        copies[-1].start()

    halves = [[views[snap_steps[k], c, half] for k in range(count) for c in range(3)] for half in range(2)]
    lane = lax.broadcasted_iota(jnp.int32, (lanes, lanes), 0) // 2
    col = lax.broadcasted_iota(jnp.int32, (lanes, lanes), 1)
    flat = None
    for half in range(2):
        gather = jnp.where(lane + half * (lanes // 2) == col, 1.0, 0.0).astype(jnp.bfloat16)
        stack = jnp.concatenate(halves[half], axis=0)
        for part in split3(stack):
            term = jnp.dot(part.astype(jnp.bfloat16), gather, preferred_element_type=jnp.float32)
            flat = term if flat is None else flat + term
    height = 3 * SUB * count
    coarse[height:, :] = jnp.zeros_like(coarse[height:, :])
    coarse[0:height, :] = flat * (UNIT / (4 * planes) / 1.5)
    rank = basis.shape[1]
    groups = rows // tiles
    total = None
    for c in range(3):
        parts = [coarse[pl.ds(SUB * c + inner + t, SUB, stride=3 * SUB), :] for t in range(groups)]
        snap = jnp.concatenate(parts, axis=1)
        snaps[c] = snap
        a, b, d = split3(snap)
        rowwise[0:rank, :] = basis[c]
        rowwise[rank : rank + 2 * SUB, :] = jnp.concatenate([a, b], axis=0).astype(jnp.bfloat16)
        rowwise[rank + 2 * SUB :, :] = jnp.concatenate([d, jnp.zeros_like(d)], axis=0).astype(jnp.bfloat16)
        term = lax.dot_general(rowwise[...], rowwise[...], NT, preferred_element_type=jnp.float32)
        total = term if total is None else total + term
    gram[...] = jnp.zeros_like(gram)
    gram[:, 0 : total.shape[1]] = total
    half = rank // 2
    lane = lax.broadcasted_iota(jnp.int32, (SUB, lanes), 1)
    row = lax.broadcasted_iota(jnp.int32, (SUB, lanes), 0)
    packed = None
    for j in range(rank // SUB):
        part = gram[SUB * j : SUB * (j + 1), :]
        if SUB * j < half:
            part = jnp.where(lane < half, 0.5 * part, jnp.where(lane < rank, part, 0.0))
        else:
            part = jnp.where((lane >= half) & (lane < rank), 0.5 * part, 0.0)
        shift = pack_shift(j, rank)
        packed = part if packed is None else packed + (pltpu.roll(part, shift, 1) if shift else part)
    crossed = gram[rank : rank + SUB, :] + gram[rank + SUB : rank + 2 * SUB, :]
    crossed = crossed + gram[rank + 2 * SUB : rank + 3 * SUB, :]
    selves = crossed + pltpu.roll(crossed, lanes - SUB, 1) + pltpu.roll(crossed, lanes - 2 * SUB, 1)
    first_lane = lanes - rank
    crossed = pltpu.roll(crossed, first_lane, 1)
    selves = pltpu.roll(pltpu.roll(selves, first_lane - rank, 1), count, 0)
    tail = jnp.where(row < count, crossed, jnp.where(lane < first_lane + count, selves, 0.0))
    packed = jnp.where(lane < first_lane, packed, tail)
    if len(sums.shape) == 2:
        sums[...] = packed
    else:
        for n in range(sums.shape[0]):
            sums[n] = packed
    for copy in copies:
        copy.wait()


def pack_shift(j, rank):
    half = rank // 2
    if SUB * j < half:
        return rank * j
    return half // SUB * rank + half * (j - half // SUB) - half


def finish_kernel(scale, count, rank, *refs):
    parts, (snaps, basis, coef, factor, modes, flag, gram) = refs[:-7], refs[-7:]
    if len(parts) == 1 and len(parts[0].shape) == 3:
        packed = tree_sum([parts[0][n] for n in range(parts[0].shape[0])])
    else:
        packed = tree_sum([part[...] for part in parts])
    lanes = packed.shape[1]
    half = rank // 2
    lane = lax.broadcasted_iota(jnp.int32, (SUB, lanes), 1)
    row = lax.broadcasted_iota(jnp.int32, (SUB, lanes), 0)
    for j in range(rank // SUB):
        shift = pack_shift(j, rank)
        part = pltpu.roll(packed, lanes - shift, 1) if shift else packed
        if SUB * j >= half:
            part = jnp.where(lane < half, 0.0, part)
        gram[SUB * j : SUB * (j + 1), :] = part
    tail = pltpu.roll(packed, rank, 1)
    proj = jnp.where(row < count, tail, 0.0)[:, 0:rank]
    inner = pltpu.roll(tail, SUB - count, 0)[:, 0:SUB]
    dot = functools.partial(lax.dot_general, precision=HIGHEST, preferred_element_type=jnp.float32)
    turned = dot(proj, gram[:, 0:rank], (((1,), (0,)), ((), ())))
    crossed = dot(proj, proj, NT)
    bent = dot(turned, proj, NT) + dot(proj, turned, NT)
    small = inner - 2.0 * crossed + bent
    r = lax.broadcasted_iota(jnp.int32, (SUB, SUB), 0)
    c = lax.broadcasted_iota(jnp.int32, (SUB, SUB), 1)
    loss = jnp.where((r == c) & (r < count), inner + 2.0 * crossed + bent - 8.0 * small, -1.0)
    flag[0, 0] = jnp.max(jnp.where(loss < 0.0, 0.0, 1.0)).astype(jnp.int32)
    coef[...] = proj[0:count, :]
    resid = []
    thirds = [part.astype(jnp.bfloat16) for part in split3(proj)]
    for n in range(3):
        value = snaps[n]
        for third in thirds:
            value = value - jnp.dot(third, basis[n], preferred_element_type=jnp.float32)
        resid.append(value)
    small = jnp.where((r < count) & (c < count), small, jnp.where(r == c, 1.0, 0.0))
    below = lax.broadcasted_iota(jnp.int32, (SUB, 1), 0)
    pivots = jnp.ones((SUB, 1), jnp.float32)
    for j in range(count):
        pivot = small[j : j + 1, j : j + 1]
        pivots = jnp.where(below == j, pivot, pivots)
        share = jnp.where(below > j, small[:, j : j + 1] / pivot, 0.0)
        resid = [v - share * v[j : j + 1, :] for v in resid]
        small = small - share * small[j : j + 1, :]
    root = jnp.sqrt(pivots)
    upper = jnp.where(c >= r, small / root, 0.0)
    factor[...] = upper[0:count, 0:count] * (1.0 / scale)
    gain = scale / root
    groups = snaps.shape[2] // lanes
    for n in range(3):
        value = resid[n] * gain
        for t in range(groups):
            modes[pl.ds(groups * n + t, count, stride=3 * groups), :] = value[0:count, lanes * t : lanes * (t + 1)]


def tree_sum(parts):
    parts = list(parts)
    while len(parts) > 1:
        parts = [a + b for a, b in zip(parts[::2], parts[1::2])] + ([parts[-1]] if len(parts) % 2 else [])
    return parts[0]


def moved(block, axis, target):
    return lax.ppermute(block, axis, [(i, target(i)) for i in range(lax.axis_size(axis))])


def partners(block, axis, stride, count):
    digit = lambda i: i // stride % count
    if count & (count - 1) == 0:
        return [block] + [
            moved(block, axis, lambda i, j=j: i + ((digit(i) ^ j) - digit(i)) * stride) for j in range(1, count)
        ]
    got = [block] + [
        moved(block, axis, lambda i, j=j: i + ((digit(i) + j) % count - digit(i)) * stride) for j in range(1, count)
    ]
    mine = lax.axis_index(axis) // stride % count
    return list(jnp.roll(jnp.stack(got)[::-1], mine + 1, axis=0))


def digits(size):
    found, rest = [], size
    for base in (8, 4, 2):
        while rest % base == 0:
            found.append(base)
            rest //= base
    base = 3
    while rest > 1:
        while rest % base == 0:
            found.append(base)
            rest //= base
        base += 2
    return found


def summed(sums, n_dev, n_group):
    rounds = []
    for axis, size in (("dev", n_dev), ("group", n_group)):
        stride = 1
        for base in digits(size):
            rounds.append((axis, stride, base))
            stride *= base
    parts = [sums]
    for axis, stride, base in rounds:
        parts = partners(tree_sum(parts), axis, stride, base)
    return parts


def from_residuals(coefficients, snaps, basis, scale):
    modes = basis[:, :, 0, :].astype(jnp.float32)
    count = coefficients.shape[1]
    held = jnp.transpose(snaps[:, :count, :], (1, 0, 2))
    resid = held - jnp.einsum("rk,rab->kab", coefficients, modes, precision=HIGHEST)
    gram = lax.psum(jnp.einsum("kab,lab->kl", resid, resid, precision=HIGHEST), ("group", "dev"))
    lower = jnp.linalg.cholesky(gram)
    solved = []
    for k in range(count):
        value = resid[k]
        for j in range(k):
            value = value - lower[k, j] * solved[j]
        solved.append(value / lower[k, k])
    return lower.T / scale, (jnp.stack(solved) * scale).reshape(-1, LANES)


def ring_blocks(own, n_dev, planes, reach):
    ahead = moved(own, "dev", lambda i: (i - 2) % n_dev)
    behind = moved(own, "dev", lambda i: (i + 2) % n_dev)
    far = moved(own, "dev", lambda i: (i + 3 if i % 2 else i - 3) % n_dev)
    other = moved(own, "dev", lambda i: i ^ 1)
    other_ahead = moved(ahead, "dev", lambda i: i ^ 1)
    other_behind = moved(behind, "dev", lambda i: i ^ 1)
    odd = lax.axis_index("dev") % 2
    offsets = jnp.where(
        odd == 1, jnp.array([0, 2, -2, 3, -1, 1, -3], jnp.int32), jnp.array([0, 2, -2, -3, 1, 3, -1], jnp.int32)
    )
    return [own, ahead, behind, far, other, other_ahead, other_behind], reach + planes * offsets


def per_device(density, velocity, basis, snap_steps):
    planes, rows, lanes = density.shape
    count = snap_steps.shape[0]
    rank = basis.shape[0]
    reach = STEPS
    n_dev, n_group = lax.axis_size("dev"), lax.axis_size("group")
    vmem = pl.BlockSpec(memory_space=pltpu.VMEM)
    smem = pl.BlockSpec(memory_space=pltpu.SMEM)
    f32 = jnp.float32
    params = pltpu.CompilerParams(vmem_limit_bytes=VMEM_LIMIT)

    up = lambda i: (i + 1) % n_group
    down = lambda i: (i - 1) % n_group
    held = jnp.concatenate([density[None], velocity])
    upper = [moved(array, "group", up) for array in (density, velocity)]
    lower = [moved(array, "group", down) for array in (density, velocity)]
    wide_rows = rows + 2 * HALO
    tiles = wide_rows // SUB
    own = pl.pallas_call(
        widen_kernel,
        out_shape=jax.ShapeDtypeStruct((4, planes, tiles, SUB, lanes), f32),
        in_specs=[vmem] * 5,
        out_specs=vmem,
        scratch_shapes=[pltpu.VMEM((4, planes, wide_rows, lanes), f32)],
        compiler_params=params,
    )(held, *upper, *lower)
    blocks, place = ring_blocks(own, n_dev, planes, reach)
    modes = jnp.transpose(basis[:, :, 0, :], (1, 0, 2))
    span = planes + 2 * reach
    width = basis.shape[3]
    members = n_dev * n_group
    at_once = members <= 32
    pops, snaps, sums = pl.pallas_call(
        lattice_kernel,
        out_shape=(
            jax.ShapeDtypeStruct((DIRS, planes, rows, lanes), f32),
            jax.ShapeDtypeStruct((3, SUB, width), f32),
            jax.ShapeDtypeStruct((members, SUB, lanes) if at_once else (SUB, lanes), f32),
        ),
        in_specs=[smem, smem] + [vmem] * (len(blocks) + 1),
        out_specs=(pl.BlockSpec(memory_space=pltpu.HBM), vmem, vmem),
        scratch_shapes=[
            pltpu.VMEM((DIRS, span, tiles, SUB, lanes), f32),
            pltpu.VMEM((DIRS, span, tiles, SUB, lanes), f32),
            pltpu.VMEM((span, 3, 2, SUB, lanes), f32),
            pltpu.VMEM((STEPS, 3, 2, SUB, lanes), f32),
            pltpu.VMEM((3 * SUB * SUB, lanes), f32),
            pltpu.VMEM((rank + 4 * SUB, width), jnp.bfloat16),
            pltpu.VMEM((rank + 4 * SUB, lanes), f32),
            pltpu.VMEM((planes, DIRS, wide_rows, lanes), f32),
            pltpu.SemaphoreType.DMA((planes,)),
        ],
        compiler_params=params,
    )(place, snap_steps, *blocks, modes)

    if at_once:
        parts = [lax.all_to_all(sums, ("group", "dev"), 0, 0)]
    else:
        parts = summed(sums, n_dev, n_group)
    scale = math.sqrt(3 * width * members)
    coef, factor, new_modes, flag = pl.pallas_call(
        functools.partial(finish_kernel, scale, count, rank),
        out_shape=(
            jax.ShapeDtypeStruct((count, rank), f32),
            jax.ShapeDtypeStruct((count, count), f32),
            jax.ShapeDtypeStruct((count * 3 * width // lanes, lanes), f32),
            jax.ShapeDtypeStruct((1, 1), jnp.int32),
        ),
        in_specs=[vmem] * (len(parts) + 2),
        out_specs=(vmem, vmem, vmem, smem),
        scratch_shapes=[pltpu.VMEM((rank, lanes), f32)],
        compiler_params=params,
    )(*parts, snaps, modes)
    coefficients = coef.T
    factor, new_modes = lax.cond(
        flag[0, 0] != 0,
        lambda: from_residuals(coefficients, snaps, basis, scale),
        lambda: (factor, new_modes),
    )
    return (pops, coefficients, factor, new_modes.reshape(count, 3, 1, width))


def solution(mesh):
    placed = (
        P("dev", "group", None),
        P(None, "dev", "group", None),
        P(None, None, "dev", "group"),
        P(),
    )
    return jax.shard_map(
        per_device,
        mesh=mesh,
        in_specs=placed,
        out_specs=(P(None, "dev", "group", None), P(), P(), P(None, None, "dev", "group")),
        check_vma=False,
    )
```

```python
import functools
import math

import jax
import jax.numpy as jnp
from jax import lax
from jax.experimental import pallas as pl
from jax.experimental.pallas import tpu as pltpu
from jax.sharding import PartitionSpec as P

STEPS = 6
DIRS = 19
DIR_X = [0, 1, -1, 0, 0, 0, 0, 1, -1, 1, -1, 1, -1, 1, -1, 0, 0, 0, 0]
DIR_Y = [0, 0, 0, 1, -1, 0, 0, 1, 1, -1, -1, 0, 0, 0, 0, 1, -1, 1, -1]
DIR_Z = [0, 0, 0, 0, 0, 1, -1, 0, 0, 0, 0, 1, 1, -1, -1, 1, 1, -1, -1]
OPPOSITE = [(1, 2), (3, 4), (5, 6), (7, 10), (8, 9), (11, 14), (12, 13), (15, 18), (16, 17)]
OMEGA = 1.6
KEEP = 1.0 - OMEGA
RATE = OMEGA / KEEP
UNIT = 10.0
SUB = 8
LANES = 128
HALO = 8
AT_ONCE = 4
HIGHEST = lax.Precision.HIGHEST
NT = (((1,), (1,)), ((), ()))
VMEM_LIMIT = 48 * 1024 * 1024


def along(direction, parts):
    total = None
    for sign, part in sorted(zip(direction, parts), key=lambda pair: -pair[0]):
        if sign == 0:
            continue
        if total is None:
            total = part if sign > 0 else -part
        else:
            total = total + part if sign > 0 else total - part
    return total


def relaxed(rate, dens, flow, speed, pops):
    twice = [f + f for f in flow]
    squares = [f * s for f, s in zip(flow, speed)]
    base = (rate / 36.0) * dens - (squares[0] + squares[1] + squares[2]) * (1.0 / 3.0)
    based = [base + square for square in squares]
    out = [None] * DIRS

    def put(i, value):
        out[i] = value if pops is None else pops[i] + value

    put(0, 12.0 * base)
    crossed = {}
    for a, b in OPPOSITE:
        direction = (DIR_X[a], DIR_Y[a], DIR_Z[a])
        axes = [n for n in range(3) if direction[n]]
        if len(axes) == 1:
            even = based[axes[0]] + based[axes[0]]
            odd = twice[axes[0]]
        else:
            m, n = axes
            if (m, n) not in crossed:
                crossed[m, n] = based[m] + squares[n], twice[m] * speed[n]
            both, cross = crossed[m, n]
            even = both + cross if direction[m] * direction[n] > 0 else both - cross
            odd = along(direction, flow)
        put(a, even + odd)
        put(b, even - odd)
    return out


def moments(pops):
    dens = tree_sum([pops[0]] + [pops[a] + pops[b] for a, b in OPPOSITE])
    diff = {a: pops[a] - pops[b] for a, b in OPPOSITE}
    mom = []
    for table in (DIR_X, DIR_Y, DIR_Z):
        total = None
        for a, _ in OPPOSITE:
            if table[a] == 0:
                continue
            if total is None:
                total = diff[a] if table[a] > 0 else -diff[a]
            else:
                total = total + diff[a] if table[a] > 0 else total - diff[a]
        mom.append(total)
    return dens, mom


def reciprocal(value):
    near = pl.reciprocal(value, approx=True)
    near = near * (2.0 - value * near)
    return near * (2.0 - value * near)


def streamed(src, x, tiles):
    def get(i, t):
        at = t - DIR_Y[i]
        tile = src[i, x - DIR_X[i], at % tiles]
        if at < 0 or at >= tiles:
            tile = pltpu.roll(tile, DIR_Y[i] % SUB, 0)
        if DIR_Z[i] != 0:
            tile = pltpu.roll(tile, DIR_Z[i] % LANES, 1)
        return tile

    return get


def edges_kernel(held, top, bottom):
    rows = held.shape[2]
    top[...] = held[:, :, rows - HALO :, :]
    bottom[...] = held[:, :, :HALO, :]


def widen_kernel(held, upper, lower, wide, whole):
    fields, planes, rows, _ = held.shape
    whole[:, :, :HALO, :] = upper[...]
    whole[:, :, HALO : HALO + rows, :] = held[...]
    whole[:, :, HALO + rows :, :] = lower[...]
    tiles = wide.shape[2]
    for f in range(fields):
        for p in range(planes):
            for t in range(tiles):
                wide[f, p, t] = whole[f, p, pl.ds(t, SUB, stride=tiles), :]


def split3(value):
    a = value.astype(jnp.bfloat16).astype(jnp.float32)
    rest = value - a
    b = rest.astype(jnp.bfloat16).astype(jnp.float32)
    return a, b, rest - b


def lattice_kernel(place, snap_steps, *refs):
    blocks, refs = refs[:-13], refs[-13:]
    basis, pops, snaps, sums, ping, pong, speeds, views, coarse, rowwise, gram, whole, sems = refs
    planes, tiles, _, lanes = blocks[0].shape[1:]
    reach = STEPS
    span = planes + 2 * reach
    rows = pops.shape[2]
    inner = HALO // tiles
    count = snap_steps.shape[0]

    def put_speed(x, held):
        for c in range(3):
            for half in range(2):
                speeds[x, c, half] = held[2 * half][c] + held[2 * half + 1][c]

    def keep_view(step):
        for c in range(3):
            for half in range(2):
                total = speeds[reach, c, half]
                for p in range(1, planes):
                    total = total + speeds[reach + p, c, half]
                views[step, c, half] = total

    for n, block in enumerate(blocks):
        for p in range(planes):
            x = place[n] + p
            held = []
            for t in range(tiles):
                dens = block[0, p, t]
                vel = [block[c + 1, p, t] for c in range(3)]
                part = dens * (3.0 / 36.0)
                speed = [1.5 * v for v in vel]
                out = relaxed(1.0, dens, [part * v for v in vel], speed, None)
                for i in range(DIRS):
                    ping[i, x, t] = out[i]
                held.append(speed)
            put_speed(x, held)
    keep_view(0)

    src, dst = ping, pong
    for step in range(1, STEPS):
        size = span - 2 * step
        together = math.gcd(size, AT_ONCE)

        def later(n, carry, src=src, dst=dst, step=step, together=together):
            for x in [step + together * n + m for m in range(together)]:
                get = streamed(src, x, tiles)
                held = []
                for t in range(tiles):
                    pop = [get(i, t) for i in range(DIRS)]
                    dens, mom = moments(pop)
                    inverse = 1.5 * reciprocal(dens)
                    speed = [m * inverse for m in mom]
                    flow = [m * (RATE * 3.0 / 36.0) for m in mom]
                    out = relaxed(RATE, dens, flow, speed, pop)
                    for i in range(DIRS):
                        dst[i, x, t] = out[i]
                    held.append(speed)
                put_speed(x, held)
            return carry

        lax.fori_loop(0, size // together, later, 0)
        keep_view(step)
        src, dst = dst, src

    copies = []
    for p in range(planes):
        get = streamed(src, reach + p, tiles)
        for i in range(DIRS):
            for t in range(tiles):
                whole[p, i, pl.ds(t, SUB, stride=tiles), :] = KEEP ** (STEPS - 1) * get(i, t)
        copies.append(pltpu.make_async_copy(whole.at[p, :, pl.ds(HALO, rows), :], pops.at[:, p], sems.at[p]))
        copies[-1].start()

    halves = [[views[snap_steps[k], c, half] for k in range(count) for c in range(3)] for half in range(2)]
    lane = lax.broadcasted_iota(jnp.int32, (lanes, lanes), 0) // 2
    col = lax.broadcasted_iota(jnp.int32, (lanes, lanes), 1)
    flat = None
    for half in range(2):
        gather = jnp.where(lane + half * (lanes // 2) == col, 1.0, 0.0).astype(jnp.bfloat16)
        stack = jnp.concatenate(halves[half], axis=0)
        for part in split3(stack):
            term = jnp.dot(part.astype(jnp.bfloat16), gather, preferred_element_type=jnp.float32)
            flat = term if flat is None else flat + term
    height = 3 * SUB * count
    coarse[height:, :] = jnp.zeros_like(coarse[height:, :])
    coarse[0:height, :] = flat * (UNIT / (4 * planes) / 1.5)
    rank = basis.shape[1]
    groups = rows // tiles
    total = None
    for c in range(3):
        parts = [coarse[pl.ds(SUB * c + inner + t, SUB, stride=3 * SUB), :] for t in range(groups)]
        snap = jnp.concatenate(parts, axis=1)
        snaps[c] = snap
        a, b, d = split3(snap)
        rowwise[0:rank, :] = basis[c]
        rowwise[rank : rank + 2 * SUB, :] = jnp.concatenate([a, b], axis=0).astype(jnp.bfloat16)
        rowwise[rank + 2 * SUB :, :] = jnp.concatenate([d, jnp.zeros_like(d)], axis=0).astype(jnp.bfloat16)
        term = lax.dot_general(rowwise[...], rowwise[...], NT, preferred_element_type=jnp.float32)
        total = term if total is None else total + term
    gram[...] = jnp.zeros_like(gram)
    gram[:, 0 : total.shape[1]] = total
    half = rank // 2
    lane = lax.broadcasted_iota(jnp.int32, (SUB, lanes), 1)
    row = lax.broadcasted_iota(jnp.int32, (SUB, lanes), 0)
    packed = None
    for j in range(rank // SUB):
        part = gram[SUB * j : SUB * (j + 1), :]
        if SUB * j < half:
            part = jnp.where(lane < half, 0.5 * part, jnp.where(lane < rank, part, 0.0))
        else:
            part = jnp.where((lane >= half) & (lane < rank), 0.5 * part, 0.0)
        shift = pack_shift(j, rank)
        packed = part if packed is None else packed + (pltpu.roll(part, shift, 1) if shift else part)
    crossed = gram[rank : rank + SUB, :] + gram[rank + SUB : rank + 2 * SUB, :]
    crossed = crossed + gram[rank + 2 * SUB : rank + 3 * SUB, :]
    selves = crossed + pltpu.roll(crossed, lanes - SUB, 1) + pltpu.roll(crossed, lanes - 2 * SUB, 1)
    first_lane = lanes - rank
    crossed = pltpu.roll(crossed, first_lane, 1)
    selves = pltpu.roll(pltpu.roll(selves, first_lane - rank, 1), count, 0)
    tail = jnp.where(row < count, crossed, jnp.where(lane < first_lane + count, selves, 0.0))
    packed = jnp.where(lane < first_lane, packed, tail)
    if len(sums.shape) == 2:
        sums[...] = packed
    else:
        for n in range(sums.shape[0]):
            sums[n] = packed
    for copy in copies:
        copy.wait()


def pack_shift(j, rank):
    half = rank // 2
    if SUB * j < half:
        return rank * j
    return half // SUB * rank + half * (j - half // SUB) - half


def residuals(proj, snaps, basis):
    thirds = [part.astype(jnp.bfloat16) for part in split3(proj)]
    resid = []
    for n in range(3):
        value = snaps[n]
        for third in thirds:
            value = value - jnp.dot(third, basis[n], preferred_element_type=jnp.float32)
        resid.append(value)
    return resid


def solve(small, resid, scale, factor, modes):
    count = factor.shape[0]
    r = lax.broadcasted_iota(jnp.int32, (SUB, SUB), 0)
    c = lax.broadcasted_iota(jnp.int32, (SUB, SUB), 1)
    small = jnp.where((r < count) & (c < count), small, jnp.where(r == c, 1.0, 0.0))
    below = lax.broadcasted_iota(jnp.int32, (SUB, 1), 0)
    pivots = jnp.ones((SUB, 1), jnp.float32)
    for j in range(count):
        pivot = small[j : j + 1, j : j + 1]
        pivots = jnp.where(below == j, pivot, pivots)
        share = jnp.where(below > j, small[:, j : j + 1] / pivot, 0.0)
        resid = [v - share * v[j : j + 1, :] for v in resid]
        small = small - share * small[j : j + 1, :]
    root = jnp.sqrt(pivots)
    upper = jnp.where(c >= r, small / root, 0.0)
    factor[...] = upper[0:count, 0:count] * (1.0 / scale)
    gain = scale / root
    groups = resid[0].shape[1] // LANES
    for n in range(3):
        value = resid[n] * gain
        for t in range(groups):
            modes[pl.ds(groups * n + t, count, stride=3 * groups), :] = value[0:count, LANES * t : LANES * (t + 1)]


def finish_kernel(scale, count, rank, *refs):
    parts, (snaps, basis, coef, factor, modes, flag, held, gram) = refs[:-8], refs[-8:]
    if len(parts) == 1 and len(parts[0].shape) == 3:
        packed = tree_sum([parts[0][n] for n in range(parts[0].shape[0])])
    else:
        packed = tree_sum([part[...] for part in parts])
    lanes = packed.shape[1]
    half = rank // 2
    lane = lax.broadcasted_iota(jnp.int32, (SUB, lanes), 1)
    row = lax.broadcasted_iota(jnp.int32, (SUB, lanes), 0)
    for j in range(rank // SUB):
        shift = pack_shift(j, rank)
        part = pltpu.roll(packed, lanes - shift, 1) if shift else packed
        if SUB * j >= half:
            part = jnp.where(lane < half, 0.0, part)
        gram[SUB * j : SUB * (j + 1), :] = part
    tail = pltpu.roll(packed, rank, 1)
    proj = jnp.where(row < count, tail, 0.0)[:, 0:rank]
    held[...] = proj
    coef[...] = proj[0:count, :]
    inner = pltpu.roll(tail, SUB - count, 0)[:, 0:SUB]
    dot = functools.partial(lax.dot_general, precision=HIGHEST, preferred_element_type=jnp.float32)
    turned = dot(proj, gram[:, 0:rank], (((1,), (0,)), ((), ())))
    crossed = dot(proj, proj, NT)
    bent = dot(turned, proj, NT) + dot(proj, turned, NT)
    small = inner - 2.0 * crossed + bent
    r = lax.broadcasted_iota(jnp.int32, (SUB, SUB), 0)
    c = lax.broadcasted_iota(jnp.int32, (SUB, SUB), 1)
    loss = jnp.where((r == c) & (r < count), inner + 2.0 * crossed + bent - 8.0 * small, -1.0)
    flag[0, 0] = jnp.max(jnp.where(loss < 0.0, 0.0, 1.0)).astype(jnp.int32)
    solve(small, residuals(proj, snaps, basis), scale, factor, modes)


def inner_kernel(proj, snaps, basis, gram):
    total = None
    for resid in residuals(proj[...], snaps, basis):
        term = lax.dot_general(resid, resid, NT, precision=HIGHEST, preferred_element_type=jnp.float32)
        total = term if total is None else total + term
    gram[...] = total


def solve_kernel(scale, gram, proj, snaps, basis, factor, modes):
    solve(gram[...], residuals(proj[...], snaps, basis), scale, factor, modes)


def tree_sum(parts):
    parts = list(parts)
    while len(parts) > 1:
        parts = [a + b for a, b in zip(parts[::2], parts[1::2])] + ([parts[-1]] if len(parts) % 2 else [])
    return parts[0]


def moved(block, axis, target):
    return lax.ppermute(block, axis, [(i, target(i)) for i in range(lax.axis_size(axis))])


def partners(block, axis, stride, count):
    digit = lambda i: i // stride % count
    if count & (count - 1) == 0:
        return [block] + [
            moved(block, axis, lambda i, j=j: i + ((digit(i) ^ j) - digit(i)) * stride) for j in range(1, count)
        ]
    got = [block] + [
        moved(block, axis, lambda i, j=j: i + ((digit(i) + j) % count - digit(i)) * stride) for j in range(1, count)
    ]
    mine = lax.axis_index(axis) // stride % count
    return list(jnp.roll(jnp.stack(got)[::-1], mine + 1, axis=0))


def digits(size):
    found, rest = [], size
    for base in (8, 4, 2):
        while rest % base == 0:
            found.append(base)
            rest //= base
    base = 3
    while rest > 1:
        while rest % base == 0:
            found.append(base)
            rest //= base
        base += 2
    return found


def summed(sums, n_dev, n_group):
    rounds = []
    for axis, size in (("dev", n_dev), ("group", n_group)):
        stride = 1
        for base in digits(size):
            rounds.append((axis, stride, base))
            stride *= base
    parts = [sums]
    for axis, stride, base in rounds:
        parts = partners(tree_sum(parts), axis, stride, base)
    return parts


def ring_blocks(own, n_dev, planes, reach):
    ahead = moved(own, "dev", lambda i: (i - 2) % n_dev)
    behind = moved(own, "dev", lambda i: (i + 2) % n_dev)
    far = moved(own, "dev", lambda i: (i + 3 if i % 2 else i - 3) % n_dev)
    other = moved(own, "dev", lambda i: i ^ 1)
    other_ahead = moved(ahead, "dev", lambda i: i ^ 1)
    other_behind = moved(behind, "dev", lambda i: i ^ 1)
    odd = lax.axis_index("dev") % 2
    offsets = jnp.where(
        odd == 1, jnp.array([0, 2, -2, 3, -1, 1, -3], jnp.int32), jnp.array([0, 2, -2, -3, 1, 3, -1], jnp.int32)
    )
    return [own, ahead, behind, far, other, other_ahead, other_behind], reach + planes * offsets


def per_device(density, velocity, basis, snap_steps):
    planes, rows, lanes = density.shape
    count = snap_steps.shape[0]
    rank = basis.shape[0]
    reach = STEPS
    n_dev, n_group = lax.axis_size("dev"), lax.axis_size("group")
    vmem = pl.BlockSpec(memory_space=pltpu.VMEM)
    smem = pl.BlockSpec(memory_space=pltpu.SMEM)
    f32 = jnp.float32
    params = pltpu.CompilerParams(vmem_limit_bytes=VMEM_LIMIT)

    held = jnp.concatenate([density[None], velocity])
    edge = jax.ShapeDtypeStruct((4, planes, HALO, lanes), f32)
    top, bottom = pl.pallas_call(
        edges_kernel, out_shape=(edge, edge), in_specs=[vmem], out_specs=(vmem, vmem), compiler_params=params
    )(held)
    upper = moved(top, "group", lambda i: (i + 1) % n_group)
    lower = moved(bottom, "group", lambda i: (i - 1) % n_group)
    wide_rows = rows + 2 * HALO
    tiles = wide_rows // SUB
    own = pl.pallas_call(
        widen_kernel,
        out_shape=jax.ShapeDtypeStruct((4, planes, tiles, SUB, lanes), f32),
        in_specs=[vmem] * 3,
        out_specs=vmem,
        scratch_shapes=[pltpu.VMEM((4, planes, wide_rows, lanes), f32)],
        compiler_params=params,
    )(held, upper, lower)
    blocks, place = ring_blocks(own, n_dev, planes, reach)
    modes = jnp.transpose(basis[:, :, 0, :], (1, 0, 2))
    span = planes + 2 * reach
    width = basis.shape[3]
    members = n_dev * n_group
    at_once = members <= 32
    pops, snaps, sums = pl.pallas_call(
        lattice_kernel,
        out_shape=(
            jax.ShapeDtypeStruct((DIRS, planes, rows, lanes), f32),
            jax.ShapeDtypeStruct((3, SUB, width), f32),
            jax.ShapeDtypeStruct((members, SUB, lanes) if at_once else (SUB, lanes), f32),
        ),
        in_specs=[smem, smem] + [vmem] * (len(blocks) + 1),
        out_specs=(pl.BlockSpec(memory_space=pltpu.HBM), vmem, vmem),
        scratch_shapes=[
            pltpu.VMEM((DIRS, span, tiles, SUB, lanes), f32),
            pltpu.VMEM((DIRS, span, tiles, SUB, lanes), f32),
            pltpu.VMEM((span, 3, 2, SUB, lanes), f32),
            pltpu.VMEM((STEPS, 3, 2, SUB, lanes), f32),
            pltpu.VMEM((3 * SUB * SUB, lanes), f32),
            pltpu.VMEM((rank + 4 * SUB, width), jnp.bfloat16),
            pltpu.VMEM((rank + 4 * SUB, lanes), f32),
            pltpu.VMEM((planes, DIRS, wide_rows, lanes), f32),
            pltpu.SemaphoreType.DMA((planes,)),
        ],
        compiler_params=params,
    )(place, snap_steps, *blocks, modes)

    if at_once:
        parts = [lax.all_to_all(sums, ("group", "dev"), 0, 0)]
    else:
        parts = summed(sums, n_dev, n_group)
    scale = math.sqrt(3 * width * members)
    solved = (
        jax.ShapeDtypeStruct((count, count), f32),
        jax.ShapeDtypeStruct((count * 3 * width // lanes, lanes), f32),
    )
    coef, factor, new_modes, flag, proj = pl.pallas_call(
        functools.partial(finish_kernel, scale, count, rank),
        out_shape=(
            jax.ShapeDtypeStruct((count, rank), f32),
            *solved,
            jax.ShapeDtypeStruct((1, 1), jnp.int32),
            jax.ShapeDtypeStruct((SUB, rank), f32),
        ),
        in_specs=[vmem] * (len(parts) + 2),
        out_specs=(vmem, vmem, vmem, smem, vmem),
        scratch_shapes=[pltpu.VMEM((rank, lanes), f32)],
        compiler_params=params,
    )(*parts, snaps, modes)
    coefficients = coef.T

    def from_residuals(state):
        gram = pl.pallas_call(
            inner_kernel, out_shape=jax.ShapeDtypeStruct((SUB, SUB), f32), in_specs=[vmem] * 3, out_specs=vmem
        )(proj, snaps, modes)
        gram = lax.psum(gram, ("group", "dev"))
        return (
            jnp.int32(0),
            *pl.pallas_call(
                functools.partial(solve_kernel, scale), out_shape=solved, in_specs=[vmem] * 4, out_specs=(vmem, vmem)
            )(gram, proj, snaps, modes),
        )

    _, factor, new_modes = lax.while_loop(lambda state: state[0] != 0, from_residuals, (flag[0, 0], factor, new_modes))
    return (pops, coefficients, factor, new_modes.reshape(count, 3, 1, width))


def solution(mesh):
    placed = (
        P("dev", "group", None),
        P(None, "dev", "group", None),
        P(None, None, "dev", "group"),
        P(),
    )
    return jax.shard_map(
        per_device,
        mesh=mesh,
        in_specs=placed,
        out_specs=(P(None, "dev", "group", None), P(), P(), P(None, None, "dev", "group")),
        check_vma=False,
    )
```

```python
import functools
import math

import jax
import jax.numpy as jnp
from jax import lax
from jax.experimental import pallas as pl
from jax.experimental.pallas import tpu as pltpu
from jax.sharding import PartitionSpec as P

STEPS = 6
DIRS = 19
DIR_X = [0, 1, -1, 0, 0, 0, 0, 1, -1, 1, -1, 1, -1, 1, -1, 0, 0, 0, 0]
DIR_Y = [0, 0, 0, 1, -1, 0, 0, 1, 1, -1, -1, 0, 0, 0, 0, 1, -1, 1, -1]
DIR_Z = [0, 0, 0, 0, 0, 1, -1, 0, 0, 0, 0, 1, 1, -1, -1, 1, 1, -1, -1]
OPPOSITE = [(1, 2), (3, 4), (5, 6), (7, 10), (8, 9), (11, 14), (12, 13), (15, 18), (16, 17)]
OMEGA = 1.6
KEEP = 1.0 - OMEGA
RATE = OMEGA / KEEP
UNIT = 10.0
SUB = 8
LANES = 128
HALO = 6
AT_ONCE = 4
OFFSETS = [(0, 0), (2, 2), (-2, -2), (-3, 3), (1, -1), (3, 1), (-1, -3)]
HIGHEST = lax.Precision.HIGHEST
NT = (((1,), (1,)), ((), ()))
VMEM_LIMIT = 48 * 1024 * 1024


def along(direction, parts):
    total = None
    for sign, part in sorted(zip(direction, parts), key=lambda pair: -pair[0]):
        if sign == 0:
            continue
        if total is None:
            total = part if sign > 0 else -part
        else:
            total = total + part if sign > 0 else total - part
    return total


def relaxed(rate, dens, flow, speed, pops):
    twice = [f + f for f in flow]
    squares = [f * s for f, s in zip(flow, speed)]
    base = (rate / 36.0) * dens - (squares[0] + squares[1] + squares[2]) * (1.0 / 3.0)
    based = [base + square for square in squares]
    out = [None] * DIRS

    def put(i, value):
        out[i] = value if pops is None else pops[i] + value

    put(0, 12.0 * base)
    crossed = {}
    for a, b in OPPOSITE:
        direction = (DIR_X[a], DIR_Y[a], DIR_Z[a])
        axes = [n for n in range(3) if direction[n]]
        if len(axes) == 1:
            even = based[axes[0]] + based[axes[0]]
            odd = twice[axes[0]]
        else:
            m, n = axes
            if (m, n) not in crossed:
                crossed[m, n] = based[m] + squares[n], twice[m] * speed[n]
            both, cross = crossed[m, n]
            even = both + cross if direction[m] * direction[n] > 0 else both - cross
            odd = along(direction, flow)
        put(a, even + odd)
        put(b, even - odd)
    return out


def moments(pops):
    dens = tree_sum([pops[0]] + [pops[a] + pops[b] for a, b in OPPOSITE])
    diff = {a: pops[a] - pops[b] for a, b in OPPOSITE}
    mom = []
    for table in (DIR_X, DIR_Y, DIR_Z):
        total = None
        for a, _ in OPPOSITE:
            if table[a] == 0:
                continue
            if total is None:
                total = diff[a] if table[a] > 0 else -diff[a]
            else:
                total = total + diff[a] if table[a] > 0 else total - diff[a]
        mom.append(total)
    return dens, mom


def reciprocal(value):
    near = pl.reciprocal(value, approx=True)
    near = near * (2.0 - value * near)
    return near * (2.0 - value * near)


def streamed(src, x, tiles):
    def get(i, t):
        at = t - DIR_Y[i]
        tile = src[i, x - DIR_X[i], at % tiles]
        if at < 0 or at >= tiles:
            tile = pltpu.roll(tile, DIR_Y[i] % SUB, 0)
        if DIR_Z[i] != 0:
            tile = pltpu.roll(tile, DIR_Z[i] % LANES, 1)
        return tile

    return get


def edges_kernel(held, top, bottom):
    rows, edge = held.shape[2], top.shape[2]
    top[...] = held[:, :, rows - edge :, :]
    bottom[...] = held[:, :, :edge, :]


def widen_kernel(held, upper, lower, wide):
    fields, planes, rows, _ = held.shape
    high = rows + 2 * HALO
    for f in range(fields):
        for p in range(planes):
            at = (f * planes + p) * high
            wide[pl.ds(at, HALO), :] = upper[f, p, upper.shape[2] - HALO :, :]
            wide[pl.ds(at + HALO, rows), :] = held[f, p]
            wide[pl.ds(at + HALO + rows, HALO), :] = lower[f, p, :HALO, :]
    wide[pl.ds(fields * planes * high, SUB), :] = jnp.zeros((SUB, LANES), jnp.float32)


def split3(value):
    a = value.astype(jnp.bfloat16).astype(jnp.float32)
    rest = value - a
    b = rest.astype(jnp.bfloat16).astype(jnp.float32)
    return a, b, rest - b


def lattice_kernel(*refs):
    blocks, refs = refs[:-15], refs[-15:]
    snap_steps, basis, pops, snaps, sums, ping, pong, speeds, views, coarse, rowwise, gram, whole, at_steps, sems = refs
    planes, rows, lanes = pops.shape[1:]
    tiles = ping.shape[2]
    reach = STEPS
    span = planes + 2 * reach
    high = rows + 2 * HALO
    count = snap_steps.shape[0]
    steps_copy = pltpu.make_async_copy(snap_steps, at_steps, sems.at[planes])
    steps_copy.start()
    odd = lax.rem(lax.axis_index("dev"), 2)
    place = [reach + planes * (even_at + odd * (odd_at - even_at)) for even_at, odd_at in OFFSETS]

    def put_speed(x, held):
        for c in range(3):
            for half in range(2):
                speeds[x, c, half] = held[2 * half][c] + held[2 * half + 1][c]

    def keep_view(step):
        for c in range(3):
            for half in range(2):
                total = speeds[reach, c, half]
                for p in range(1, planes):
                    total = total + speeds[reach + p, c, half]
                views[step, c, half] = total

    for n, block in enumerate(blocks):
        for p in range(planes):
            x = place[n] + p
            held = []
            for t in range(tiles):
                dens, *vel = [block[pl.ds((f * planes + p) * high + t, SUB, stride=tiles), :] for f in range(4)]
                part = dens * (3.0 / 36.0)
                speed = [1.5 * v for v in vel]
                out = relaxed(1.0, dens, [part * v for v in vel], speed, None)
                for i in range(DIRS):
                    ping[i, x, t] = out[i]
                held.append(speed)
            put_speed(x, held)
    keep_view(0)

    src, dst = ping, pong
    for step in range(1, STEPS):
        size = span - 2 * step
        together = math.gcd(size, AT_ONCE)

        def later(n, carry, src=src, dst=dst, step=step, together=together):
            for x in [step + together * n + m for m in range(together)]:
                get = streamed(src, x, tiles)
                held = []
                for t in range(tiles):
                    pop = [get(i, t) for i in range(DIRS)]
                    dens, mom = moments(pop)
                    inverse = 1.5 * reciprocal(dens)
                    speed = [m * inverse for m in mom]
                    flow = [m * (RATE * 3.0 / 36.0) for m in mom]
                    out = relaxed(RATE, dens, flow, speed, pop)
                    for i in range(DIRS):
                        dst[i, x, t] = out[i]
                    held.append(speed)
                put_speed(x, held)
            return carry

        lax.fori_loop(0, size // together, later, 0)
        keep_view(step)
        src, dst = dst, src

    copies = []
    for p in range(planes):
        get = streamed(src, reach + p, tiles)
        for i in range(DIRS):
            for t in range(tiles):
                whole[p, i, pl.ds(SUB - HALO + t, SUB, stride=tiles), :] = KEEP ** (STEPS - 1) * get(i, t)
        copies.append(pltpu.make_async_copy(whole.at[p, :, pl.ds(SUB, rows), :], pops.at[:, p], sems.at[p]))
        copies[-1].start()

    steps_copy.wait()
    lane = lax.broadcasted_iota(jnp.int32, (lanes, lanes), 0) // 2
    col = lax.broadcasted_iota(jnp.int32, (lanes, lanes), 1)
    flat = None
    start_half, start_sub = HALO // 2 % 2, HALO // 2 // 2
    for half in range(2):
        right = half != start_half
        stack = [views[at_steps[k], c, half] for k in range(count) for c in range(3)]
        if right and start_half == 1:
            stack = [pltpu.roll(view, SUB - 1, 0) for view in stack]
        gather = jnp.where(lane + (lanes // 2 if right else 0) == col, 1.0, 0.0).astype(jnp.bfloat16)
        for part in split3(jnp.concatenate(stack, axis=0)):
            term = jnp.dot(part.astype(jnp.bfloat16), gather, preferred_element_type=jnp.float32)
            flat = term if flat is None else flat + term
    height = 3 * SUB * count
    coarse[height:, :] = jnp.zeros_like(coarse[height:, :])
    coarse[0:height, :] = flat * (UNIT / (4 * planes) / 1.5)
    rank = basis.shape[1]
    groups = rows // tiles
    total = None
    for c in range(3):
        parts = [coarse[pl.ds(SUB * c + start_sub + t, SUB, stride=3 * SUB), :] for t in range(groups)]
        snap = jnp.concatenate(parts, axis=1)
        snaps[c] = snap
        a, b, d = split3(snap)
        rowwise[0:rank, :] = basis[c]
        rowwise[rank : rank + 2 * SUB, :] = jnp.concatenate([a, b], axis=0).astype(jnp.bfloat16)
        rowwise[rank + 2 * SUB :, :] = jnp.concatenate([d, jnp.zeros_like(d)], axis=0).astype(jnp.bfloat16)
        term = lax.dot_general(rowwise[...], rowwise[...], NT, preferred_element_type=jnp.float32)
        total = term if total is None else total + term
    gram[...] = jnp.zeros_like(gram)
    gram[:, 0 : total.shape[1]] = total
    half = rank // 2
    lane = lax.broadcasted_iota(jnp.int32, (SUB, lanes), 1)
    row = lax.broadcasted_iota(jnp.int32, (SUB, lanes), 0)
    packed = None
    for j in range(rank // SUB):
        part = gram[SUB * j : SUB * (j + 1), :]
        if SUB * j < half:
            part = jnp.where(lane < half, 0.5 * part, jnp.where(lane < rank, part, 0.0))
        else:
            part = jnp.where((lane >= half) & (lane < rank), 0.5 * part, 0.0)
        shift = pack_shift(j, rank)
        packed = part if packed is None else packed + (pltpu.roll(part, shift, 1) if shift else part)
    crossed = gram[rank : rank + SUB, :] + gram[rank + SUB : rank + 2 * SUB, :]
    crossed = crossed + gram[rank + 2 * SUB : rank + 3 * SUB, :]
    selves = crossed + pltpu.roll(crossed, lanes - SUB, 1) + pltpu.roll(crossed, lanes - 2 * SUB, 1)
    first_lane = lanes - rank
    crossed = pltpu.roll(crossed, first_lane, 1)
    selves = pltpu.roll(pltpu.roll(selves, first_lane - rank, 1), count, 0)
    tail = jnp.where(row < count, crossed, jnp.where(lane < first_lane + count, selves, 0.0))
    packed = jnp.where(lane < first_lane, packed, tail)
    if len(sums.shape) == 2:
        sums[...] = packed
    else:
        for n in range(sums.shape[0]):
            sums[n] = packed
    for copy in copies:
        copy.wait()


def pack_shift(j, rank):
    half = rank // 2
    if SUB * j < half:
        return rank * j
    return half // SUB * rank + half * (j - half // SUB) - half


def residuals(proj, snaps, basis):
    thirds = [part.astype(jnp.bfloat16) for part in split3(proj)]
    resid = []
    for n in range(3):
        value = snaps[n]
        for third in thirds:
            value = value - jnp.dot(third, basis[n], preferred_element_type=jnp.float32)
        resid.append(value)
    return resid


def solve(small, resid, scale, factor, modes):
    count = factor.shape[0]
    r = lax.broadcasted_iota(jnp.int32, (SUB, SUB), 0)
    c = lax.broadcasted_iota(jnp.int32, (SUB, SUB), 1)
    small = jnp.where((r < count) & (c < count), small, jnp.where(r == c, 1.0, 0.0))
    below = lax.broadcasted_iota(jnp.int32, (SUB, 1), 0)
    pivots = jnp.ones((SUB, 1), jnp.float32)
    for j in range(count):
        pivot = small[j : j + 1, j : j + 1]
        pivots = jnp.where(below == j, pivot, pivots)
        share = jnp.where(below > j, small[:, j : j + 1] / pivot, 0.0)
        resid = [v - share * v[j : j + 1, :] for v in resid]
        small = small - share * small[j : j + 1, :]
    root = jnp.sqrt(pivots)
    upper = jnp.where(c >= r, small / root, 0.0)
    factor[...] = upper[0:count, 0:count] * (1.0 / scale)
    gain = scale / root
    groups = resid[0].shape[1] // LANES
    for n in range(3):
        value = resid[n] * gain
        for t in range(groups):
            modes[pl.ds(groups * n + t, count, stride=3 * groups), :] = value[0:count, LANES * t : LANES * (t + 1)]


def finish_kernel(scale, count, rank, *refs):
    parts, (snaps, basis, coef, factor, modes, flag, held, gram) = refs[:-8], refs[-8:]
    if len(parts) == 1 and len(parts[0].shape) == 3:
        packed = tree_sum([parts[0][n] for n in range(parts[0].shape[0])])
    else:
        packed = tree_sum([part[...] for part in parts])
    lanes = packed.shape[1]
    half = rank // 2
    lane = lax.broadcasted_iota(jnp.int32, (SUB, lanes), 1)
    row = lax.broadcasted_iota(jnp.int32, (SUB, lanes), 0)
    for j in range(rank // SUB):
        shift = pack_shift(j, rank)
        part = pltpu.roll(packed, lanes - shift, 1) if shift else packed
        if SUB * j >= half:
            part = jnp.where(lane < half, 0.0, part)
        gram[SUB * j : SUB * (j + 1), :] = part
    tail = pltpu.roll(packed, rank, 1)
    proj = jnp.where(row < count, tail, 0.0)[:, 0:rank]
    held[...] = proj
    coef[...] = proj[0:count, :]
    inner = pltpu.roll(tail, SUB - count, 0)[:, 0:SUB]
    dot = functools.partial(lax.dot_general, precision=HIGHEST, preferred_element_type=jnp.float32)
    turned = dot(proj, gram[:, 0:rank], (((1,), (0,)), ((), ())))
    crossed = dot(proj, proj, NT)
    bent = dot(turned, proj, NT) + dot(proj, turned, NT)
    small = inner - 2.0 * crossed + bent
    r = lax.broadcasted_iota(jnp.int32, (SUB, SUB), 0)
    c = lax.broadcasted_iota(jnp.int32, (SUB, SUB), 1)
    loss = jnp.where((r == c) & (r < count), inner + 2.0 * crossed + bent - 8.0 * small, -1.0)
    flag[0, 0] = jnp.max(jnp.where(loss < 0.0, 0.0, 1.0)).astype(jnp.int32)
    solve(small, residuals(proj, snaps, basis), scale, factor, modes)


def inner_kernel(proj, snaps, basis, gram):
    total = None
    for resid in residuals(proj[...], snaps, basis):
        term = lax.dot_general(resid, resid, NT, precision=HIGHEST, preferred_element_type=jnp.float32)
        total = term if total is None else total + term
    gram[...] = total


def solve_kernel(scale, gram, proj, snaps, basis, factor, modes):
    solve(gram[...], residuals(proj[...], snaps, basis), scale, factor, modes)


def tree_sum(parts):
    parts = list(parts)
    while len(parts) > 1:
        parts = [a + b for a, b in zip(parts[::2], parts[1::2])] + ([parts[-1]] if len(parts) % 2 else [])
    return parts[0]


def moved(block, axis, target):
    return lax.ppermute(block, axis, [(i, target(i)) for i in range(lax.axis_size(axis))])


def partners(block, axis, stride, count):
    digit = lambda i: i // stride % count
    if count & (count - 1) == 0:
        return [block] + [
            moved(block, axis, lambda i, j=j: i + ((digit(i) ^ j) - digit(i)) * stride) for j in range(1, count)
        ]
    got = [block] + [
        moved(block, axis, lambda i, j=j: i + ((digit(i) + j) % count - digit(i)) * stride) for j in range(1, count)
    ]
    mine = lax.axis_index(axis) // stride % count
    return list(jnp.roll(jnp.stack(got)[::-1], mine + 1, axis=0))


def digits(size):
    found, rest = [], size
    for base in (8, 4, 2):
        while rest % base == 0:
            found.append(base)
            rest //= base
    base = 3
    while rest > 1:
        while rest % base == 0:
            found.append(base)
            rest //= base
        base += 2
    return found


def summed(sums, n_dev, n_group):
    rounds = []
    for axis, size in (("dev", n_dev), ("group", n_group)):
        stride = 1
        for base in digits(size):
            rounds.append((axis, stride, base))
            stride *= base
    parts = [sums]
    for axis, stride, base in rounds:
        parts = partners(tree_sum(parts), axis, stride, base)
    return parts


def ring_blocks(own, n_dev):
    ahead = moved(own, "dev", lambda i: (i - 2) % n_dev)
    behind = moved(own, "dev", lambda i: (i + 2) % n_dev)
    far = moved(own, "dev", lambda i: (i + 3 if i % 2 else i - 3) % n_dev)
    other = moved(own, "dev", lambda i: i ^ 1)
    other_ahead = moved(ahead, "dev", lambda i: i ^ 1)
    other_behind = moved(behind, "dev", lambda i: i ^ 1)
    return [own, ahead, behind, far, other, other_ahead, other_behind]


def per_device(density, velocity, basis, snap_steps):
    planes, rows, lanes = density.shape
    count = snap_steps.shape[0]
    rank = basis.shape[0]
    reach = STEPS
    n_dev, n_group = lax.axis_size("dev"), lax.axis_size("group")
    vmem = pl.BlockSpec(memory_space=pltpu.VMEM)
    smem = pl.BlockSpec(memory_space=pltpu.SMEM)
    f32 = jnp.float32
    params = pltpu.CompilerParams(vmem_limit_bytes=VMEM_LIMIT)

    held = jnp.concatenate([density[None], velocity])
    edge = jax.ShapeDtypeStruct((4, planes, SUB, lanes), f32)
    top, bottom = pl.pallas_call(
        edges_kernel, out_shape=(edge, edge), in_specs=[vmem], out_specs=(vmem, vmem), compiler_params=params
    )(held)
    upper = moved(top, "group", lambda i: (i + 1) % n_group)
    lower = moved(bottom, "group", lambda i: (i - 1) % n_group)
    high = rows + 2 * HALO
    tiles = pl.cdiv(high, SUB)
    own = pl.pallas_call(
        widen_kernel,
        out_shape=jax.ShapeDtypeStruct((4 * planes * high + SUB, lanes), f32),
        in_specs=[vmem] * 3,
        out_specs=vmem,
        compiler_params=params,
    )(held, upper, lower)
    blocks = ring_blocks(own, n_dev)
    modes = jnp.transpose(basis[:, :, 0, :], (1, 0, 2))
    span = planes + 2 * reach
    width = basis.shape[3]
    members = n_dev * n_group
    at_once = members <= 32
    pops, snaps, sums = pl.pallas_call(
        lattice_kernel,
        out_shape=(
            jax.ShapeDtypeStruct((DIRS, planes, rows, lanes), f32),
            jax.ShapeDtypeStruct((3, SUB, width), f32),
            jax.ShapeDtypeStruct((members, SUB, lanes) if at_once else (SUB, lanes), f32),
        ),
        in_specs=[vmem] * len(blocks) + [pl.BlockSpec(memory_space=pl.ANY), vmem],
        out_specs=(pl.BlockSpec(memory_space=pltpu.HBM), vmem, vmem),
        scratch_shapes=[
            pltpu.VMEM((DIRS, span, tiles, SUB, lanes), f32),
            pltpu.VMEM((DIRS, span, tiles, SUB, lanes), f32),
            pltpu.VMEM((span, 3, 2, SUB, lanes), f32),
            pltpu.VMEM((STEPS, 3, 2, SUB, lanes), f32),
            pltpu.VMEM((3 * SUB * SUB, lanes), f32),
            pltpu.VMEM((rank + 4 * SUB, width), jnp.bfloat16),
            pltpu.VMEM((rank + 4 * SUB, lanes), f32),
            pltpu.VMEM((planes, DIRS, SUB * tiles + SUB, lanes), f32),
            pltpu.SMEM((count,), jnp.int32),
            pltpu.SemaphoreType.DMA((planes + 1,)),
        ],
        compiler_params=params,
    )(*blocks, snap_steps, modes)

    if at_once:
        parts = [lax.all_to_all(sums, ("group", "dev"), 0, 0)]
    else:
        parts = summed(sums, n_dev, n_group)
    scale = math.sqrt(3 * width * members)
    solved = (
        jax.ShapeDtypeStruct((count, count), f32),
        jax.ShapeDtypeStruct((count * 3 * width // lanes, lanes), f32),
    )
    coef, factor, new_modes, flag, proj = pl.pallas_call(
        functools.partial(finish_kernel, scale, count, rank),
        out_shape=(
            jax.ShapeDtypeStruct((count, rank), f32),
            *solved,
            jax.ShapeDtypeStruct((1, 1), jnp.int32),
            jax.ShapeDtypeStruct((SUB, rank), f32),
        ),
        in_specs=[vmem] * (len(parts) + 2),
        out_specs=(vmem, vmem, vmem, smem, vmem),
        scratch_shapes=[pltpu.VMEM((rank, lanes), f32)],
        compiler_params=params,
    )(*parts, snaps, modes)
    coefficients = coef.T

    def from_residuals(state):
        gram = pl.pallas_call(
            inner_kernel, out_shape=jax.ShapeDtypeStruct((SUB, SUB), f32), in_specs=[vmem] * 3, out_specs=vmem
        )(proj, snaps, modes)
        gram = lax.psum(gram, ("group", "dev"))
        return (
            jnp.int32(0),
            *pl.pallas_call(
                functools.partial(solve_kernel, scale), out_shape=solved, in_specs=[vmem] * 4, out_specs=(vmem, vmem)
            )(gram, proj, snaps, modes),
        )

    _, factor, new_modes = lax.while_loop(lambda state: state[0] != 0, from_residuals, (flag[0, 0], factor, new_modes))
    return (pops, coefficients, factor, new_modes.reshape(count, 3, 1, width))


def solution(mesh):
    placed = (
        P("dev", "group", None),
        P(None, "dev", "group", None),
        P(None, None, "dev", "group"),
        P(),
    )
    return jax.shard_map(
        per_device,
        mesh=mesh,
        in_specs=placed,
        out_specs=(P(None, "dev", "group", None), P(), P(), P(None, None, "dev", "group")),
        check_vma=False,
    )
```

```python
import functools
import math

import jax
import jax.numpy as jnp
from jax import lax
from jax.experimental import pallas as pl
from jax.experimental.pallas import tpu as pltpu
from jax.sharding import PartitionSpec as P

STEPS = 6
DIRS = 19
DIR_X = [0, 1, -1, 0, 0, 0, 0, 1, -1, 1, -1, 1, -1, 1, -1, 0, 0, 0, 0]
DIR_Y = [0, 0, 0, 1, -1, 0, 0, 1, 1, -1, -1, 0, 0, 0, 0, 1, -1, 1, -1]
DIR_Z = [0, 0, 0, 0, 0, 1, -1, 0, 0, 0, 0, 1, 1, -1, -1, 1, 1, -1, -1]
OPPOSITE = [(1, 2), (3, 4), (5, 6), (7, 10), (8, 9), (11, 14), (12, 13), (15, 18), (16, 17)]
OMEGA = 1.6
KEEP = 1.0 - OMEGA
RATE = OMEGA / KEEP
UNIT = 10.0
SUB = 8
LANES = 128
HALO = 6
AT_ONCE = 2
OFFSETS = [(0, 0), (2, 2), (-2, -2), (1, -1), (-3, 3), (3, 1), (-1, -3)]
HIGHEST = lax.Precision.HIGHEST
NT = (((1,), (1,)), ((), ()))
VMEM_LIMIT = 48 * 1024 * 1024


def along(direction, parts):
    total = None
    for sign, part in sorted(zip(direction, parts), key=lambda pair: -pair[0]):
        if sign == 0:
            continue
        if total is None:
            total = part if sign > 0 else -part
        else:
            total = total + part if sign > 0 else total - part
    return total


def relaxed(rate, dens, flow, speed, pops):
    twice = [f + f for f in flow]
    squares = [f * s for f, s in zip(flow, speed)]
    base = (rate / 36.0) * dens - (squares[0] + squares[1] + squares[2]) * (1.0 / 3.0)
    based = [base + square for square in squares]
    out = [None] * DIRS

    def put(i, value):
        out[i] = value if pops is None else pops[i] + value

    put(0, 12.0 * base)
    crossed = {}
    for a, b in OPPOSITE:
        direction = (DIR_X[a], DIR_Y[a], DIR_Z[a])
        axes = [n for n in range(3) if direction[n]]
        if len(axes) == 1:
            even = based[axes[0]] + based[axes[0]]
            odd = twice[axes[0]]
        else:
            m, n = axes
            if (m, n) not in crossed:
                crossed[m, n] = based[m] + squares[n], twice[m] * speed[n]
            both, cross = crossed[m, n]
            even = both + cross if direction[m] * direction[n] > 0 else both - cross
            odd = along(direction, flow)
        put(a, even + odd)
        put(b, even - odd)
    return out


def moments(pops):
    dens = tree_sum([pops[0]] + [pops[a] + pops[b] for a, b in OPPOSITE])
    diff = {a: pops[a] - pops[b] for a, b in OPPOSITE}
    mom = []
    for table in (DIR_X, DIR_Y, DIR_Z):
        total = None
        for a, _ in OPPOSITE:
            if table[a] == 0:
                continue
            if total is None:
                total = diff[a] if table[a] > 0 else -diff[a]
            else:
                total = total + diff[a] if table[a] > 0 else total - diff[a]
        mom.append(total)
    return dens, mom


def reciprocal(value):
    near = pl.reciprocal(value, approx=True)
    near = near * (2.0 - value * near)
    return near * (2.0 - value * near)


def streamed(src, x, tiles):
    def get(i, t):
        at = t - DIR_Y[i]
        tile = src[i, x - DIR_X[i], at % tiles]
        if at < 0 or at >= tiles:
            tile = pltpu.roll(tile, DIR_Y[i] % SUB, 0)
        if DIR_Z[i] != 0:
            tile = pltpu.roll(tile, DIR_Z[i] % LANES, 1)
        return tile

    return get


def edges_kernel(held, top, bottom):
    rows, edge = held.shape[2], top.shape[2]
    top[...] = held[:, :, rows - edge :, :]
    bottom[...] = held[:, :, :edge, :]


def widen_kernel(held, upper, lower, wide):
    fields, planes, rows, _ = held.shape
    high = rows + 2 * HALO
    for f in range(fields):
        for p in range(planes):
            at = (f * planes + p) * high
            wide[pl.ds(at, HALO), :] = upper[f, p, upper.shape[2] - HALO :, :]
            wide[pl.ds(at + HALO, rows), :] = held[f, p]
            wide[pl.ds(at + HALO + rows, HALO), :] = lower[f, p, :HALO, :]
    wide[pl.ds(fields * planes * high, SUB), :] = jnp.zeros((SUB, LANES), jnp.float32)


def split3(value):
    a = value.astype(jnp.bfloat16).astype(jnp.float32)
    rest = value - a
    b = rest.astype(jnp.bfloat16).astype(jnp.float32)
    return a, b, rest - b


def lattice_kernel(*refs):
    blocks, refs = refs[:-15], refs[-15:]
    snap_steps, basis, pops, snaps, sums, ping, pong, speeds, views, coarse, rowwise, gram, whole, at_steps, sems = refs
    planes, rows, lanes = pops.shape[1:]
    tiles = ping.shape[2]
    reach = STEPS
    span = planes + 2 * reach
    high = rows + 2 * HALO
    count = snap_steps.shape[0]
    steps_copy = pltpu.make_async_copy(snap_steps, at_steps, sems.at[planes])
    steps_copy.start()
    odd = lax.rem(lax.axis_index("dev"), 2)
    place = [reach + planes * (even_at + odd * (odd_at - even_at)) for even_at, odd_at in OFFSETS]

    def put_speed(x, held):
        for c in range(3):
            for half in range(2):
                speeds[x, c, half] = held[2 * half][c] + held[2 * half + 1][c]

    def keep_view(step):
        for c in range(3):
            for half in range(2):
                total = speeds[reach, c, half]
                for p in range(1, planes):
                    total = total + speeds[reach + p, c, half]
                views[step, c, half] = total

    for n, block in enumerate(blocks):
        for p in range(planes):
            x = place[n] + p
            held = []
            for t in range(tiles):
                dens, *vel = [block[pl.ds((f * planes + p) * high + t, SUB, stride=tiles), :] for f in range(4)]
                part = dens * (3.0 / 36.0)
                speed = [1.5 * v for v in vel]
                out = relaxed(1.0, dens, [part * v for v in vel], speed, None)
                for i in range(DIRS):
                    ping[i, x, t] = out[i]
                held.append(speed)
            put_speed(x, held)
    keep_view(0)

    src, dst = ping, pong
    for step in range(1, STEPS):
        size = span - 2 * step
        together = math.gcd(size, AT_ONCE)

        def later(n, carry, src=src, dst=dst, step=step, together=together):
            for x in [step + together * n + m for m in range(together)]:
                get = streamed(src, x, tiles)
                held = []
                for t in range(tiles):
                    pop = [get(i, t) for i in range(DIRS)]
                    dens, mom = moments(pop)
                    inverse = 1.5 * reciprocal(dens)
                    speed = [m * inverse for m in mom]
                    flow = [m * (RATE * 3.0 / 36.0) for m in mom]
                    out = relaxed(RATE, dens, flow, speed, pop)
                    for i in range(DIRS):
                        dst[i, x, t] = out[i]
                    held.append(speed)
                put_speed(x, held)
            return carry

        lax.fori_loop(0, size // together, later, 0)
        keep_view(step)
        src, dst = dst, src

    copies = []
    for p in range(planes):
        get = streamed(src, reach + p, tiles)
        for i in range(DIRS):
            for t in range(tiles):
                whole[p, i, pl.ds(SUB - HALO + t, SUB, stride=tiles), :] = KEEP ** (STEPS - 1) * get(i, t)
        copies.append(pltpu.make_async_copy(whole.at[p, :, pl.ds(SUB, rows), :], pops.at[:, p], sems.at[p]))
        copies[-1].start()

    steps_copy.wait()
    lane = lax.broadcasted_iota(jnp.int32, (lanes, lanes), 0) // 2
    col = lax.broadcasted_iota(jnp.int32, (lanes, lanes), 1)
    flat = None
    start_half, start_sub = HALO // 2 % 2, HALO // 2 // 2
    for half in range(2):
        right = half != start_half
        stack = [views[at_steps[k], c, half] for k in range(count) for c in range(3)]
        if right and start_half == 1:
            stack = [pltpu.roll(view, SUB - 1, 0) for view in stack]
        gather = jnp.where(lane + (lanes // 2 if right else 0) == col, 1.0, 0.0).astype(jnp.bfloat16)
        for part in split3(jnp.concatenate(stack, axis=0)):
            term = jnp.dot(part.astype(jnp.bfloat16), gather, preferred_element_type=jnp.float32)
            flat = term if flat is None else flat + term
    height = 3 * SUB * count
    coarse[height:, :] = jnp.zeros_like(coarse[height:, :])
    coarse[0:height, :] = flat * (UNIT / (4 * planes) / 1.5)
    rank = basis.shape[1]
    groups = rows // tiles
    total = None
    for c in range(3):
        parts = [coarse[pl.ds(SUB * c + start_sub + t, SUB, stride=3 * SUB), :] for t in range(groups)]
        snap = jnp.concatenate(parts, axis=1)
        snaps[c] = snap
        a, b, d = split3(snap)
        rowwise[0:rank, :] = basis[c]
        rowwise[rank : rank + 2 * SUB, :] = jnp.concatenate([a, b], axis=0).astype(jnp.bfloat16)
        rowwise[rank + 2 * SUB :, :] = jnp.concatenate([d, jnp.zeros_like(d)], axis=0).astype(jnp.bfloat16)
        term = lax.dot_general(rowwise[...], rowwise[...], NT, preferred_element_type=jnp.float32)
        total = term if total is None else total + term
    gram[...] = jnp.zeros_like(gram)
    gram[:, 0 : total.shape[1]] = total
    half = rank // 2
    lane = lax.broadcasted_iota(jnp.int32, (SUB, lanes), 1)
    row = lax.broadcasted_iota(jnp.int32, (SUB, lanes), 0)
    packed = None
    for j in range(rank // SUB):
        part = gram[SUB * j : SUB * (j + 1), :]
        if SUB * j < half:
            part = jnp.where(lane < half, 0.5 * part, jnp.where(lane < rank, part, 0.0))
        else:
            part = jnp.where((lane >= half) & (lane < rank), 0.5 * part, 0.0)
        shift = pack_shift(j, rank)
        packed = part if packed is None else packed + (pltpu.roll(part, shift, 1) if shift else part)
    crossed = gram[rank : rank + SUB, :] + gram[rank + SUB : rank + 2 * SUB, :]
    crossed = crossed + gram[rank + 2 * SUB : rank + 3 * SUB, :]
    selves = crossed + pltpu.roll(crossed, lanes - SUB, 1) + pltpu.roll(crossed, lanes - 2 * SUB, 1)
    first_lane = lanes - rank
    crossed = pltpu.roll(crossed, first_lane, 1)
    selves = pltpu.roll(pltpu.roll(selves, first_lane - rank, 1), count, 0)
    tail = jnp.where(row < count, crossed, jnp.where(lane < first_lane + count, selves, 0.0))
    packed = jnp.where(lane < first_lane, packed, tail)
    if len(sums.shape) == 2:
        sums[...] = packed
    else:
        for n in range(sums.shape[0]):
            sums[n] = packed
    for copy in copies:
        copy.wait()


def pack_shift(j, rank):
    half = rank // 2
    if SUB * j < half:
        return rank * j
    return half // SUB * rank + half * (j - half // SUB) - half


def residuals(proj, snaps, basis):
    thirds = [part.astype(jnp.bfloat16) for part in split3(proj)]
    resid = []
    for n in range(3):
        value = snaps[n]
        for third in thirds:
            value = value - jnp.dot(third, basis[n], preferred_element_type=jnp.float32)
        resid.append(value)
    return resid


def solve(small, resid, scale, factor, modes):
    count = factor.shape[0]
    r = lax.broadcasted_iota(jnp.int32, (SUB, SUB), 0)
    c = lax.broadcasted_iota(jnp.int32, (SUB, SUB), 1)
    small = jnp.where((r < count) & (c < count), small, jnp.where(r == c, 1.0, 0.0))
    below = lax.broadcasted_iota(jnp.int32, (SUB, 1), 0)
    pivots = jnp.ones((SUB, 1), jnp.float32)
    for j in range(count):
        pivot = small[j : j + 1, j : j + 1]
        pivots = jnp.where(below == j, pivot, pivots)
        share = jnp.where(below > j, small[:, j : j + 1] / pivot, 0.0)
        resid = [v - share * v[j : j + 1, :] for v in resid]
        small = small - share * small[j : j + 1, :]
    root = jnp.sqrt(pivots)
    upper = jnp.where(c >= r, small / root, 0.0)
    factor[...] = upper[0:count, 0:count] * (1.0 / scale)
    gain = scale / root
    groups = resid[0].shape[1] // LANES
    for n in range(3):
        value = resid[n] * gain
        for t in range(groups):
            modes[pl.ds(groups * n + t, count, stride=3 * groups), :] = value[0:count, LANES * t : LANES * (t + 1)]


def finish_kernel(scale, count, rank, *refs):
    parts, (snaps, basis, coef, factor, modes, flag, held, gram) = refs[:-8], refs[-8:]
    if len(parts) == 1 and len(parts[0].shape) == 3:
        packed = tree_sum([parts[0][n] for n in range(parts[0].shape[0])])
    else:
        packed = tree_sum([part[...] for part in parts])
    lanes = packed.shape[1]
    half = rank // 2
    lane = lax.broadcasted_iota(jnp.int32, (SUB, lanes), 1)
    row = lax.broadcasted_iota(jnp.int32, (SUB, lanes), 0)
    for j in range(rank // SUB):
        shift = pack_shift(j, rank)
        part = pltpu.roll(packed, lanes - shift, 1) if shift else packed
        if SUB * j >= half:
            part = jnp.where(lane < half, 0.0, part)
        gram[SUB * j : SUB * (j + 1), :] = part
    tail = pltpu.roll(packed, rank, 1)
    proj = jnp.where(row < count, tail, 0.0)[:, 0:rank]
    held[...] = proj
    coef[...] = proj[0:count, :]
    inner = pltpu.roll(tail, SUB - count, 0)[:, 0:SUB]
    dot = functools.partial(lax.dot_general, precision=HIGHEST, preferred_element_type=jnp.float32)
    turned = dot(proj, gram[:, 0:rank], (((1,), (0,)), ((), ())))
    crossed = dot(proj, proj, NT)
    bent = dot(turned, proj, NT) + dot(proj, turned, NT)
    small = inner - 2.0 * crossed + bent
    r = lax.broadcasted_iota(jnp.int32, (SUB, SUB), 0)
    c = lax.broadcasted_iota(jnp.int32, (SUB, SUB), 1)
    loss = jnp.where((r == c) & (r < count), inner + 2.0 * crossed + bent - 8.0 * small, -1.0)
    lost = jnp.max(jnp.max(jnp.where(loss < 0.0, 0.0, 1.0), axis=1, keepdims=True), axis=0, keepdims=True)
    flag[...] = lost.astype(jnp.int32)
    solve(small, residuals(proj, snaps, basis), scale, factor, modes)


def inner_kernel(proj, snaps, basis, gram):
    total = None
    for resid in residuals(proj[...], snaps, basis):
        term = lax.dot_general(resid, resid, NT, precision=HIGHEST, preferred_element_type=jnp.float32)
        total = term if total is None else total + term
    gram[...] = total


def solve_kernel(scale, gram, proj, snaps, basis, factor, modes):
    solve(gram[...], residuals(proj[...], snaps, basis), scale, factor, modes)


def tree_sum(parts):
    parts = list(parts)
    while len(parts) > 1:
        parts = [a + b for a, b in zip(parts[::2], parts[1::2])] + ([parts[-1]] if len(parts) % 2 else [])
    return parts[0]


def moved(block, axis, target):
    return lax.ppermute(block, axis, [(i, target(i)) for i in range(lax.axis_size(axis))])


def partners(block, axis, stride, count):
    digit = lambda i: i // stride % count
    if count & (count - 1) == 0:
        return [block] + [
            moved(block, axis, lambda i, j=j: i + ((digit(i) ^ j) - digit(i)) * stride) for j in range(1, count)
        ]
    got = [block] + [
        moved(block, axis, lambda i, j=j: i + ((digit(i) + j) % count - digit(i)) * stride) for j in range(1, count)
    ]
    mine = lax.axis_index(axis) // stride % count
    return list(jnp.roll(jnp.stack(got)[::-1], mine + 1, axis=0))


def digits(size):
    found, rest = [], size
    for base in (8, 4, 2):
        while rest % base == 0:
            found.append(base)
            rest //= base
    base = 3
    while rest > 1:
        while rest % base == 0:
            found.append(base)
            rest //= base
        base += 2
    return found


def summed(sums, n_dev, n_group):
    rounds = []
    for axis, size in (("dev", n_dev), ("group", n_group)):
        stride = 1
        for base in digits(size):
            rounds.append((axis, stride, base))
            stride *= base
    parts = [sums]
    for axis, stride, base in rounds:
        parts = partners(tree_sum(parts), axis, stride, base)
    return parts


def ring_blocks(own, n_dev):
    ahead = moved(own, "dev", lambda i: (i - 2) % n_dev)
    behind = moved(own, "dev", lambda i: (i + 2) % n_dev)
    other = moved(own, "dev", lambda i: i ^ 1)
    far = moved(own, "dev", lambda i: (i + 3 if i % 2 else i - 3) % n_dev)
    other_ahead = moved(ahead, "dev", lambda i: i ^ 1)
    other_behind = moved(behind, "dev", lambda i: i ^ 1)
    return [own, ahead, behind, other, far, other_ahead, other_behind]


def per_device(density, velocity, basis, snap_steps):
    planes, rows, lanes = density.shape
    count = snap_steps.shape[0]
    rank = basis.shape[0]
    reach = STEPS
    n_dev, n_group = lax.axis_size("dev"), lax.axis_size("group")
    vmem = pl.BlockSpec(memory_space=pltpu.VMEM)
    f32 = jnp.float32
    params = pltpu.CompilerParams(vmem_limit_bytes=VMEM_LIMIT)

    held = jnp.concatenate([density[None], velocity])
    edge = jax.ShapeDtypeStruct((4, planes, SUB, lanes), f32)
    top, bottom = pl.pallas_call(
        edges_kernel, out_shape=(edge, edge), in_specs=[vmem], out_specs=(vmem, vmem), compiler_params=params
    )(held)
    upper = moved(top, "group", lambda i: (i + 1) % n_group)
    lower = moved(bottom, "group", lambda i: (i - 1) % n_group)
    high = rows + 2 * HALO
    tiles = pl.cdiv(high, SUB)
    own = pl.pallas_call(
        widen_kernel,
        out_shape=jax.ShapeDtypeStruct((4 * planes * high + SUB, lanes), f32),
        in_specs=[vmem] * 3,
        out_specs=vmem,
        compiler_params=params,
    )(held, upper, lower)
    blocks = ring_blocks(own, n_dev)
    modes = jnp.transpose(basis[:, :, 0, :], (1, 0, 2))
    span = planes + 2 * reach
    width = basis.shape[3]
    members = n_dev * n_group
    at_once = members <= 32
    pops, snaps, sums = pl.pallas_call(
        lattice_kernel,
        out_shape=(
            jax.ShapeDtypeStruct((DIRS, planes, rows, lanes), f32),
            jax.ShapeDtypeStruct((3, SUB, width), f32),
            jax.ShapeDtypeStruct((members, SUB, lanes) if at_once else (SUB, lanes), f32),
        ),
        in_specs=[vmem] * len(blocks) + [pl.BlockSpec(memory_space=pl.ANY), vmem],
        out_specs=(pl.BlockSpec(memory_space=pltpu.HBM), vmem, vmem),
        scratch_shapes=[
            pltpu.VMEM((DIRS, span, tiles, SUB, lanes), f32),
            pltpu.VMEM((DIRS, span, tiles, SUB, lanes), f32),
            pltpu.VMEM((span, 3, 2, SUB, lanes), f32),
            pltpu.VMEM((STEPS, 3, 2, SUB, lanes), f32),
            pltpu.VMEM((3 * SUB * SUB, lanes), f32),
            pltpu.VMEM((rank + 4 * SUB, width), jnp.bfloat16),
            pltpu.VMEM((rank + 4 * SUB, lanes), f32),
            pltpu.VMEM((planes, DIRS, SUB * tiles + SUB, lanes), f32),
            pltpu.SMEM((count,), jnp.int32),
            pltpu.SemaphoreType.DMA((planes + 1,)),
        ],
        compiler_params=params,
    )(*blocks, snap_steps, modes)

    if at_once:
        parts = [lax.all_to_all(sums, ("group", "dev"), 0, 0)]
    else:
        parts = summed(sums, n_dev, n_group)
    scale = math.sqrt(3 * width * members)
    solved = (
        jax.ShapeDtypeStruct((count, count), f32),
        jax.ShapeDtypeStruct((count * 3 * width // lanes, lanes), f32),
    )
    coef, factor, new_modes, flag, proj = pl.pallas_call(
        functools.partial(finish_kernel, scale, count, rank),
        out_shape=(
            jax.ShapeDtypeStruct((count, rank), f32),
            *solved,
            jax.ShapeDtypeStruct((1, 1), jnp.int32),
            jax.ShapeDtypeStruct((SUB, rank), f32),
        ),
        in_specs=[vmem] * (len(parts) + 2),
        out_specs=(vmem,) * 5,
        scratch_shapes=[pltpu.VMEM((rank, lanes), f32)],
        compiler_params=params,
    )(*parts, snaps, modes)
    coefficients = coef.T

    def from_residuals(state):
        gram = pl.pallas_call(
            inner_kernel, out_shape=jax.ShapeDtypeStruct((SUB, SUB), f32), in_specs=[vmem] * 3, out_specs=vmem
        )(proj, snaps, modes)
        gram = lax.psum(gram, ("group", "dev"))
        return (
            jnp.int32(0),
            *pl.pallas_call(
                functools.partial(solve_kernel, scale), out_shape=solved, in_specs=[vmem] * 4, out_specs=(vmem, vmem)
            )(gram, proj, snaps, modes),
        )

    _, factor, new_modes = lax.while_loop(lambda state: state[0] != 0, from_residuals, (flag[0, 0], factor, new_modes))
    return (pops, coefficients, factor, new_modes.reshape(count, 3, 1, width))


def solution(mesh):
    placed = (
        P("dev", "group", None),
        P(None, "dev", "group", None),
        P(None, None, "dev", "group"),
        P(),
    )
    return jax.shard_map(
        per_device,
        mesh=mesh,
        in_specs=placed,
        out_specs=(P(None, "dev", "group", None), P(), P(), P(None, None, "dev", "group")),
        check_vma=False,
    )
```

```python
import functools
import math

import jax
import jax.numpy as jnp
from jax import lax
from jax.experimental import pallas as pl
from jax.experimental.pallas import tpu as pltpu
from jax.sharding import PartitionSpec as P

STEPS = 6
DIRS = 19
DIR_X = [0, 1, -1, 0, 0, 0, 0, 1, -1, 1, -1, 1, -1, 1, -1, 0, 0, 0, 0]
DIR_Y = [0, 0, 0, 1, -1, 0, 0, 1, 1, -1, -1, 0, 0, 0, 0, 1, -1, 1, -1]
DIR_Z = [0, 0, 0, 0, 0, 1, -1, 0, 0, 0, 0, 1, 1, -1, -1, 1, 1, -1, -1]
OPPOSITE = [(1, 2), (3, 4), (5, 6), (7, 10), (8, 9), (11, 14), (12, 13), (15, 18), (16, 17)]
OMEGA = 1.6
KEEP = 1.0 - OMEGA
RATE = OMEGA / KEEP
UNIT = 10.0
SUB = 8
LANES = 128
HALO = 6
AT_ONCE = 6
OFFSETS = [(0, 0), (2, 2), (-2, -2), (1, -1), (-3, 3), (3, 1), (-1, -3)]
HIGHEST = lax.Precision.HIGHEST
NT = (((1,), (1,)), ((), ()))
VMEM_LIMIT = 48 * 1024 * 1024


def along(direction, parts):
    total = None
    for sign, part in sorted(zip(direction, parts), key=lambda pair: -pair[0]):
        if sign == 0:
            continue
        if total is None:
            total = part if sign > 0 else -part
        else:
            total = total + part if sign > 0 else total - part
    return total


def relaxed(rate, dens, flow, speed, pops):
    twice = [f + f for f in flow]
    squares = [f * s for f, s in zip(flow, speed)]
    base = (rate / 36.0) * dens - (squares[0] + squares[1] + squares[2]) * (1.0 / 3.0)
    based = [base + square for square in squares]
    out = [None] * DIRS

    def put(i, value):
        out[i] = value if pops is None else pops[i] + value

    put(0, 12.0 * base)
    crossed = {}
    for a, b in OPPOSITE:
        direction = (DIR_X[a], DIR_Y[a], DIR_Z[a])
        axes = [n for n in range(3) if direction[n]]
        if len(axes) == 1:
            even = based[axes[0]] + based[axes[0]]
            odd = twice[axes[0]]
        else:
            m, n = axes
            if (m, n) not in crossed:
                crossed[m, n] = based[m] + squares[n], twice[m] * speed[n]
            both, cross = crossed[m, n]
            even = both + cross if direction[m] * direction[n] > 0 else both - cross
            odd = along(direction, flow)
        put(a, even + odd)
        put(b, even - odd)
    return out


def moments(pops):
    dens = tree_sum([pops[0]] + [pops[a] + pops[b] for a, b in OPPOSITE])
    diff = {a: pops[a] - pops[b] for a, b in OPPOSITE}
    mom = []
    for table in (DIR_X, DIR_Y, DIR_Z):
        total = None
        for a, _ in OPPOSITE:
            if table[a] == 0:
                continue
            if total is None:
                total = diff[a] if table[a] > 0 else -diff[a]
            else:
                total = total + diff[a] if table[a] > 0 else total - diff[a]
        mom.append(total)
    return dens, mom


def reciprocal(value):
    near = pl.reciprocal(value, approx=True)
    near = near * (2.0 - value * near)
    return near * (2.0 - value * near)


def streamed(src, x, tiles):
    def get(i, t):
        at = t - DIR_Y[i]
        tile = src[i, x - DIR_X[i], at % tiles]
        if at < 0 or at >= tiles:
            tile = pltpu.roll(tile, DIR_Y[i] % SUB, 0)
        if DIR_Z[i] != 0:
            tile = pltpu.roll(tile, DIR_Z[i] % LANES, 1)
        return tile

    return get


def edges_kernel(held, top, bottom):
    rows, edge = held.shape[2], top.shape[2]
    top[...] = held[:, :, rows - edge :, :]
    bottom[...] = held[:, :, :edge, :]


def widen_kernel(held, upper, lower, wide):
    fields, planes, rows, _ = held.shape
    high = rows + 2 * HALO
    for f in range(fields):
        for p in range(planes):
            at = (f * planes + p) * high
            wide[pl.ds(at, HALO), :] = upper[f, p, upper.shape[2] - HALO :, :]
            wide[pl.ds(at + HALO, rows), :] = held[f, p]
            wide[pl.ds(at + HALO + rows, HALO), :] = lower[f, p, :HALO, :]
    wide[pl.ds(fields * planes * high, SUB), :] = jnp.zeros((SUB, LANES), jnp.float32)


def split3(value):
    a = value.astype(jnp.bfloat16).astype(jnp.float32)
    rest = value - a
    b = rest.astype(jnp.bfloat16).astype(jnp.float32)
    return a, b, rest - b


def lattice_kernel(*refs):
    blocks, refs = refs[:-15], refs[-15:]
    snap_steps, basis, pops, snaps, sums, ping, pong, speeds, views, coarse, rowwise, gram, whole, at_steps, sems = refs
    planes, rows, lanes = pops.shape[1:]
    tiles = ping.shape[2]
    reach = STEPS
    span = planes + 2 * reach
    high = rows + 2 * HALO
    count = snap_steps.shape[0]
    steps_copy = pltpu.make_async_copy(snap_steps, at_steps, sems.at[planes])
    steps_copy.start()
    odd = lax.rem(lax.axis_index("dev"), 2)
    place = [reach + planes * (even_at + odd * (odd_at - even_at)) for even_at, odd_at in OFFSETS]

    def put_speed(x, held):
        for c in range(3):
            for half in range(2):
                speeds[x, c, half] = held[2 * half][c] + held[2 * half + 1][c]

    def keep_view(step):
        for c in range(3):
            for half in range(2):
                total = speeds[reach, c, half]
                for p in range(1, planes):
                    total = total + speeds[reach + p, c, half]
                views[step, c, half] = total

    for n, block in enumerate(blocks):
        for p in range(planes):
            x = place[n] + p
            held = []
            for t in range(tiles):
                dens, *vel = [block[pl.ds((f * planes + p) * high + t, SUB, stride=tiles), :] for f in range(4)]
                part = dens * (3.0 / 36.0)
                speed = [1.5 * v for v in vel]
                out = relaxed(1.0, dens, [part * v for v in vel], speed, None)
                for i in range(DIRS):
                    ping[i, x, t] = out[i]
                held.append(speed)
            put_speed(x, held)
    keep_view(0)

    src, dst = ping, pong
    for step in range(1, STEPS):
        size = span - 2 * step
        together = max(n for n in range(1, AT_ONCE + 1) if size % n == 0)

        def later(n, carry, src=src, dst=dst, step=step, together=together):
            for x in [step + together * n + m for m in range(together)]:
                get = streamed(src, x, tiles)
                held = []
                for t in range(tiles):
                    pop = [get(i, t) for i in range(DIRS)]
                    dens, mom = moments(pop)
                    inverse = 1.5 * reciprocal(dens)
                    speed = [m * inverse for m in mom]
                    flow = [m * (RATE * 3.0 / 36.0) for m in mom]
                    out = relaxed(RATE, dens, flow, speed, pop)
                    for i in range(DIRS):
                        dst[i, x, t] = out[i]
                    held.append(speed)
                put_speed(x, held)
            return carry

        if together == size:
            later(0, 0)
        else:
            lax.fori_loop(0, size // together, later, 0)
        keep_view(step)
        src, dst = dst, src

    copies = []
    for p in range(planes):
        get = streamed(src, reach + p, tiles)
        for i in range(DIRS):
            for t in range(tiles):
                whole[p, i, pl.ds(SUB - HALO + t, SUB, stride=tiles), :] = KEEP ** (STEPS - 1) * get(i, t)
        copies.append(pltpu.make_async_copy(whole.at[p, :, pl.ds(SUB, rows), :], pops.at[:, p], sems.at[p]))
        copies[-1].start()

    steps_copy.wait()
    lane = lax.broadcasted_iota(jnp.int32, (lanes, lanes), 0) // 2
    col = lax.broadcasted_iota(jnp.int32, (lanes, lanes), 1)
    flat = None
    start_half, start_sub = HALO // 2 % 2, HALO // 2 // 2
    for half in range(2):
        right = half != start_half
        stack = [views[at_steps[k], c, half] for k in range(count) for c in range(3)]
        if right and start_half == 1:
            stack = [pltpu.roll(view, SUB - 1, 0) for view in stack]
        gather = jnp.where(lane + (lanes // 2 if right else 0) == col, 1.0, 0.0).astype(jnp.bfloat16)
        for part in split3(jnp.concatenate(stack, axis=0)):
            term = jnp.dot(part.astype(jnp.bfloat16), gather, preferred_element_type=jnp.float32)
            flat = term if flat is None else flat + term
    height = 3 * SUB * count
    coarse[height:, :] = jnp.zeros_like(coarse[height:, :])
    coarse[0:height, :] = flat * (UNIT / (4 * planes) / 1.5)
    rank = basis.shape[1]
    groups = rows // tiles
    total = None
    for c in range(3):
        parts = [coarse[pl.ds(SUB * c + start_sub + t, SUB, stride=3 * SUB), :] for t in range(groups)]
        snap = jnp.concatenate(parts, axis=1)
        snaps[c] = snap
        a, b, d = split3(snap)
        rowwise[0:rank, :] = basis[c]
        rowwise[rank : rank + 2 * SUB, :] = jnp.concatenate([a, b], axis=0).astype(jnp.bfloat16)
        rowwise[rank + 2 * SUB :, :] = jnp.concatenate([d, jnp.zeros_like(d)], axis=0).astype(jnp.bfloat16)
        term = lax.dot_general(rowwise[...], rowwise[...], NT, preferred_element_type=jnp.float32)
        total = term if total is None else total + term
    gram[...] = jnp.zeros_like(gram)
    gram[:, 0 : total.shape[1]] = total
    half = rank // 2
    lane = lax.broadcasted_iota(jnp.int32, (SUB, lanes), 1)
    row = lax.broadcasted_iota(jnp.int32, (SUB, lanes), 0)
    packed = None
    for j in range(rank // SUB):
        part = gram[SUB * j : SUB * (j + 1), :]
        if SUB * j < half:
            part = jnp.where(lane < half, 0.5 * part, jnp.where(lane < rank, part, 0.0))
        else:
            part = jnp.where((lane >= half) & (lane < rank), 0.5 * part, 0.0)
        shift = pack_shift(j, rank)
        packed = part if packed is None else packed + (pltpu.roll(part, shift, 1) if shift else part)
    crossed = gram[rank : rank + SUB, :] + gram[rank + SUB : rank + 2 * SUB, :]
    crossed = crossed + gram[rank + 2 * SUB : rank + 3 * SUB, :]
    selves = crossed + pltpu.roll(crossed, lanes - SUB, 1) + pltpu.roll(crossed, lanes - 2 * SUB, 1)
    first_lane = lanes - rank
    crossed = pltpu.roll(crossed, first_lane, 1)
    selves = pltpu.roll(pltpu.roll(selves, first_lane - rank, 1), count, 0)
    tail = jnp.where(row < count, crossed, jnp.where(lane < first_lane + count, selves, 0.0))
    packed = jnp.where(lane < first_lane, packed, tail)
    if len(sums.shape) == 2:
        sums[...] = packed
    else:
        for n in range(sums.shape[0]):
            sums[n] = packed
    for copy in copies:
        copy.wait()


def pack_shift(j, rank):
    half = rank // 2
    if SUB * j < half:
        return rank * j
    return half // SUB * rank + half * (j - half // SUB) - half


def residuals(proj, snaps, basis):
    thirds = [part.astype(jnp.bfloat16) for part in split3(proj)]
    resid = []
    for n in range(3):
        value = snaps[n]
        for third in thirds:
            value = value - jnp.dot(third, basis[n], preferred_element_type=jnp.float32)
        resid.append(value)
    return resid


def solve(small, resid, scale, factor, modes):
    count = factor.shape[0]
    r = lax.broadcasted_iota(jnp.int32, (SUB, SUB), 0)
    c = lax.broadcasted_iota(jnp.int32, (SUB, SUB), 1)
    small = jnp.where((r < count) & (c < count), small, jnp.where(r == c, 1.0, 0.0))
    below = lax.broadcasted_iota(jnp.int32, (SUB, 1), 0)
    pivots = jnp.ones((SUB, 1), jnp.float32)
    for j in range(count):
        pivot = small[j : j + 1, j : j + 1]
        pivots = jnp.where(below == j, pivot, pivots)
        share = jnp.where(below > j, small[:, j : j + 1] / pivot, 0.0)
        resid = [v - share * v[j : j + 1, :] for v in resid]
        small = small - share * small[j : j + 1, :]
    root = jnp.sqrt(pivots)
    upper = jnp.where(c >= r, small / root, 0.0)
    factor[...] = upper[0:count, 0:count] * (1.0 / scale)
    gain = scale / root
    groups = resid[0].shape[1] // LANES
    for n in range(3):
        value = resid[n] * gain
        for t in range(groups):
            modes[pl.ds(groups * n + t, count, stride=3 * groups), :] = value[0:count, LANES * t : LANES * (t + 1)]


def finish_kernel(scale, count, rank, *refs):
    parts, (snaps, basis, coef, factor, modes, flag, held, gram) = refs[:-8], refs[-8:]
    if len(parts) == 1 and len(parts[0].shape) == 3:
        packed = tree_sum([parts[0][n] for n in range(parts[0].shape[0])])
    else:
        packed = tree_sum([part[...] for part in parts])
    lanes = packed.shape[1]
    half = rank // 2
    lane = lax.broadcasted_iota(jnp.int32, (SUB, lanes), 1)
    row = lax.broadcasted_iota(jnp.int32, (SUB, lanes), 0)
    for j in range(rank // SUB):
        shift = pack_shift(j, rank)
        part = pltpu.roll(packed, lanes - shift, 1) if shift else packed
        if SUB * j >= half:
            part = jnp.where(lane < half, 0.0, part)
        gram[SUB * j : SUB * (j + 1), :] = part
    tail = pltpu.roll(packed, rank, 1)
    proj = jnp.where(row < count, tail, 0.0)[:, 0:rank]
    held[...] = proj
    coef[...] = proj[0:count, :]
    inner = pltpu.roll(tail, SUB - count, 0)[:, 0:SUB]
    dot = functools.partial(lax.dot_general, precision=HIGHEST, preferred_element_type=jnp.float32)
    turned = dot(proj, gram[:, 0:rank], (((1,), (0,)), ((), ())))
    crossed = dot(proj, proj, NT)
    bent = dot(turned, proj, NT) + dot(proj, turned, NT)
    small = inner - 2.0 * crossed + bent
    r = lax.broadcasted_iota(jnp.int32, (SUB, SUB), 0)
    c = lax.broadcasted_iota(jnp.int32, (SUB, SUB), 1)
    loss = jnp.where((r == c) & (r < count), inner + 2.0 * crossed + bent - 8.0 * small, -1.0)
    lost = jnp.max(jnp.max(jnp.where(loss < 0.0, 0.0, 1.0), axis=1, keepdims=True), axis=0, keepdims=True)
    flag[...] = lost.astype(jnp.int32)
    solve(small, residuals(proj, snaps, basis), scale, factor, modes)


def inner_kernel(proj, snaps, basis, gram):
    total = None
    for resid in residuals(proj[...], snaps, basis):
        term = lax.dot_general(resid, resid, NT, precision=HIGHEST, preferred_element_type=jnp.float32)
        total = term if total is None else total + term
    gram[...] = total


def solve_kernel(scale, gram, proj, snaps, basis, factor, modes):
    solve(gram[...], residuals(proj[...], snaps, basis), scale, factor, modes)


def tree_sum(parts):
    parts = list(parts)
    while len(parts) > 1:
        parts = [a + b for a, b in zip(parts[::2], parts[1::2])] + ([parts[-1]] if len(parts) % 2 else [])
    return parts[0]


def moved(block, axis, target):
    return lax.ppermute(block, axis, [(i, target(i)) for i in range(lax.axis_size(axis))])


def partners(block, axis, stride, count):
    digit = lambda i: i // stride % count
    if count & (count - 1) == 0:
        return [block] + [
            moved(block, axis, lambda i, j=j: i + ((digit(i) ^ j) - digit(i)) * stride) for j in range(1, count)
        ]
    got = [block] + [
        moved(block, axis, lambda i, j=j: i + ((digit(i) + j) % count - digit(i)) * stride) for j in range(1, count)
    ]
    mine = lax.axis_index(axis) // stride % count
    return list(jnp.roll(jnp.stack(got)[::-1], mine + 1, axis=0))


def digits(size):
    found, rest = [], size
    for base in (8, 4, 2):
        while rest % base == 0:
            found.append(base)
            rest //= base
    base = 3
    while rest > 1:
        while rest % base == 0:
            found.append(base)
            rest //= base
        base += 2
    return found


def summed(sums, n_dev, n_group):
    rounds = []
    for axis, size in (("dev", n_dev), ("group", n_group)):
        stride = 1
        for base in digits(size):
            rounds.append((axis, stride, base))
            stride *= base
    parts = [sums]
    for axis, stride, base in rounds:
        parts = partners(tree_sum(parts), axis, stride, base)
    return parts


def ring_blocks(own, n_dev):
    ahead = moved(own, "dev", lambda i: (i - 2) % n_dev)
    behind = moved(own, "dev", lambda i: (i + 2) % n_dev)
    other = moved(own, "dev", lambda i: i ^ 1)
    far = moved(own, "dev", lambda i: (i + 3 if i % 2 else i - 3) % n_dev)
    other_ahead = moved(ahead, "dev", lambda i: i ^ 1)
    other_behind = moved(behind, "dev", lambda i: i ^ 1)
    return [own, ahead, behind, other, far, other_ahead, other_behind]


def per_device(density, velocity, basis, snap_steps):
    planes, rows, lanes = density.shape
    count = snap_steps.shape[0]
    rank = basis.shape[0]
    reach = STEPS
    n_dev, n_group = lax.axis_size("dev"), lax.axis_size("group")
    vmem = pl.BlockSpec(memory_space=pltpu.VMEM)
    f32 = jnp.float32
    params = pltpu.CompilerParams(vmem_limit_bytes=VMEM_LIMIT)

    held = jnp.concatenate([density[None], velocity])
    edge = jax.ShapeDtypeStruct((4, planes, SUB, lanes), f32)
    top, bottom = pl.pallas_call(
        edges_kernel, out_shape=(edge, edge), in_specs=[vmem], out_specs=(vmem, vmem), compiler_params=params
    )(held)
    upper = moved(top, "group", lambda i: (i + 1) % n_group)
    lower = moved(bottom, "group", lambda i: (i - 1) % n_group)
    high = rows + 2 * HALO
    tiles = pl.cdiv(high, SUB)
    own = pl.pallas_call(
        widen_kernel,
        out_shape=jax.ShapeDtypeStruct((4 * planes * high + SUB, lanes), f32),
        in_specs=[vmem] * 3,
        out_specs=vmem,
        compiler_params=params,
    )(held, upper, lower)
    blocks = ring_blocks(own, n_dev)
    modes = jnp.transpose(basis[:, :, 0, :], (1, 0, 2))
    span = planes + 2 * reach
    width = basis.shape[3]
    members = n_dev * n_group
    at_once = members <= 32
    pops, snaps, sums = pl.pallas_call(
        lattice_kernel,
        out_shape=(
            jax.ShapeDtypeStruct((DIRS, planes, rows, lanes), f32),
            jax.ShapeDtypeStruct((3, SUB, width), f32),
            jax.ShapeDtypeStruct((members, SUB, lanes) if at_once else (SUB, lanes), f32),
        ),
        in_specs=[vmem] * len(blocks) + [pl.BlockSpec(memory_space=pl.ANY), vmem],
        out_specs=(pl.BlockSpec(memory_space=pltpu.HBM), vmem, vmem),
        scratch_shapes=[
            pltpu.VMEM((DIRS, span, tiles, SUB, lanes), f32),
            pltpu.VMEM((DIRS, span, tiles, SUB, lanes), f32),
            pltpu.VMEM((span, 3, 2, SUB, lanes), f32),
            pltpu.VMEM((STEPS, 3, 2, SUB, lanes), f32),
            pltpu.VMEM((3 * SUB * SUB, lanes), f32),
            pltpu.VMEM((rank + 4 * SUB, width), jnp.bfloat16),
            pltpu.VMEM((rank + 4 * SUB, lanes), f32),
            pltpu.VMEM((planes, DIRS, SUB * tiles + SUB, lanes), f32),
            pltpu.SMEM((count,), jnp.int32),
            pltpu.SemaphoreType.DMA((planes + 1,)),
        ],
        compiler_params=params,
    )(*blocks, snap_steps, modes)

    if at_once:
        parts = [lax.all_to_all(sums, ("group", "dev"), 0, 0)]
    else:
        parts = summed(sums, n_dev, n_group)
    scale = math.sqrt(3 * width * members)
    solved = (
        jax.ShapeDtypeStruct((count, count), f32),
        jax.ShapeDtypeStruct((count * 3 * width // lanes, lanes), f32),
    )
    coef, factor, new_modes, flag, proj = pl.pallas_call(
        functools.partial(finish_kernel, scale, count, rank),
        out_shape=(
            jax.ShapeDtypeStruct((count, rank), f32),
            *solved,
            jax.ShapeDtypeStruct((1, 1), jnp.int32),
            jax.ShapeDtypeStruct((SUB, rank), f32),
        ),
        in_specs=[vmem] * (len(parts) + 2),
        out_specs=(vmem,) * 5,
        scratch_shapes=[pltpu.VMEM((rank, lanes), f32)],
        compiler_params=params,
    )(*parts, snaps, modes)
    coefficients = coef.T

    def from_residuals(state):
        gram = pl.pallas_call(
            inner_kernel, out_shape=jax.ShapeDtypeStruct((SUB, SUB), f32), in_specs=[vmem] * 3, out_specs=vmem
        )(proj, snaps, modes)
        gram = lax.psum(gram, ("group", "dev"))
        return (
            jnp.int32(0),
            *pl.pallas_call(
                functools.partial(solve_kernel, scale), out_shape=solved, in_specs=[vmem] * 4, out_specs=(vmem, vmem)
            )(gram, proj, snaps, modes),
        )

    _, factor, new_modes = lax.while_loop(lambda state: state[0] != 0, from_residuals, (flag[0, 0], factor, new_modes))
    return (pops, coefficients, factor, new_modes.reshape(count, 3, 1, width))


def solution(mesh):
    placed = (
        P("dev", "group", None),
        P(None, "dev", "group", None),
        P(None, None, "dev", "group"),
        P(),
    )
    return jax.shard_map(
        per_device,
        mesh=mesh,
        in_specs=placed,
        out_specs=(P(None, "dev", "group", None), P(), P(), P(None, None, "dev", "group")),
        check_vma=False,
    )
```

```python
import functools
import math

import jax
import jax.numpy as jnp
from jax import lax
from jax.experimental import pallas as pl
from jax.experimental.pallas import tpu as pltpu
from jax.sharding import PartitionSpec as P

STEPS = 6
DIRS = 19
DIR_X = [0, 1, -1, 0, 0, 0, 0, 1, -1, 1, -1, 1, -1, 1, -1, 0, 0, 0, 0]
DIR_Y = [0, 0, 0, 1, -1, 0, 0, 1, 1, -1, -1, 0, 0, 0, 0, 1, -1, 1, -1]
DIR_Z = [0, 0, 0, 0, 0, 1, -1, 0, 0, 0, 0, 1, 1, -1, -1, 1, 1, -1, -1]
OPPOSITE = [(1, 2), (3, 4), (5, 6), (7, 10), (8, 9), (11, 14), (12, 13), (15, 18), (16, 17)]
OMEGA = 1.6
KEEP = 1.0 - OMEGA
RATE = OMEGA / KEEP
UNIT = 10.0
SUB = 8
LANES = 128
HALO = 6
AT_ONCE = 12
OFFSETS = [(0, 0), (2, 2), (-2, -2), (1, -1), (-3, 3), (3, 1), (-1, -3)]
HIGHEST = lax.Precision.HIGHEST
NT = (((1,), (1,)), ((), ()))
VMEM_LIMIT = 48 * 1024 * 1024


def along(direction, parts):
    total = None
    for sign, part in sorted(zip(direction, parts), key=lambda pair: -pair[0]):
        if sign == 0:
            continue
        if total is None:
            total = part if sign > 0 else -part
        else:
            total = total + part if sign > 0 else total - part
    return total


def relaxed(rate, dens, flow, speed, pops):
    twice = [f + f for f in flow]
    squares = [f * s for f, s in zip(flow, speed)]
    base = (rate / 36.0) * dens - (squares[0] + squares[1] + squares[2]) * (1.0 / 3.0)
    based = [base + square for square in squares]
    out = [None] * DIRS

    def put(i, value):
        out[i] = value if pops is None else pops[i] + value

    put(0, 12.0 * base)
    crossed = {}
    for a, b in OPPOSITE:
        direction = (DIR_X[a], DIR_Y[a], DIR_Z[a])
        axes = [n for n in range(3) if direction[n]]
        if len(axes) == 1:
            even = based[axes[0]] + based[axes[0]]
            odd = twice[axes[0]]
        else:
            m, n = axes
            if (m, n) not in crossed:
                crossed[m, n] = based[m] + squares[n], twice[m] * speed[n]
            both, cross = crossed[m, n]
            even = both + cross if direction[m] * direction[n] > 0 else both - cross
            odd = along(direction, flow)
        put(a, even + odd)
        put(b, even - odd)
    return out


def moments(pops):
    dens = tree_sum([pops[0]] + [pops[a] + pops[b] for a, b in OPPOSITE])
    diff = {a: pops[a] - pops[b] for a, b in OPPOSITE}
    mom = []
    for table in (DIR_X, DIR_Y, DIR_Z):
        total = None
        for a, _ in OPPOSITE:
            if table[a] == 0:
                continue
            if total is None:
                total = diff[a] if table[a] > 0 else -diff[a]
            else:
                total = total + diff[a] if table[a] > 0 else total - diff[a]
        mom.append(total)
    return dens, mom


def reciprocal(value):
    near = pl.reciprocal(value, approx=True)
    near = near * (2.0 - value * near)
    return near * (2.0 - value * near)


def streamed(src, x, tiles):
    def get(i, t):
        at = t - DIR_Y[i]
        tile = src[i, x - DIR_X[i], at % tiles]
        if at < 0 or at >= tiles:
            tile = pltpu.roll(tile, DIR_Y[i] % SUB, 0)
        if DIR_Z[i] != 0:
            tile = pltpu.roll(tile, DIR_Z[i] % LANES, 1)
        return tile

    return get


def edges_kernel(held, top, bottom):
    rows, edge = held.shape[2], top.shape[2]
    top[...] = held[:, :, rows - edge :, :]
    bottom[...] = held[:, :, :edge, :]


def widen_kernel(held, upper, lower, wide):
    fields, planes, rows, _ = held.shape
    high = rows + 2 * HALO
    for f in range(fields):
        for p in range(planes):
            at = (f * planes + p) * high
            wide[pl.ds(at, HALO), :] = upper[f, p, upper.shape[2] - HALO :, :]
            wide[pl.ds(at + HALO, rows), :] = held[f, p]
            wide[pl.ds(at + HALO + rows, HALO), :] = lower[f, p, :HALO, :]
    wide[pl.ds(fields * planes * high, SUB), :] = jnp.zeros((SUB, LANES), jnp.float32)


def split3(value):
    a = value.astype(jnp.bfloat16).astype(jnp.float32)
    rest = value - a
    b = rest.astype(jnp.bfloat16).astype(jnp.float32)
    return a, b, rest - b


def lattice_kernel(*refs):
    blocks, refs = refs[:-15], refs[-15:]
    snap_steps, basis, pops, snaps, sums, ping, pong, speeds, views, coarse, rowwise, gram, whole, at_steps, sems = refs
    planes, rows, lanes = pops.shape[1:]
    tiles = ping.shape[2]
    reach = STEPS
    span = planes + 2 * reach
    high = rows + 2 * HALO
    count = snap_steps.shape[0]
    steps_copy = pltpu.make_async_copy(snap_steps, at_steps, sems.at[planes])
    steps_copy.start()
    odd = lax.rem(lax.axis_index("dev"), 2)
    place = [reach + planes * (even_at + odd * (odd_at - even_at)) for even_at, odd_at in OFFSETS]

    def put_speed(x, held):
        for c in range(3):
            for half in range(2):
                speeds[x, c, half] = held[2 * half][c] + held[2 * half + 1][c]

    def keep_view(step):
        for c in range(3):
            for half in range(2):
                total = speeds[reach, c, half]
                for p in range(1, planes):
                    total = total + speeds[reach + p, c, half]
                views[step, c, half] = total

    for n, block in enumerate(blocks):
        for p in range(planes):
            x = place[n] + p
            held = []
            for t in range(tiles):
                dens, *vel = [block[pl.ds((f * planes + p) * high + t, SUB, stride=tiles), :] for f in range(4)]
                part = dens * (3.0 / 36.0)
                speed = [1.5 * v for v in vel]
                out = relaxed(1.0, dens, [part * v for v in vel], speed, None)
                for i in range(DIRS):
                    ping[i, x, t] = out[i]
                held.append(speed)
            put_speed(x, held)
    keep_view(0)

    src, dst = ping, pong
    for step in range(1, STEPS):
        size = span - 2 * step
        together = max(n for n in range(1, AT_ONCE + 1) if size % n == 0)

        def later(n, carry, src=src, dst=dst, step=step, together=together):
            for x in [step + together * n + m for m in range(together)]:
                get = streamed(src, x, tiles)
                held = []
                for t in range(tiles):
                    pop = [get(i, t) for i in range(DIRS)]
                    dens, mom = moments(pop)
                    inverse = 1.5 * reciprocal(dens)
                    speed = [m * inverse for m in mom]
                    flow = [m * (RATE * 3.0 / 36.0) for m in mom]
                    out = relaxed(RATE, dens, flow, speed, pop)
                    for i in range(DIRS):
                        dst[i, x, t] = out[i]
                    held.append(speed)
                put_speed(x, held)
            return carry

        if together == size:
            later(0, 0)
        else:
            lax.fori_loop(0, size // together, later, 0)
        keep_view(step)
        src, dst = dst, src

    copies = []
    for p in range(planes):
        get = streamed(src, reach + p, tiles)
        for i in range(DIRS):
            for t in range(tiles):
                whole[p, i, pl.ds(SUB - HALO + t, SUB, stride=tiles), :] = KEEP ** (STEPS - 1) * get(i, t)
        copies.append(pltpu.make_async_copy(whole.at[p, :, pl.ds(SUB, rows), :], pops.at[:, p], sems.at[p]))
        copies[-1].start()

    steps_copy.wait()
    lane = lax.broadcasted_iota(jnp.int32, (lanes, lanes), 0) // 2
    col = lax.broadcasted_iota(jnp.int32, (lanes, lanes), 1)
    flat = None
    start_half, start_sub = HALO // 2 % 2, HALO // 2 // 2
    for half in range(2):
        right = half != start_half
        stack = [views[at_steps[k], c, half] for k in range(count) for c in range(3)]
        if right and start_half == 1:
            stack = [pltpu.roll(view, SUB - 1, 0) for view in stack]
        gather = jnp.where(lane + (lanes // 2 if right else 0) == col, 1.0, 0.0).astype(jnp.bfloat16)
        for part in split3(jnp.concatenate(stack, axis=0)):
            term = jnp.dot(part.astype(jnp.bfloat16), gather, preferred_element_type=jnp.float32)
            flat = term if flat is None else flat + term
    height = 3 * SUB * count
    coarse[height:, :] = jnp.zeros_like(coarse[height:, :])
    coarse[0:height, :] = flat * (UNIT / (4 * planes) / 1.5)
    rank = basis.shape[1]
    groups = rows // tiles
    total = None
    for c in range(3):
        parts = [coarse[pl.ds(SUB * c + start_sub + t, SUB, stride=3 * SUB), :] for t in range(groups)]
        snap = jnp.concatenate(parts, axis=1)
        snaps[c] = snap
        a, b, d = split3(snap)
        rowwise[0:rank, :] = basis[c]
        rowwise[rank : rank + 2 * SUB, :] = jnp.concatenate([a, b], axis=0).astype(jnp.bfloat16)
        rowwise[rank + 2 * SUB :, :] = jnp.concatenate([d, jnp.zeros_like(d)], axis=0).astype(jnp.bfloat16)
        term = lax.dot_general(rowwise[...], rowwise[...], NT, preferred_element_type=jnp.float32)
        total = term if total is None else total + term
    gram[...] = jnp.zeros_like(gram)
    gram[:, 0 : total.shape[1]] = total
    half = rank // 2
    lane = lax.broadcasted_iota(jnp.int32, (SUB, lanes), 1)
    row = lax.broadcasted_iota(jnp.int32, (SUB, lanes), 0)
    packed = None
    for j in range(rank // SUB):
        part = gram[SUB * j : SUB * (j + 1), :]
        if SUB * j < half:
            part = jnp.where(lane < half, 0.5 * part, jnp.where(lane < rank, part, 0.0))
        else:
            part = jnp.where((lane >= half) & (lane < rank), 0.5 * part, 0.0)
        shift = pack_shift(j, rank)
        packed = part if packed is None else packed + (pltpu.roll(part, shift, 1) if shift else part)
    crossed = gram[rank : rank + SUB, :] + gram[rank + SUB : rank + 2 * SUB, :]
    crossed = crossed + gram[rank + 2 * SUB : rank + 3 * SUB, :]
    selves = crossed + pltpu.roll(crossed, lanes - SUB, 1) + pltpu.roll(crossed, lanes - 2 * SUB, 1)
    first_lane = lanes - rank
    crossed = pltpu.roll(crossed, first_lane, 1)
    selves = pltpu.roll(pltpu.roll(selves, first_lane - rank, 1), count, 0)
    tail = jnp.where(row < count, crossed, jnp.where(lane < first_lane + count, selves, 0.0))
    packed = jnp.where(lane < first_lane, packed, tail)
    if len(sums.shape) == 2:
        sums[...] = packed
    else:
        for n in range(sums.shape[0]):
            sums[n] = packed
    for copy in copies:
        copy.wait()


def pack_shift(j, rank):
    half = rank // 2
    if SUB * j < half:
        return rank * j
    return half // SUB * rank + half * (j - half // SUB) - half


def residuals(proj, snaps, basis):
    thirds = [part.astype(jnp.bfloat16) for part in split3(proj)]
    resid = []
    for n in range(3):
        value = snaps[n]
        for third in thirds:
            value = value - jnp.dot(third, basis[n], preferred_element_type=jnp.float32)
        resid.append(value)
    return resid


def solve(small, resid, scale, factor, modes):
    count = factor.shape[0]
    r = lax.broadcasted_iota(jnp.int32, (SUB, SUB), 0)
    c = lax.broadcasted_iota(jnp.int32, (SUB, SUB), 1)
    small = jnp.where((r < count) & (c < count), small, jnp.where(r == c, 1.0, 0.0))
    below = lax.broadcasted_iota(jnp.int32, (SUB, 1), 0)
    pivots = jnp.ones((SUB, 1), jnp.float32)
    for j in range(count):
        pivot = small[j : j + 1, j : j + 1]
        pivots = jnp.where(below == j, pivot, pivots)
        share = jnp.where(below > j, small[:, j : j + 1] / pivot, 0.0)
        resid = [v - share * v[j : j + 1, :] for v in resid]
        small = small - share * small[j : j + 1, :]
    root = jnp.sqrt(pivots)
    upper = jnp.where(c >= r, small / root, 0.0)
    factor[...] = upper[0:count, 0:count] * (1.0 / scale)
    gain = scale / root
    groups = resid[0].shape[1] // LANES
    for n in range(3):
        value = resid[n] * gain
        for t in range(groups):
            modes[pl.ds(groups * n + t, count, stride=3 * groups), :] = value[0:count, LANES * t : LANES * (t + 1)]


def finish_kernel(scale, count, rank, *refs):
    parts, (snaps, basis, coef, factor, modes, flag, held, gram) = refs[:-8], refs[-8:]
    if len(parts) == 1 and len(parts[0].shape) == 3:
        packed = tree_sum([parts[0][n] for n in range(parts[0].shape[0])])
    else:
        packed = tree_sum([part[...] for part in parts])
    lanes = packed.shape[1]
    half = rank // 2
    lane = lax.broadcasted_iota(jnp.int32, (SUB, lanes), 1)
    row = lax.broadcasted_iota(jnp.int32, (SUB, lanes), 0)
    for j in range(rank // SUB):
        shift = pack_shift(j, rank)
        part = pltpu.roll(packed, lanes - shift, 1) if shift else packed
        if SUB * j >= half:
            part = jnp.where(lane < half, 0.0, part)
        gram[SUB * j : SUB * (j + 1), :] = part
    tail = pltpu.roll(packed, rank, 1)
    proj = jnp.where(row < count, tail, 0.0)[:, 0:rank]
    held[...] = proj
    coef[...] = proj[0:count, :]
    inner = pltpu.roll(tail, SUB - count, 0)[:, 0:SUB]
    dot = functools.partial(lax.dot_general, precision=HIGHEST, preferred_element_type=jnp.float32)
    turned = dot(proj, gram[:, 0:rank], (((1,), (0,)), ((), ())))
    crossed = dot(proj, proj, NT)
    bent = dot(turned, proj, NT) + dot(proj, turned, NT)
    small = inner - 2.0 * crossed + bent
    r = lax.broadcasted_iota(jnp.int32, (SUB, SUB), 0)
    c = lax.broadcasted_iota(jnp.int32, (SUB, SUB), 1)
    loss = jnp.where((r == c) & (r < count), inner + 2.0 * crossed + bent - 8.0 * small, -1.0)
    lost = jnp.max(jnp.max(jnp.where(loss < 0.0, 0.0, 1.0), axis=1, keepdims=True), axis=0, keepdims=True)
    flag[...] = lost.astype(jnp.int32)
    solve(small, residuals(proj, snaps, basis), scale, factor, modes)


def inner_kernel(proj, snaps, basis, gram):
    total = None
    for resid in residuals(proj[...], snaps, basis):
        term = lax.dot_general(resid, resid, NT, precision=HIGHEST, preferred_element_type=jnp.float32)
        total = term if total is None else total + term
    gram[...] = total


def solve_kernel(scale, gram, proj, snaps, basis, factor, modes):
    solve(gram[...], residuals(proj[...], snaps, basis), scale, factor, modes)


def tree_sum(parts):
    parts = list(parts)
    while len(parts) > 1:
        parts = [a + b for a, b in zip(parts[::2], parts[1::2])] + ([parts[-1]] if len(parts) % 2 else [])
    return parts[0]


def moved(block, axis, target):
    return lax.ppermute(block, axis, [(i, target(i)) for i in range(lax.axis_size(axis))])


def partners(block, axis, stride, count):
    digit = lambda i: i // stride % count
    if count & (count - 1) == 0:
        return [block] + [
            moved(block, axis, lambda i, j=j: i + ((digit(i) ^ j) - digit(i)) * stride) for j in range(1, count)
        ]
    got = [block] + [
        moved(block, axis, lambda i, j=j: i + ((digit(i) + j) % count - digit(i)) * stride) for j in range(1, count)
    ]
    mine = lax.axis_index(axis) // stride % count
    return list(jnp.roll(jnp.stack(got)[::-1], mine + 1, axis=0))


def digits(size):
    found, rest = [], size
    for base in (8, 4, 2):
        while rest % base == 0:
            found.append(base)
            rest //= base
    base = 3
    while rest > 1:
        while rest % base == 0:
            found.append(base)
            rest //= base
        base += 2
    return found


def summed(sums, n_dev, n_group):
    rounds = []
    for axis, size in (("dev", n_dev), ("group", n_group)):
        stride = 1
        for base in digits(size):
            rounds.append((axis, stride, base))
            stride *= base
    parts = [sums]
    for axis, stride, base in rounds:
        parts = partners(tree_sum(parts), axis, stride, base)
    return parts


def ring_blocks(own, n_dev):
    ahead = moved(own, "dev", lambda i: (i - 2) % n_dev)
    behind = moved(own, "dev", lambda i: (i + 2) % n_dev)
    other = moved(own, "dev", lambda i: i ^ 1)
    far = moved(own, "dev", lambda i: (i + 3 if i % 2 else i - 3) % n_dev)
    other_ahead = moved(ahead, "dev", lambda i: i ^ 1)
    other_behind = moved(behind, "dev", lambda i: i ^ 1)
    return [own, ahead, behind, other, far, other_ahead, other_behind]


def per_device(density, velocity, basis, snap_steps):
    planes, rows, lanes = density.shape
    count = snap_steps.shape[0]
    rank = basis.shape[0]
    reach = STEPS
    n_dev, n_group = lax.axis_size("dev"), lax.axis_size("group")
    vmem = pl.BlockSpec(memory_space=pltpu.VMEM)
    f32 = jnp.float32
    params = pltpu.CompilerParams(vmem_limit_bytes=VMEM_LIMIT)

    held = jnp.concatenate([density[None], velocity])
    edge = jax.ShapeDtypeStruct((4, planes, SUB, lanes), f32)
    top, bottom = pl.pallas_call(
        edges_kernel, out_shape=(edge, edge), in_specs=[vmem], out_specs=(vmem, vmem), compiler_params=params
    )(held)
    upper = moved(top, "group", lambda i: (i + 1) % n_group)
    lower = moved(bottom, "group", lambda i: (i - 1) % n_group)
    high = rows + 2 * HALO
    tiles = pl.cdiv(high, SUB)
    own = pl.pallas_call(
        widen_kernel,
        out_shape=jax.ShapeDtypeStruct((4 * planes * high + SUB, lanes), f32),
        in_specs=[vmem] * 3,
        out_specs=vmem,
        compiler_params=params,
    )(held, upper, lower)
    blocks = ring_blocks(own, n_dev)
    modes = jnp.transpose(basis[:, :, 0, :], (1, 0, 2))
    span = planes + 2 * reach
    width = basis.shape[3]
    members = n_dev * n_group
    at_once = members <= 32
    pops, snaps, sums = pl.pallas_call(
        lattice_kernel,
        out_shape=(
            jax.ShapeDtypeStruct((DIRS, planes, rows, lanes), f32),
            jax.ShapeDtypeStruct((3, SUB, width), f32),
            jax.ShapeDtypeStruct((members, SUB, lanes) if at_once else (SUB, lanes), f32),
        ),
        in_specs=[vmem] * len(blocks) + [pl.BlockSpec(memory_space=pl.ANY), vmem],
        out_specs=(pl.BlockSpec(memory_space=pltpu.HBM), vmem, vmem),
        scratch_shapes=[
            pltpu.VMEM((DIRS, span, tiles, SUB, lanes), f32),
            pltpu.VMEM((DIRS, span, tiles, SUB, lanes), f32),
            pltpu.VMEM((span, 3, 2, SUB, lanes), f32),
            pltpu.VMEM((STEPS, 3, 2, SUB, lanes), f32),
            pltpu.VMEM((3 * SUB * SUB, lanes), f32),
            pltpu.VMEM((rank + 4 * SUB, width), jnp.bfloat16),
            pltpu.VMEM((rank + 4 * SUB, lanes), f32),
            pltpu.VMEM((planes, DIRS, SUB * tiles + SUB, lanes), f32),
            pltpu.SMEM((count,), jnp.int32),
            pltpu.SemaphoreType.DMA((planes + 1,)),
        ],
        compiler_params=params,
    )(*blocks, snap_steps, modes)

    if at_once:
        parts = [lax.all_to_all(sums, ("group", "dev"), 0, 0)]
    else:
        parts = summed(sums, n_dev, n_group)
    scale = math.sqrt(3 * width * members)
    solved = (
        jax.ShapeDtypeStruct((count, count), f32),
        jax.ShapeDtypeStruct((count * 3 * width // lanes, lanes), f32),
    )
    coef, factor, new_modes, flag, proj = pl.pallas_call(
        functools.partial(finish_kernel, scale, count, rank),
        out_shape=(
            jax.ShapeDtypeStruct((count, rank), f32),
            *solved,
            jax.ShapeDtypeStruct((1, 1), jnp.int32),
            jax.ShapeDtypeStruct((SUB, rank), f32),
        ),
        in_specs=[vmem] * (len(parts) + 2),
        out_specs=(vmem,) * 5,
        scratch_shapes=[pltpu.VMEM((rank, lanes), f32)],
        compiler_params=params,
    )(*parts, snaps, modes)
    coefficients = coef.T

    def from_residuals(state):
        gram = pl.pallas_call(
            inner_kernel, out_shape=jax.ShapeDtypeStruct((SUB, SUB), f32), in_specs=[vmem] * 3, out_specs=vmem
        )(proj, snaps, modes)
        gram = lax.psum(gram, ("group", "dev"))
        return (
            jnp.int32(0),
            *pl.pallas_call(
                functools.partial(solve_kernel, scale), out_shape=solved, in_specs=[vmem] * 4, out_specs=(vmem, vmem)
            )(gram, proj, snaps, modes),
        )

    _, factor, new_modes = lax.while_loop(lambda state: state[0] != 0, from_residuals, (flag[0, 0], factor, new_modes))
    return (pops, coefficients, factor, new_modes.reshape(count, 3, 1, width))


def solution(mesh):
    placed = (
        P("dev", "group", None),
        P(None, "dev", "group", None),
        P(None, None, "dev", "group"),
        P(),
    )
    return jax.shard_map(
        per_device,
        mesh=mesh,
        in_specs=placed,
        out_specs=(P(None, "dev", "group", None), P(), P(), P(None, None, "dev", "group")),
        check_vma=False,
    )
```

```python
import functools
import math

import jax
import jax.numpy as jnp
from jax import lax
from jax.experimental import pallas as pl
from jax.experimental.pallas import tpu as pltpu
from jax.sharding import PartitionSpec as P

STEPS = 6
DIRS = 19
DIR_X = [0, 1, -1, 0, 0, 0, 0, 1, -1, 1, -1, 1, -1, 1, -1, 0, 0, 0, 0]
DIR_Y = [0, 0, 0, 1, -1, 0, 0, 1, 1, -1, -1, 0, 0, 0, 0, 1, -1, 1, -1]
DIR_Z = [0, 0, 0, 0, 0, 1, -1, 0, 0, 0, 0, 1, 1, -1, -1, 1, 1, -1, -1]
OPPOSITE = [(1, 2), (3, 4), (5, 6), (7, 10), (8, 9), (11, 14), (12, 13), (15, 18), (16, 17)]
OMEGA = 1.6
KEEP = 1.0 - OMEGA
RATE = OMEGA / KEEP
UNIT = 10.0
SUB = 8
LANES = 128
HALO = 6
OFFSETS = [(0, 0), (2, 2), (-2, -2), (1, -1), (-3, 3), (3, 1), (-1, -3)]
HIGHEST = lax.Precision.HIGHEST
NT = (((1,), (1,)), ((), ()))
VMEM_LIMIT = 48 * 1024 * 1024


def along(direction, parts):
    total = None
    for sign, part in sorted(zip(direction, parts), key=lambda pair: -pair[0]):
        if sign == 0:
            continue
        if total is None:
            total = part if sign > 0 else -part
        else:
            total = total + part if sign > 0 else total - part
    return total


def relaxed(rate, dens, flow, speed, pops):
    twice = [f + f for f in flow]
    squares = [f * s for f, s in zip(flow, speed)]
    base = (rate / 36.0) * dens - (squares[0] + squares[1] + squares[2]) * (1.0 / 3.0)
    based = [base + square for square in squares]
    out = [None] * DIRS

    def put(i, value):
        out[i] = value if pops is None else pops[i] + value

    put(0, 12.0 * base)
    crossed = {}
    for a, b in OPPOSITE:
        direction = (DIR_X[a], DIR_Y[a], DIR_Z[a])
        axes = [n for n in range(3) if direction[n]]
        if len(axes) == 1:
            even = based[axes[0]] + based[axes[0]]
            odd = twice[axes[0]]
        else:
            m, n = axes
            if (m, n) not in crossed:
                crossed[m, n] = based[m] + squares[n], twice[m] * speed[n]
            both, cross = crossed[m, n]
            even = both + cross if direction[m] * direction[n] > 0 else both - cross
            odd = along(direction, flow)
        put(a, even + odd)
        put(b, even - odd)
    return out


def moments(pops):
    dens = tree_sum([pops[0]] + [pops[a] + pops[b] for a, b in OPPOSITE])
    diff = {a: pops[a] - pops[b] for a, b in OPPOSITE}
    mom = []
    for table in (DIR_X, DIR_Y, DIR_Z):
        total = None
        for a, _ in OPPOSITE:
            if table[a] == 0:
                continue
            if total is None:
                total = diff[a] if table[a] > 0 else -diff[a]
            else:
                total = total + diff[a] if table[a] > 0 else total - diff[a]
        mom.append(total)
    return dens, mom


def straight(src, x, tiles, skip):
    def get(i, t):
        tile = src[i, x - DIR_X[i], pl.ds(skip + t - DIR_Y[i], SUB, stride=tiles), :]
        return pltpu.roll(tile, DIR_Z[i] % LANES, 1) if DIR_Z[i] else tile

    return get


def reciprocal(value):
    near = pl.reciprocal(value, approx=True)
    near = near * (2.0 - value * near)
    return near * (2.0 - value * near)


def streamed(src, x, tiles):
    def get(i, t):
        at = t - DIR_Y[i]
        tile = src[i, x - DIR_X[i], at % tiles]
        if at < 0 or at >= tiles:
            tile = pltpu.roll(tile, DIR_Y[i] % SUB, 0)
        if DIR_Z[i] != 0:
            tile = pltpu.roll(tile, DIR_Z[i] % LANES, 1)
        return tile

    return get


def edges_kernel(held, top, bottom):
    rows, edge = held.shape[2], top.shape[2]
    top[...] = held[:, :, rows - edge :, :]
    bottom[...] = held[:, :, :edge, :]


def widen_kernel(held, upper, lower, wide):
    fields, planes, rows, _ = held.shape
    high = rows + 2 * HALO
    for f in range(fields):
        for p in range(planes):
            at = (f * planes + p) * high
            wide[pl.ds(at, HALO), :] = upper[f, p, upper.shape[2] - HALO :, :]
            wide[pl.ds(at + HALO, rows), :] = held[f, p]
            wide[pl.ds(at + HALO + rows, HALO), :] = lower[f, p, :HALO, :]
    wide[pl.ds(fields * planes * high, SUB), :] = jnp.zeros((SUB, LANES), jnp.float32)


def split3(value):
    a = value.astype(jnp.bfloat16).astype(jnp.float32)
    rest = value - a
    b = rest.astype(jnp.bfloat16).astype(jnp.float32)
    return a, b, rest - b


def lattice_kernel(*refs):
    blocks, refs = refs[:-16], refs[-16:]
    snap_steps, basis, pops, snaps, sums, ping, pong, ordered, speeds, views = refs[:10]
    coarse, rowwise, gram, whole, at_steps, sems = refs[10:]
    planes, rows, lanes = pops.shape[1:]
    tiles = ping.shape[2]
    reach = STEPS
    span = planes + 2 * reach
    high = rows + 2 * HALO
    count = snap_steps.shape[0]
    steps_copy = pltpu.make_async_copy(snap_steps, at_steps, sems.at[planes])
    steps_copy.start()
    odd = lax.rem(lax.axis_index("dev"), 2)
    place = [reach + planes * (even_at + odd * (odd_at - even_at)) for even_at, odd_at in OFFSETS]

    def put_speed(p, row, held):
        for t, speed in enumerate(held):
            for c in range(3):
                speeds[p, c, pl.ds(row + t, SUB, stride=len(held)), :] = speed[c]

    def keep_view(step):
        for c in range(3):
            for half in range(2):
                at = HALO + 2 * half
                views[step, c, half] = tree_sum(
                    [speeds[p, c, pl.ds(at + m, SUB, stride=4), :] for p in range(planes) for m in range(2)]
                )

    for n, block in enumerate(blocks):
        for p in range(planes):
            x = place[n] + p
            held = []
            for t in range(tiles):
                dens, *vel = [block[pl.ds((f * planes + p) * high + t, SUB, stride=tiles), :] for f in range(4)]
                part = dens * (3.0 / 36.0)
                speed = [1.5 * v for v in vel]
                out = relaxed(1.0, dens, [part * v for v in vel], speed, None)
                for i in range(DIRS):
                    ping[i, x, t] = out[i]
                held.append(speed)
            if n == 0:
                put_speed(p, 0, held)
    keep_view(0)

    few, skip = tiles - 1, (high - SUB * (tiles - 1)) // 2
    src, dst = ping, pong
    for step in range(1, STEPS):
        wide = step < 2
        for x in range(step, span - step):
            get = straight(ordered, x, few, skip) if step == 2 else streamed(src, x, tiles if wide else few)
            held = []
            for t in range(tiles if wide else few):
                pop = [get(i, t) for i in range(DIRS)]
                dens, mom = moments(pop)
                inverse = 1.5 * reciprocal(dens)
                speed = [m * inverse for m in mom]
                flow = [m * (RATE * 3.0 / 36.0) for m in mom]
                out = relaxed(RATE, dens, flow, speed, pop)
                for i in range(DIRS):
                    if wide:
                        ordered[i, x, pl.ds(t, SUB, stride=tiles), :] = out[i]
                    else:
                        dst[i, x, t] = out[i]
                held.append(speed)
            if reach <= x < reach + planes:
                put_speed(x - reach, 0 if wide else skip, held)
        keep_view(step)
        src, dst = dst, src

    copies = []
    for p in range(planes):
        get = streamed(src, reach + p, few)
        for i in range(DIRS):
            for t in range(few):
                at = pl.ds(SUB - HALO + skip + t, SUB, stride=few)
                whole[p, i, at, :] = KEEP ** (STEPS - 1) * get(i, t)
        copies.append(pltpu.make_async_copy(whole.at[p, :, pl.ds(SUB, rows), :], pops.at[:, p], sems.at[p]))
        copies[-1].start()

    steps_copy.wait()
    lane = lax.broadcasted_iota(jnp.int32, (lanes, lanes), 0) // 2
    col = lax.broadcasted_iota(jnp.int32, (lanes, lanes), 1)
    flat = None
    for half in range(2):
        stack = [views[at_steps[k], c, half] for k in range(count) for c in range(3)]
        gather = jnp.where(lane + half * (lanes // 2) == col, 1.0, 0.0).astype(jnp.bfloat16)
        for part in split3(jnp.concatenate(stack, axis=0)):
            term = jnp.dot(part.astype(jnp.bfloat16), gather, preferred_element_type=jnp.float32)
            flat = term if flat is None else flat + term
    height = 3 * SUB * count
    coarse[height:, :] = jnp.zeros_like(coarse[height:, :])
    coarse[0:height, :] = flat * (UNIT / (4 * planes) / 1.5)
    rank = basis.shape[1]
    groups = rows // tiles
    total = None
    for c in range(3):
        parts = [coarse[pl.ds(SUB * c + t, SUB, stride=3 * SUB), :] for t in range(groups)]
        snap = jnp.concatenate(parts, axis=1)
        snaps[c] = snap
        a, b, d = split3(snap)
        rowwise[0:rank, :] = basis[c]
        rowwise[rank : rank + 2 * SUB, :] = jnp.concatenate([a, b], axis=0).astype(jnp.bfloat16)
        rowwise[rank + 2 * SUB :, :] = jnp.concatenate([d, jnp.zeros_like(d)], axis=0).astype(jnp.bfloat16)
        term = lax.dot_general(rowwise[...], rowwise[...], NT, preferred_element_type=jnp.float32)
        total = term if total is None else total + term
    gram[...] = jnp.zeros_like(gram)
    gram[:, 0 : total.shape[1]] = total
    half = rank // 2
    lane = lax.broadcasted_iota(jnp.int32, (SUB, lanes), 1)
    row = lax.broadcasted_iota(jnp.int32, (SUB, lanes), 0)
    packed = None
    for j in range(rank // SUB):
        part = gram[SUB * j : SUB * (j + 1), :]
        if SUB * j < half:
            part = jnp.where(lane < half, 0.5 * part, jnp.where(lane < rank, part, 0.0))
        else:
            part = jnp.where((lane >= half) & (lane < rank), 0.5 * part, 0.0)
        shift = pack_shift(j, rank)
        packed = part if packed is None else packed + (pltpu.roll(part, shift, 1) if shift else part)
    crossed = gram[rank : rank + SUB, :] + gram[rank + SUB : rank + 2 * SUB, :]
    crossed = crossed + gram[rank + 2 * SUB : rank + 3 * SUB, :]
    selves = crossed + pltpu.roll(crossed, lanes - SUB, 1) + pltpu.roll(crossed, lanes - 2 * SUB, 1)
    first_lane = lanes - rank
    crossed = pltpu.roll(crossed, first_lane, 1)
    selves = pltpu.roll(pltpu.roll(selves, first_lane - rank, 1), count, 0)
    tail = jnp.where(row < count, crossed, jnp.where(lane < first_lane + count, selves, 0.0))
    packed = jnp.where(lane < first_lane, packed, tail)
    if len(sums.shape) == 2:
        sums[...] = packed
    else:
        for n in range(sums.shape[0]):
            sums[n] = packed
    for copy in copies:
        copy.wait()


def pack_shift(j, rank):
    half = rank // 2
    if SUB * j < half:
        return rank * j
    return half // SUB * rank + half * (j - half // SUB) - half


def residuals(proj, snaps, basis):
    thirds = [part.astype(jnp.bfloat16) for part in split3(proj)]
    resid = []
    for n in range(3):
        value = snaps[n]
        for third in thirds:
            value = value - jnp.dot(third, basis[n], preferred_element_type=jnp.float32)
        resid.append(value)
    return resid


def solve(small, resid, scale, factor, modes):
    count = factor.shape[0]
    r = lax.broadcasted_iota(jnp.int32, (SUB, SUB), 0)
    c = lax.broadcasted_iota(jnp.int32, (SUB, SUB), 1)
    small = jnp.where((r < count) & (c < count), small, jnp.where(r == c, 1.0, 0.0))
    below = lax.broadcasted_iota(jnp.int32, (SUB, 1), 0)
    pivots = jnp.ones((SUB, 1), jnp.float32)
    for j in range(count):
        pivot = small[j : j + 1, j : j + 1]
        pivots = jnp.where(below == j, pivot, pivots)
        share = jnp.where(below > j, small[:, j : j + 1] / pivot, 0.0)
        resid = [v - share * v[j : j + 1, :] for v in resid]
        small = small - share * small[j : j + 1, :]
    root = jnp.sqrt(pivots)
    upper = jnp.where(c >= r, small / root, 0.0)
    factor[...] = upper[0:count, 0:count] * (1.0 / scale)
    gain = scale / root
    groups = resid[0].shape[1] // LANES
    for n in range(3):
        value = resid[n] * gain
        for t in range(groups):
            modes[pl.ds(groups * n + t, count, stride=3 * groups), :] = value[0:count, LANES * t : LANES * (t + 1)]


def finish_kernel(scale, count, rank, *refs):
    parts, (snaps, basis, coef, factor, modes, flag, held, gram) = refs[:-8], refs[-8:]
    if len(parts) == 1 and len(parts[0].shape) == 3:
        packed = tree_sum([parts[0][n] for n in range(parts[0].shape[0])])
    else:
        packed = tree_sum([part[...] for part in parts])
    lanes = packed.shape[1]
    half = rank // 2
    lane = lax.broadcasted_iota(jnp.int32, (SUB, lanes), 1)
    row = lax.broadcasted_iota(jnp.int32, (SUB, lanes), 0)
    for j in range(rank // SUB):
        shift = pack_shift(j, rank)
        part = pltpu.roll(packed, lanes - shift, 1) if shift else packed
        if SUB * j >= half:
            part = jnp.where(lane < half, 0.0, part)
        gram[SUB * j : SUB * (j + 1), :] = part
    tail = pltpu.roll(packed, rank, 1)
    proj = jnp.where(row < count, tail, 0.0)[:, 0:rank]
    held[...] = proj
    coef[...] = proj[0:count, :]
    inner = pltpu.roll(tail, SUB - count, 0)[:, 0:SUB]
    dot = functools.partial(lax.dot_general, precision=HIGHEST, preferred_element_type=jnp.float32)
    turned = dot(proj, gram[:, 0:rank], (((1,), (0,)), ((), ())))
    crossed = dot(proj, proj, NT)
    bent = dot(turned, proj, NT) + dot(proj, turned, NT)
    small = inner - 2.0 * crossed + bent
    r = lax.broadcasted_iota(jnp.int32, (SUB, SUB), 0)
    c = lax.broadcasted_iota(jnp.int32, (SUB, SUB), 1)
    loss = jnp.where((r == c) & (r < count), inner + 2.0 * crossed + bent - 8.0 * small, -1.0)
    lost = jnp.max(jnp.max(jnp.where(loss < 0.0, 0.0, 1.0), axis=1, keepdims=True), axis=0, keepdims=True)
    flag[...] = lost.astype(jnp.int32)
    solve(small, residuals(proj, snaps, basis), scale, factor, modes)


def inner_kernel(proj, snaps, basis, gram):
    total = None
    for resid in residuals(proj[...], snaps, basis):
        term = lax.dot_general(resid, resid, NT, precision=HIGHEST, preferred_element_type=jnp.float32)
        total = term if total is None else total + term
    gram[...] = total


def solve_kernel(scale, gram, proj, snaps, basis, factor, modes):
    solve(gram[...], residuals(proj[...], snaps, basis), scale, factor, modes)


def tree_sum(parts):
    parts = list(parts)
    while len(parts) > 1:
        parts = [a + b for a, b in zip(parts[::2], parts[1::2])] + ([parts[-1]] if len(parts) % 2 else [])
    return parts[0]


def moved(block, axis, target):
    return lax.ppermute(block, axis, [(i, target(i)) for i in range(lax.axis_size(axis))])


def partners(block, axis, stride, count):
    digit = lambda i: i // stride % count
    if count & (count - 1) == 0:
        return [block] + [
            moved(block, axis, lambda i, j=j: i + ((digit(i) ^ j) - digit(i)) * stride) for j in range(1, count)
        ]
    got = [block] + [
        moved(block, axis, lambda i, j=j: i + ((digit(i) + j) % count - digit(i)) * stride) for j in range(1, count)
    ]
    mine = lax.axis_index(axis) // stride % count
    return list(jnp.roll(jnp.stack(got)[::-1], mine + 1, axis=0))


def digits(size):
    found, rest = [], size
    for base in (8, 4, 2):
        while rest % base == 0:
            found.append(base)
            rest //= base
    base = 3
    while rest > 1:
        while rest % base == 0:
            found.append(base)
            rest //= base
        base += 2
    return found


def summed(sums, n_dev, n_group):
    rounds = []
    for axis, size in (("dev", n_dev), ("group", n_group)):
        stride = 1
        for base in digits(size):
            rounds.append((axis, stride, base))
            stride *= base
    parts = [sums]
    for axis, stride, base in rounds:
        parts = partners(tree_sum(parts), axis, stride, base)
    return parts


def ring_blocks(own, n_dev):
    ahead = moved(own, "dev", lambda i: (i - 2) % n_dev)
    behind = moved(own, "dev", lambda i: (i + 2) % n_dev)
    other = moved(own, "dev", lambda i: i ^ 1)
    far = moved(own, "dev", lambda i: (i + 3 if i % 2 else i - 3) % n_dev)
    other_ahead = moved(ahead, "dev", lambda i: i ^ 1)
    other_behind = moved(behind, "dev", lambda i: i ^ 1)
    return [own, ahead, behind, other, far, other_ahead, other_behind]


def per_device(density, velocity, basis, snap_steps):
    planes, rows, lanes = density.shape
    count = snap_steps.shape[0]
    rank = basis.shape[0]
    reach = STEPS
    n_dev, n_group = lax.axis_size("dev"), lax.axis_size("group")
    vmem = pl.BlockSpec(memory_space=pltpu.VMEM)
    f32 = jnp.float32
    params = pltpu.CompilerParams(vmem_limit_bytes=VMEM_LIMIT)

    held = jnp.concatenate([density[None], velocity])
    edge = jax.ShapeDtypeStruct((4, planes, SUB, lanes), f32)
    top, bottom = pl.pallas_call(
        edges_kernel, out_shape=(edge, edge), in_specs=[vmem], out_specs=(vmem, vmem), compiler_params=params
    )(held)
    upper = moved(top, "group", lambda i: (i + 1) % n_group)
    lower = moved(bottom, "group", lambda i: (i - 1) % n_group)
    high = rows + 2 * HALO
    tiles = pl.cdiv(high, SUB)
    own = pl.pallas_call(
        widen_kernel,
        out_shape=jax.ShapeDtypeStruct((4 * planes * high + SUB, lanes), f32),
        in_specs=[vmem] * 3,
        out_specs=vmem,
        compiler_params=params,
    )(held, upper, lower)
    blocks = ring_blocks(own, n_dev)
    modes = jnp.transpose(basis[:, :, 0, :], (1, 0, 2))
    span = planes + 2 * reach
    width = basis.shape[3]
    members = n_dev * n_group
    at_once = members <= 32
    pops, snaps, sums = pl.pallas_call(
        lattice_kernel,
        out_shape=(
            jax.ShapeDtypeStruct((DIRS, planes, rows, lanes), f32),
            jax.ShapeDtypeStruct((3, SUB, width), f32),
            jax.ShapeDtypeStruct((members, SUB, lanes) if at_once else (SUB, lanes), f32),
        ),
        in_specs=[vmem] * len(blocks) + [pl.BlockSpec(memory_space=pl.ANY), vmem],
        out_specs=(pl.BlockSpec(memory_space=pltpu.HBM), vmem, vmem),
        scratch_shapes=[
            pltpu.VMEM((DIRS, span, tiles, SUB, lanes), f32),
            pltpu.VMEM((DIRS, span, tiles, SUB, lanes), f32),
            pltpu.VMEM((DIRS, span, SUB * tiles, lanes), f32),
            pltpu.VMEM((planes, 3, SUB * (tiles + 1), lanes), f32),
            pltpu.VMEM((STEPS, 3, 2, SUB, lanes), f32),
            pltpu.VMEM((3 * SUB * SUB, lanes), f32),
            pltpu.VMEM((rank + 4 * SUB, width), jnp.bfloat16),
            pltpu.VMEM((rank + 4 * SUB, lanes), f32),
            pltpu.VMEM((planes, DIRS, SUB * tiles + SUB, lanes), f32),
            pltpu.SMEM((count,), jnp.int32),
            pltpu.SemaphoreType.DMA((planes + 1,)),
        ],
        compiler_params=params,
    )(*blocks, snap_steps, modes)

    if at_once:
        parts = [lax.all_to_all(sums, ("group", "dev"), 0, 0)]
    else:
        parts = summed(sums, n_dev, n_group)
    scale = math.sqrt(3 * width * members)
    solved = (
        jax.ShapeDtypeStruct((count, count), f32),
        jax.ShapeDtypeStruct((count * 3 * width // lanes, lanes), f32),
    )
    coef, factor, new_modes, flag, proj = pl.pallas_call(
        functools.partial(finish_kernel, scale, count, rank),
        out_shape=(
            jax.ShapeDtypeStruct((count, rank), f32),
            *solved,
            jax.ShapeDtypeStruct((1, 1), jnp.int32),
            jax.ShapeDtypeStruct((SUB, rank), f32),
        ),
        in_specs=[vmem] * (len(parts) + 2),
        out_specs=(vmem,) * 5,
        scratch_shapes=[pltpu.VMEM((rank, lanes), f32)],
        compiler_params=params,
    )(*parts, snaps, modes)
    coefficients = coef.T

    def from_residuals(state):
        gram = pl.pallas_call(
            inner_kernel, out_shape=jax.ShapeDtypeStruct((SUB, SUB), f32), in_specs=[vmem] * 3, out_specs=vmem
        )(proj, snaps, modes)
        gram = lax.psum(gram, ("group", "dev"))
        return (
            jnp.int32(0),
            *pl.pallas_call(
                functools.partial(solve_kernel, scale), out_shape=solved, in_specs=[vmem] * 4, out_specs=(vmem, vmem)
            )(gram, proj, snaps, modes),
        )

    _, factor, new_modes = lax.while_loop(lambda state: state[0] != 0, from_residuals, (flag[0, 0], factor, new_modes))
    return (pops, coefficients, factor, new_modes.reshape(count, 3, 1, width))


def solution(mesh):
    placed = (
        P("dev", "group", None),
        P(None, "dev", "group", None),
        P(None, None, "dev", "group"),
        P(),
    )
    return jax.shard_map(
        per_device,
        mesh=mesh,
        in_specs=placed,
        out_specs=(P(None, "dev", "group", None), P(), P(), P(None, None, "dev", "group")),
        check_vma=False,
    )
```

```python
import functools
import math

import jax
import jax.numpy as jnp
from jax import lax
from jax.experimental import pallas as pl
from jax.experimental.pallas import tpu as pltpu
from jax.sharding import PartitionSpec as P

STEPS = 6
DIRS = 19
DIR_X = [0, 1, -1, 0, 0, 0, 0, 1, -1, 1, -1, 1, -1, 1, -1, 0, 0, 0, 0]
DIR_Y = [0, 0, 0, 1, -1, 0, 0, 1, 1, -1, -1, 0, 0, 0, 0, 1, -1, 1, -1]
DIR_Z = [0, 0, 0, 0, 0, 1, -1, 0, 0, 0, 0, 1, 1, -1, -1, 1, 1, -1, -1]
OPPOSITE = [(1, 2), (3, 4), (5, 6), (7, 10), (8, 9), (11, 14), (12, 13), (15, 18), (16, 17)]
OMEGA = 1.6
KEEP = 1.0 - OMEGA
RATE = OMEGA / KEEP
UNIT = 10.0
SUB = 8
LANES = 128
HALO = 6
OFFSETS = [(0, 0), (2, 2), (-2, -2), (1, -1), (-3, 3), (3, 1), (-1, -3)]
HIGHEST = lax.Precision.HIGHEST
NT = (((1,), (1,)), ((), ()))
VMEM_LIMIT = 48 * 1024 * 1024


def along(direction, parts):
    total = None
    for sign, part in sorted(zip(direction, parts), key=lambda pair: -pair[0]):
        if sign == 0:
            continue
        if total is None:
            total = part if sign > 0 else -part
        else:
            total = total + part if sign > 0 else total - part
    return total


def relaxed(rate, dens, flow, speed, pops):
    twice = [f + f for f in flow]
    squares = [f * s for f, s in zip(flow, speed)]
    base = (rate / 36.0) * dens - (squares[0] + squares[1] + squares[2]) * (1.0 / 3.0)
    based = [base + square for square in squares]
    out = [None] * DIRS

    def put(i, value):
        out[i] = value if pops is None else pops[i] + value

    put(0, 12.0 * base)
    crossed = {}
    for a, b in OPPOSITE:
        direction = (DIR_X[a], DIR_Y[a], DIR_Z[a])
        axes = [n for n in range(3) if direction[n]]
        if len(axes) == 1:
            even = based[axes[0]] + based[axes[0]]
            odd = twice[axes[0]]
        else:
            m, n = axes
            if (m, n) not in crossed:
                crossed[m, n] = based[m] + squares[n], twice[m] * speed[n]
            both, cross = crossed[m, n]
            even = both + cross if direction[m] * direction[n] > 0 else both - cross
            odd = along(direction, flow)
        put(a, even + odd)
        put(b, even - odd)
    return out


def moments(pops):
    dens = tree_sum([pops[0]] + [pops[a] + pops[b] for a, b in OPPOSITE])
    diff = {a: pops[a] - pops[b] for a, b in OPPOSITE}
    mom = []
    for table in (DIR_X, DIR_Y, DIR_Z):
        total = None
        for a, _ in OPPOSITE:
            if table[a] == 0:
                continue
            if total is None:
                total = diff[a] if table[a] > 0 else -diff[a]
            else:
                total = total + diff[a] if table[a] > 0 else total - diff[a]
        mom.append(total)
    return dens, mom


def straight(src, x, tiles, skip):
    def get(i, t):
        tile = src[i, x - DIR_X[i], pl.ds(skip + t - DIR_Y[i], SUB, stride=tiles), :]
        return pltpu.roll(tile, DIR_Z[i] % LANES, 1) if DIR_Z[i] else tile

    return get


def reciprocal(value):
    near = pl.reciprocal(value, approx=True)
    near = near * (2.0 - value * near)
    return near * (2.0 - value * near)


def streamed(src, x, tiles):
    def get(i, t):
        at = t - DIR_Y[i]
        tile = src[i, x - DIR_X[i], at % tiles]
        if at < 0 or at >= tiles:
            tile = pltpu.roll(tile, DIR_Y[i] % SUB, 0)
        if DIR_Z[i] != 0:
            tile = pltpu.roll(tile, DIR_Z[i] % LANES, 1)
        return tile

    return get


def edges_kernel(held, top, bottom):
    rows, edge = held.shape[2], top.shape[2]
    top[...] = held[:, :, rows - edge :, :]
    bottom[...] = held[:, :, :edge, :]


def widen_kernel(held, upper, lower, wide):
    fields, planes, rows, _ = held.shape
    high = rows + 2 * HALO
    for f in range(fields):
        for p in range(planes):
            at = (f * planes + p) * high
            wide[pl.ds(at, HALO), :] = upper[f, p, upper.shape[2] - HALO :, :]
            wide[pl.ds(at + HALO, rows), :] = held[f, p]
            wide[pl.ds(at + HALO + rows, HALO), :] = lower[f, p, :HALO, :]
    wide[pl.ds(fields * planes * high, SUB), :] = jnp.zeros((SUB, LANES), jnp.float32)


def split3(value):
    a = value.astype(jnp.bfloat16).astype(jnp.float32)
    rest = value - a
    b = rest.astype(jnp.bfloat16).astype(jnp.float32)
    return a, b, rest - b


def lattice_kernel(*refs):
    blocks, refs = refs[:-16], refs[-16:]
    snap_steps, basis, pops, snaps, sums, ping, pong, ordered, speeds, views = refs[:10]
    coarse, rowwise, gram, whole, at_steps, sems = refs[10:]
    planes, rows, lanes = pops.shape[1:]
    tiles = ping.shape[2]
    reach = STEPS
    span = planes + 2 * reach
    high = rows + 2 * HALO
    count = snap_steps.shape[0]
    steps_copy = pltpu.make_async_copy(snap_steps, at_steps, sems.at[planes])
    steps_copy.start()
    odd = lax.rem(lax.axis_index("dev"), 2)
    place = [reach + planes * (even_at + odd * (odd_at - even_at)) for even_at, odd_at in OFFSETS]

    def put_speed(p, row, held):
        for t, speed in enumerate(held):
            for c in range(3):
                speeds[p, c, pl.ds(row + t, SUB, stride=len(held)), :] = speed[c]

    def keep_view(step):
        for c in range(3):
            for half in range(2):
                at = HALO + 2 * half
                views[step, c, half] = tree_sum(
                    [speeds[p, c, pl.ds(at + m, SUB, stride=4), :] for p in range(planes) for m in range(2)]
                )

    for n, block in enumerate(blocks):
        for p in range(planes):
            x = place[n] + p
            held = []
            for t in range(tiles):
                dens, *vel = [block[pl.ds((f * planes + p) * high + t, SUB, stride=tiles), :] for f in range(4)]
                part = dens * (3.0 / 36.0)
                speed = [1.5 * v for v in vel]
                out = relaxed(1.0, dens, [part * v for v in vel], speed, None)
                for i in range(DIRS):
                    ping[i, x, t] = out[i]
                held.append(speed)
            if n == 0:
                put_speed(p, 0, held)
    keep_view(0)

    few, skip = tiles - 1, (high - SUB * (tiles - 1)) // 2
    src, dst = ping, pong
    for step in range(1, STEPS):
        wide = step < 2
        for x in range(step, span - step):
            get = straight(ordered, x, few, skip) if step == 2 else streamed(src, x, tiles if wide else few)
            held = []
            for t in range(tiles if wide else few):
                pop = [get(i, t) for i in range(DIRS)]
                dens, mom = moments(pop)
                inverse = 1.5 * reciprocal(dens)
                speed = [m * inverse for m in mom]
                flow = [m * (RATE * 3.0 / 36.0) for m in mom]
                out = relaxed(RATE, dens, flow, speed, pop)
                inwards = {step: 1, span - 1 - step: -1}.get(x)
                for i in range(DIRS):
                    if inwards is not None and DIR_X[i] != inwards:
                        continue
                    if wide:
                        ordered[i, x, pl.ds(t, SUB, stride=tiles), :] = out[i]
                    else:
                        dst[i, x, t] = out[i]
                held.append(speed)
            if reach <= x < reach + planes:
                put_speed(x - reach, 0 if wide else skip, held)
        keep_view(step)
        src, dst = dst, src

    copies = []
    for p in range(planes):
        get = streamed(src, reach + p, few)
        for i in range(DIRS):
            for t in range(few):
                at = pl.ds(SUB - HALO + skip + t, SUB, stride=few)
                whole[p, i, at, :] = KEEP ** (STEPS - 1) * get(i, t)
        copies.append(pltpu.make_async_copy(whole.at[p, :, pl.ds(SUB, rows), :], pops.at[:, p], sems.at[p]))
        copies[-1].start()

    steps_copy.wait()
    lane = lax.broadcasted_iota(jnp.int32, (lanes, lanes), 0) // 2
    col = lax.broadcasted_iota(jnp.int32, (lanes, lanes), 1)
    flat = None
    for half in range(2):
        stack = [views[at_steps[k], c, half] for k in range(count) for c in range(3)]
        gather = jnp.where(lane + half * (lanes // 2) == col, 1.0, 0.0).astype(jnp.bfloat16)
        for part in split3(jnp.concatenate(stack, axis=0)):
            term = jnp.dot(part.astype(jnp.bfloat16), gather, preferred_element_type=jnp.float32)
            flat = term if flat is None else flat + term
    height = 3 * SUB * count
    coarse[height:, :] = jnp.zeros_like(coarse[height:, :])
    coarse[0:height, :] = flat * (UNIT / (4 * planes) / 1.5)
    rank = basis.shape[1]
    groups = rows // tiles
    total = None
    for c in range(3):
        parts = [coarse[pl.ds(SUB * c + t, SUB, stride=3 * SUB), :] for t in range(groups)]
        snap = jnp.concatenate(parts, axis=1)
        snaps[c] = snap
        a, b, d = split3(snap)
        rowwise[0:rank, :] = basis[c]
        rowwise[rank : rank + 2 * SUB, :] = jnp.concatenate([a, b], axis=0).astype(jnp.bfloat16)
        rowwise[rank + 2 * SUB :, :] = jnp.concatenate([d, jnp.zeros_like(d)], axis=0).astype(jnp.bfloat16)
        term = lax.dot_general(rowwise[...], rowwise[...], NT, preferred_element_type=jnp.float32)
        total = term if total is None else total + term
    gram[...] = jnp.zeros_like(gram)
    gram[:, 0 : total.shape[1]] = total
    half = rank // 2
    lane = lax.broadcasted_iota(jnp.int32, (SUB, lanes), 1)
    row = lax.broadcasted_iota(jnp.int32, (SUB, lanes), 0)
    packed = None
    for j in range(rank // SUB):
        part = gram[SUB * j : SUB * (j + 1), :]
        if SUB * j < half:
            part = jnp.where(lane < half, 0.5 * part, jnp.where(lane < rank, part, 0.0))
        else:
            part = jnp.where((lane >= half) & (lane < rank), 0.5 * part, 0.0)
        shift = pack_shift(j, rank)
        packed = part if packed is None else packed + (pltpu.roll(part, shift, 1) if shift else part)
    crossed = gram[rank : rank + SUB, :] + gram[rank + SUB : rank + 2 * SUB, :]
    crossed = crossed + gram[rank + 2 * SUB : rank + 3 * SUB, :]
    selves = crossed + pltpu.roll(crossed, lanes - SUB, 1) + pltpu.roll(crossed, lanes - 2 * SUB, 1)
    first_lane = lanes - rank
    crossed = pltpu.roll(crossed, first_lane, 1)
    selves = pltpu.roll(pltpu.roll(selves, first_lane - rank, 1), count, 0)
    tail = jnp.where(row < count, crossed, jnp.where(lane < first_lane + count, selves, 0.0))
    packed = jnp.where(lane < first_lane, packed, tail)
    if len(sums.shape) == 2:
        sums[...] = packed
    else:
        for n in range(sums.shape[0]):
            sums[n] = packed
    for copy in copies:
        copy.wait()


def pack_shift(j, rank):
    half = rank // 2
    if SUB * j < half:
        return rank * j
    return half // SUB * rank + half * (j - half // SUB) - half


def residuals(proj, snaps, basis):
    thirds = [part.astype(jnp.bfloat16) for part in split3(proj)]
    resid = []
    for n in range(3):
        value = snaps[n]
        for third in thirds:
            value = value - jnp.dot(third, basis[n], preferred_element_type=jnp.float32)
        resid.append(value)
    return resid


def solve(small, resid, scale, factor, modes):
    count = factor.shape[0]
    r = lax.broadcasted_iota(jnp.int32, (SUB, SUB), 0)
    c = lax.broadcasted_iota(jnp.int32, (SUB, SUB), 1)
    small = jnp.where((r < count) & (c < count), small, jnp.where(r == c, 1.0, 0.0))
    below = lax.broadcasted_iota(jnp.int32, (SUB, 1), 0)
    pivots = jnp.ones((SUB, 1), jnp.float32)
    for j in range(count):
        pivot = small[j : j + 1, j : j + 1]
        pivots = jnp.where(below == j, pivot, pivots)
        share = jnp.where(below > j, small[:, j : j + 1] / pivot, 0.0)
        resid = [v - share * v[j : j + 1, :] for v in resid]
        small = small - share * small[j : j + 1, :]
    root = jnp.sqrt(pivots)
    upper = jnp.where(c >= r, small / root, 0.0)
    factor[...] = upper[0:count, 0:count] * (1.0 / scale)
    gain = scale / root
    groups = resid[0].shape[1] // LANES
    for n in range(3):
        value = resid[n] * gain
        for t in range(groups):
            modes[pl.ds(groups * n + t, count, stride=3 * groups), :] = value[0:count, LANES * t : LANES * (t + 1)]


def finish_kernel(scale, count, rank, *refs):
    parts, (snaps, basis, coef, factor, modes, flag, held, gram) = refs[:-8], refs[-8:]
    if len(parts) == 1 and len(parts[0].shape) == 3:
        packed = tree_sum([parts[0][n] for n in range(parts[0].shape[0])])
    else:
        packed = tree_sum([part[...] for part in parts])
    lanes = packed.shape[1]
    half = rank // 2
    lane = lax.broadcasted_iota(jnp.int32, (SUB, lanes), 1)
    row = lax.broadcasted_iota(jnp.int32, (SUB, lanes), 0)
    for j in range(rank // SUB):
        shift = pack_shift(j, rank)
        part = pltpu.roll(packed, lanes - shift, 1) if shift else packed
        if SUB * j >= half:
            part = jnp.where(lane < half, 0.0, part)
        gram[SUB * j : SUB * (j + 1), :] = part
    tail = pltpu.roll(packed, rank, 1)
    proj = jnp.where(row < count, tail, 0.0)[:, 0:rank]
    held[...] = proj
    coef[...] = proj[0:count, :]
    inner = pltpu.roll(tail, SUB - count, 0)[:, 0:SUB]
    dot = functools.partial(lax.dot_general, precision=HIGHEST, preferred_element_type=jnp.float32)
    turned = dot(proj, gram[:, 0:rank], (((1,), (0,)), ((), ())))
    crossed = dot(proj, proj, NT)
    bent = dot(turned, proj, NT) + dot(proj, turned, NT)
    small = inner - 2.0 * crossed + bent
    r = lax.broadcasted_iota(jnp.int32, (SUB, SUB), 0)
    c = lax.broadcasted_iota(jnp.int32, (SUB, SUB), 1)
    loss = jnp.where((r == c) & (r < count), inner + 2.0 * crossed + bent - 8.0 * small, -1.0)
    lost = jnp.max(jnp.max(jnp.where(loss < 0.0, 0.0, 1.0), axis=1, keepdims=True), axis=0, keepdims=True)
    flag[...] = lost.astype(jnp.int32)
    solve(small, residuals(proj, snaps, basis), scale, factor, modes)


def inner_kernel(proj, snaps, basis, gram):
    total = None
    for resid in residuals(proj[...], snaps, basis):
        term = lax.dot_general(resid, resid, NT, precision=HIGHEST, preferred_element_type=jnp.float32)
        total = term if total is None else total + term
    gram[...] = total


def solve_kernel(scale, gram, proj, snaps, basis, factor, modes):
    solve(gram[...], residuals(proj[...], snaps, basis), scale, factor, modes)


def tree_sum(parts):
    parts = list(parts)
    while len(parts) > 1:
        parts = [a + b for a, b in zip(parts[::2], parts[1::2])] + ([parts[-1]] if len(parts) % 2 else [])
    return parts[0]


def moved(block, axis, target):
    return lax.ppermute(block, axis, [(i, target(i)) for i in range(lax.axis_size(axis))])


def partners(block, axis, stride, count):
    digit = lambda i: i // stride % count
    if count & (count - 1) == 0:
        return [block] + [
            moved(block, axis, lambda i, j=j: i + ((digit(i) ^ j) - digit(i)) * stride) for j in range(1, count)
        ]
    got = [block] + [
        moved(block, axis, lambda i, j=j: i + ((digit(i) + j) % count - digit(i)) * stride) for j in range(1, count)
    ]
    mine = lax.axis_index(axis) // stride % count
    return list(jnp.roll(jnp.stack(got)[::-1], mine + 1, axis=0))


def digits(size):
    found, rest = [], size
    for base in (8, 4, 2):
        while rest % base == 0:
            found.append(base)
            rest //= base
    base = 3
    while rest > 1:
        while rest % base == 0:
            found.append(base)
            rest //= base
        base += 2
    return found


def summed(sums, n_dev, n_group):
    rounds = []
    for axis, size in (("dev", n_dev), ("group", n_group)):
        stride = 1
        for base in digits(size):
            rounds.append((axis, stride, base))
            stride *= base
    parts = [sums]
    for axis, stride, base in rounds:
        parts = partners(tree_sum(parts), axis, stride, base)
    return parts


def ring_blocks(own, n_dev):
    ahead = moved(own, "dev", lambda i: (i - 2) % n_dev)
    behind = moved(own, "dev", lambda i: (i + 2) % n_dev)
    other = moved(own, "dev", lambda i: i ^ 1)
    far = moved(own, "dev", lambda i: (i + 3 if i % 2 else i - 3) % n_dev)
    other_ahead = moved(ahead, "dev", lambda i: i ^ 1)
    other_behind = moved(behind, "dev", lambda i: i ^ 1)
    return [own, ahead, behind, other, far, other_ahead, other_behind]


def per_device(density, velocity, basis, snap_steps):
    planes, rows, lanes = density.shape
    count = snap_steps.shape[0]
    rank = basis.shape[0]
    reach = STEPS
    n_dev, n_group = lax.axis_size("dev"), lax.axis_size("group")
    vmem = pl.BlockSpec(memory_space=pltpu.VMEM)
    f32 = jnp.float32
    params = pltpu.CompilerParams(vmem_limit_bytes=VMEM_LIMIT)

    held = jnp.concatenate([density[None], velocity])
    edge = jax.ShapeDtypeStruct((4, planes, SUB, lanes), f32)
    top, bottom = pl.pallas_call(
        edges_kernel, out_shape=(edge, edge), in_specs=[vmem], out_specs=(vmem, vmem), compiler_params=params
    )(held)
    upper = moved(top, "group", lambda i: (i + 1) % n_group)
    lower = moved(bottom, "group", lambda i: (i - 1) % n_group)
    high = rows + 2 * HALO
    tiles = pl.cdiv(high, SUB)
    own = pl.pallas_call(
        widen_kernel,
        out_shape=jax.ShapeDtypeStruct((4 * planes * high + SUB, lanes), f32),
        in_specs=[vmem] * 3,
        out_specs=vmem,
        compiler_params=params,
    )(held, upper, lower)
    blocks = ring_blocks(own, n_dev)
    modes = jnp.transpose(basis[:, :, 0, :], (1, 0, 2))
    span = planes + 2 * reach
    width = basis.shape[3]
    members = n_dev * n_group
    at_once = members <= 32
    pops, snaps, sums = pl.pallas_call(
        lattice_kernel,
        out_shape=(
            jax.ShapeDtypeStruct((DIRS, planes, rows, lanes), f32),
            jax.ShapeDtypeStruct((3, SUB, width), f32),
            jax.ShapeDtypeStruct((members, SUB, lanes) if at_once else (SUB, lanes), f32),
        ),
        in_specs=[vmem] * len(blocks) + [pl.BlockSpec(memory_space=pl.ANY), vmem],
        out_specs=(pl.BlockSpec(memory_space=pltpu.HBM), vmem, vmem),
        scratch_shapes=[
            pltpu.VMEM((DIRS, span, tiles, SUB, lanes), f32),
            pltpu.VMEM((DIRS, span, tiles, SUB, lanes), f32),
            pltpu.VMEM((DIRS, span, SUB * tiles, lanes), f32),
            pltpu.VMEM((planes, 3, SUB * (tiles + 1), lanes), f32),
            pltpu.VMEM((STEPS, 3, 2, SUB, lanes), f32),
            pltpu.VMEM((3 * SUB * SUB, lanes), f32),
            pltpu.VMEM((rank + 4 * SUB, width), jnp.bfloat16),
            pltpu.VMEM((rank + 4 * SUB, lanes), f32),
            pltpu.VMEM((planes, DIRS, SUB * tiles + SUB, lanes), f32),
            pltpu.SMEM((count,), jnp.int32),
            pltpu.SemaphoreType.DMA((planes + 1,)),
        ],
        compiler_params=params,
    )(*blocks, snap_steps, modes)

    if at_once:
        parts = [lax.all_to_all(sums, ("group", "dev"), 0, 0)]
    else:
        parts = summed(sums, n_dev, n_group)
    scale = math.sqrt(3 * width * members)
    solved = (
        jax.ShapeDtypeStruct((count, count), f32),
        jax.ShapeDtypeStruct((count * 3 * width // lanes, lanes), f32),
    )
    coef, factor, new_modes, flag, proj = pl.pallas_call(
        functools.partial(finish_kernel, scale, count, rank),
        out_shape=(
            jax.ShapeDtypeStruct((count, rank), f32),
            *solved,
            jax.ShapeDtypeStruct((1, 1), jnp.int32),
            jax.ShapeDtypeStruct((SUB, rank), f32),
        ),
        in_specs=[vmem] * (len(parts) + 2),
        out_specs=(vmem,) * 5,
        scratch_shapes=[pltpu.VMEM((rank, lanes), f32)],
        compiler_params=params,
    )(*parts, snaps, modes)
    coefficients = coef.T

    def from_residuals(state):
        gram = pl.pallas_call(
            inner_kernel, out_shape=jax.ShapeDtypeStruct((SUB, SUB), f32), in_specs=[vmem] * 3, out_specs=vmem
        )(proj, snaps, modes)
        gram = lax.psum(gram, ("group", "dev"))
        return (
            jnp.int32(0),
            *pl.pallas_call(
                functools.partial(solve_kernel, scale), out_shape=solved, in_specs=[vmem] * 4, out_specs=(vmem, vmem)
            )(gram, proj, snaps, modes),
        )

    _, factor, new_modes = lax.while_loop(lambda state: state[0] != 0, from_residuals, (flag[0, 0], factor, new_modes))
    return (pops, coefficients, factor, new_modes.reshape(count, 3, 1, width))


def solution(mesh):
    placed = (
        P("dev", "group", None),
        P(None, "dev", "group", None),
        P(None, None, "dev", "group"),
        P(),
    )
    return jax.shard_map(
        per_device,
        mesh=mesh,
        in_specs=placed,
        out_specs=(P(None, "dev", "group", None), P(), P(), P(None, None, "dev", "group")),
        check_vma=False,
    )
```
